32 devices in a mesh: dp: 4 (over y, x), seq: 8 (over z, core).
Axes of the slice: x: 2, y: 2, z: 4, core: 2. Of those that a mesh axis runs over, the one named last changes fastest.
Arguments:
- latents: bfloat16 [4, 1024, 1024], P('dp', 'seq'), may hold values from -6 to 6
- d_out: bfloat16 [4, 1024, 1024], P('dp', 'seq'), may hold values from -6 to 6
- lengths: int32 [4, 4], P('dp'), may hold values from 1 to 898, as said below
- gain_attn: bfloat16 [1024], P(('dp', 'seq')), may hold values from 0.5 to 1.5
- w_query: bfloat16 [1024, 1024], P(('dp', 'seq')), may hold values from -0.1875 to 0.1875
- w_key: bfloat16 [1024, 1024], P(('dp', 'seq')), may hold values from -0.1875 to 0.1875
- w_value: bfloat16 [1024, 1024], P(('dp', 'seq')), may hold values from -0.1875 to 0.1875
- w_out: bfloat16 [1024, 1024], P(('dp', 'seq')), may hold values from -1 to 1
- gain_ffn: bfloat16 [1024], P(('dp', 'seq')), may hold values from 0.5 to 1.5
- w_gate: bfloat16 [1024, 2816], P(('dp', 'seq')), may hold values from -0.1875 to 0.1875
- w_up: bfloat16 [1024, 2816], P(('dp', 'seq')), may hold values from -0.1875 to 0.1875
- w_down: bfloat16 [2816, 1024], P(('dp', 'seq')), may hold values from -0.109375 to 0.109375
Outputs:
- latents_out: bfloat16 [4, 1024, 1024], P('dp', 'seq')
- d_latents: bfloat16 [4, 1024, 1024], P('dp', 'seq')
- grad_gain_attn: float32 [1024], P(('dp', 'seq'))
- grad_w_query: float32 [1024, 1024], P(('dp', 'seq'))
- grad_w_key: float32 [1024, 1024], P(('dp', 'seq'))
- grad_w_value: float32 [1024, 1024], P(('dp', 'seq'))
- grad_w_out: float32 [1024, 1024], P(('dp', 'seq'))
- grad_gain_ffn: float32 [1024], P(('dp', 'seq'))
- grad_w_gate: float32 [1024, 2816], P(('dp', 'seq'))
- grad_w_up: float32 [1024, 2816], P(('dp', 'seq'))
- grad_w_down: float32 [2816, 1024], P(('dp', 'seq'))
The draws below stay inside these ranges and needn't reach their ends.
Inputs may be any that keep to these rules, and one draw needn't show every extreme that they name: Each row holds the lengths of the 4 patch sequences of one group in order; they sum to 1024; in every group one sequence has the largest length.
All inputs are finite; a program needn't handle non-finite values.
Results may differ from the reference program's by a relative error of at most 0.018.
Values may be sent and summed in bfloat16 or wider, within the bound.
A program may use at most 256 MiB of HBM per device.

```python
import math
import jax
import jax.numpy as jnp
from jax import lax

D = 1024
HEADS = 16
HEAD_DIM = 64
FF = 2816
TOK_DEV = 128
SEQS = 4
GROUPS = 4
GROUP_TOK = 1024


def draw_lengths(key, part):
    key = jax.random.fold_in(key, 11)
    first_key, second_key = jax.random.split(key)
    common = (TOK_DEV - 1) // 3
    offset = jax.random.randint(first_key, (GROUPS, 1), 0, common, dtype=jnp.int32)
    longest = jax.random.randint(second_key, (GROUPS, 1), 0, SEQS, dtype=jnp.int32)
    columns = jnp.arange(SEQS, dtype=jnp.int32)[None, :]
    chosen = columns == longest
    rank = columns - (columns > longest).astype(jnp.int32)
    others = jnp.where(rank == 0, 1, jnp.where(rank == 1, common + offset, jnp.where(rank == 2, 2 * common - 1 - offset, common)))
    big = GROUP_TOK - (SEQS - 1) * common
    return jnp.where(chosen, big, others).astype(jnp.int32)


def steps_of(rng, dims, shards, smallest, high):
    level = 1.0
    for axis_at, parts in shards:
        heights = jax.random.uniform(jax.random.fold_in(jax.random.fold_in(rng, 6), axis_at), (parts,), jnp.float32, smallest / len(shards), high / len(shards))
        level = level * jnp.repeat(jnp.exp(heights), dims[axis_at] // parts).reshape((-1,) + (1,) * (len(dims) - 1 - axis_at))
    return level


def centred(key, extent, spread, most, cuts=(), kind=jnp.bfloat16):
    loudness = steps_of(key, extent, cuts, -0.22, 0.18) if cuts else 1.0
    entries = jax.random.normal(key, extent, jnp.float32) * spread * loudness
    return jnp.minimum(jnp.maximum(entries, -most), most).astype(kind)


def setup_inputs(seed: int = 0) -> dict:
    splits = jax.random.split(jax.random.key(seed), 13)
    return {
        "latents": centred(splits[0], (GROUPS, GROUP_TOK, D), 1.0, 6.0, ((0, 4), (1, 8))),
        "d_out": centred(splits[1], (GROUPS, GROUP_TOK, D), 1.0, 6.0, ((0, 4), (1, 8))),
        "lengths": draw_lengths(jax.random.fold_in(splits[12], 71), 0),
        "gain_attn": jnp.clip(1.0 + 0.1 * jax.random.normal(splits[3], (D,), jnp.float32), 0.5, 1.5).astype(jnp.bfloat16),
        "w_query": centred(splits[4], (D, D), D ** -0.5, 0.1875, ((0, 32),)),
        "w_key": centred(splits[5], (D, D), D ** -0.5, 0.1875, ((0, 32),)),
        "w_value": centred(splits[6], (D, D), D ** -0.5, 0.1875, ((0, 32),)),
        "w_out": centred(splits[7], (D, D), (D // 32) ** -0.5, 1.0, ((0, 32),)),
        "gain_ffn": jnp.clip(1.0 + 0.1 * jax.random.normal(splits[8], (D,), jnp.float32), 0.5, 1.5).astype(jnp.bfloat16),
        "w_gate": centred(splits[9], (D, FF), D ** -0.5, 0.1875, ((0, 32),)),
        "w_up": centred(splits[10], (D, FF), D ** -0.5, 0.1875, ((0, 32),)),
        "w_down": centred(splits[11], (FF, D), FF ** -0.5, 0.109375, ((0, 32),)),
    }


EPS = 1e-05

@jax.custom_vjp
def low(v):
    return lax.optimization_barrier(v.astype(jnp.bfloat16)).astype(jnp.float32)

@jax.custom_vjp
def low_back(v):
    return v

def low_keep(v):
    return (low(v), None)

def low_pass(kept, grad):
    return (grad,)

def back_keep(v):
    return (v, None)

def back_low(kept, grad):
    return (low(grad),)
low.defvjp(low_keep, low_pass)
low_back.defvjp(back_keep, back_low)

def matmul_high(left, right):
    return jnp.dot(left, right, precision=lax.Precision.HIGHEST, preferred_element_type=jnp.float32)

def norm_rows(values, gain_vec):
    return values * lax.rsqrt(lax.optimization_barrier(jnp.mean(values * values, axis=-1, keepdims=True)) + EPS) * gain_vec

def attention(query_proj, key_proj, value_proj, positions, begins):
    row_count = query_proj.shape[0]
    span = math.gcd(row_count, 512)

    def one_block(pieces):
        query_piece, pos_piece, begin_piece = pieces
        scores = jnp.einsum('qhd,khd->hqk', query_piece, key_proj, precision=lax.Precision.HIGHEST) * 0.125
        scores = low_back(scores)
        allowed = (positions[None, None, :] <= pos_piece[None, :, None]) & (positions[None, None, :] >= begin_piece[None, :, None])
        masked = jnp.where(allowed, scores, -1e+30)
        row_max = lax.optimization_barrier(jnp.max(masked, axis=-1, keepdims=True))
        expon = jnp.where(allowed, jnp.exp(masked - row_max), 0.0)
        rounded = low(expon)
        total_sum = lax.optimization_barrier(jnp.sum(rounded, axis=-1))
        raw_sum = low_back(jnp.einsum('hqk,khd->qhd', rounded, value_proj, precision=lax.Precision.HIGHEST))
        return raw_sum / jnp.transpose(total_sum)[:, :, None]
    shaped = (query_proj.reshape(row_count // span, span, HEADS, HEAD_DIM), positions.reshape(row_count // span, span), begins.reshape(row_count // span, span))
    return lax.map(jax.checkpoint(one_block), shaped).reshape(row_count, HEADS * HEAD_DIM)

def layer(inputs_f, gain_attn, w_query, w_key, w_value, w_out, gain_ffn, w_gate, w_up, w_down, positions, begins):
    h_one = low(norm_rows(inputs_f, gain_attn))
    query_proj = low_back(low(matmul_high(h_one, w_query))).reshape(-1, HEADS, HEAD_DIM)
    key_proj = low_back(low(matmul_high(h_one, w_key))).reshape(-1, HEADS, HEAD_DIM)
    value_proj = low_back(low(matmul_high(h_one, w_value))).reshape(-1, HEADS, HEAD_DIM)
    attended = low_back(low(attention(query_proj, key_proj, value_proj, positions, begins)))
    resid = inputs_f + low_back(matmul_high(attended, w_out))
    h_two = low(norm_rows(resid, gain_ffn))
    gate_proj = low_back(matmul_high(h_two, w_gate))
    up_proj = low_back(matmul_high(h_two, w_up))
    hidden = low(jax.nn.silu(gate_proj) * up_proj)
    return resid + matmul_high(hidden, w_down)

def reference(latents, d_out, lengths, gain_attn, w_query, w_key, w_value, w_out, gain_ffn, w_gate, w_up, w_down):
    params = tuple((item.astype(jnp.float32) for item in (gain_attn, w_query, w_key, w_value, w_out, gain_ffn, w_gate, w_up, w_down)))
    positions = jnp.arange(GROUP_TOK, dtype=jnp.int32)

    def per_group(running, pieces):
        inputs_b, cotan_b, seq_lens = pieces
        seq_ends = jnp.cumsum(seq_lens, dtype=jnp.int32)
        begins = lax.optimization_barrier(jnp.sum(jnp.where(seq_ends[None, :] <= positions[:, None], seq_lens[None, :], 0), axis=1, dtype=jnp.int32))

        def forward(inputs_f, *weights):
            return layer(inputs_f, *weights, positions, begins)
        result, pullback = jax.vjp(forward, inputs_b.astype(jnp.float32), *params)
        all_grads = pullback(cotan_b.astype(jnp.float32))
        running = tuple((left_term + right_term for left_term, right_term in zip(running, all_grads[1:])))
        return (running, (result.astype(jnp.bfloat16), all_grads[0].astype(jnp.bfloat16)))
    zero_grads = tuple((jnp.zeros_like(item) for item in params))
    grad_sums, (outputs, d_inputs) = lax.scan(per_group, zero_grads, (latents, d_out, lengths))
    return (outputs, d_inputs, grad_sums[0], grad_sums[1], grad_sums[2], grad_sums[3], grad_sums[4], grad_sums[5], grad_sums[6], grad_sums[7], grad_sums[8])
```

```python
import functools
import math

import jax
import jax.numpy as jnp
from jax import lax
from jax.experimental import pallas as pl
from jax.experimental.pallas import tpu as pltpu
from jax.sharding import PartitionSpec as P

HEADS = 16


EPS = 1e-05


def norm_rows(values, gain_vec):
    factor = lax.rsqrt(jnp.mean(values * values, axis=-1, keepdims=True) + EPS)
    normed = values * factor
    return (normed * gain_vec, normed, factor)


def norm_back(grad_out, normed, factor, gain_vec):
    scaled = grad_out * gain_vec
    inner = jnp.mean(scaled * normed, axis=-1, keepdims=True)
    return (factor * (scaled - normed * inner), jnp.sum(grad_out * normed, axis=0))


def dot_left(left, right):
    return lax.dot_general(
        left, right, (((0,), (0,)), ((), ())), preferred_element_type=jnp.float32
    )


def dot_right(left, right):
    return lax.dot_general(
        left, right, (((1,), (1,)), ((), ())), preferred_element_type=jnp.float32
    )


def per_device(
    latents,
    d_out,
    lengths,
    gain_attn,
    w_query,
    w_key,
    w_value,
    w_out,
    gain_ffn,
    w_gate,
    w_up,
    w_down,
):
    g_attn, full_query, full_key, full_value, full_out, g_ffn, full_gate, full_up, full_down = (
        lax.all_gather(gain_attn, ("dp", "seq"), axis=0, tiled=True),
        lax.all_gather(w_query, ("dp", "seq"), axis=0, tiled=True),
        lax.all_gather(w_key, ("dp", "seq"), axis=0, tiled=True),
        lax.all_gather(w_value, ("dp", "seq"), axis=0, tiled=True),
        lax.all_gather(w_out, ("dp", "seq"), axis=0, tiled=True),
        lax.all_gather(gain_ffn, ("dp", "seq"), axis=0, tiled=True),
        lax.all_gather(w_gate, ("dp", "seq"), axis=0, tiled=True),
        lax.all_gather(w_up, ("dp", "seq"), axis=0, tiled=True),
        lax.all_gather(w_down, ("dp", "seq"), axis=0, tiled=True),
    )
    gain_one = g_attn.astype(jnp.float32)
    gain_two = g_ffn.astype(jnp.float32)
    inputs_f = latents[0].astype(jnp.float32)
    row_count, model_width = inputs_f.shape
    head_size = model_width // HEADS
    group_rows = row_count * lax.axis_size("seq")
    here = lax.axis_index("seq") * row_count + jnp.arange(row_count, dtype=jnp.int32)
    seq_lens = lengths[0]
    seq_ends = jnp.cumsum(seq_lens, dtype=jnp.int32)
    begins = jnp.sum(
        jnp.where(seq_ends[None, :] <= here[:, None], seq_lens[None, :], 0), axis=1, dtype=jnp.int32
    )
    key_block = math.gcd(group_rows, 1024)
    block_count = group_rows // key_block
    key_positions = jnp.arange(group_rows, dtype=jnp.int32).reshape(block_count, key_block)
    h_one_f, normed_one, factor_one = norm_rows(inputs_f, gain_one)
    h_one = h_one_f.astype(jnp.bfloat16)
    query_proj = jnp.dot(h_one, full_query, preferred_element_type=jnp.float32).astype(jnp.bfloat16)
    key_proj = jnp.dot(h_one, full_key, preferred_element_type=jnp.float32).astype(jnp.bfloat16)
    value_proj = jnp.dot(h_one, full_value, preferred_element_type=jnp.float32).astype(jnp.bfloat16)
    keys_all, values_all = (
        lax.all_gather(key_proj, "seq", axis=0, tiled=True),
        lax.all_gather(value_proj, "seq", axis=0, tiled=True),
    )
    query_heads = query_proj.reshape(row_count, HEADS, head_size)

    def split_blocks(array):
        return array.reshape(block_count, key_block, HEADS, head_size)

    def block_scores(key_piece, pos_piece):
        scores = (
            jnp.einsum("qhd,khd->hqk", query_heads, key_piece, preferred_element_type=jnp.float32)
            * 0.125
        )
        allowed = (pos_piece[None, :] <= here[:, None]) & (pos_piece[None, :] >= begins[:, None])
        return (scores, allowed[None])

    def max_step(running, pieces):
        key_piece, pos_piece = pieces
        scores, allowed = block_scores(key_piece, pos_piece)
        return (jnp.maximum(running, jnp.max(jnp.where(allowed, scores, -1e30), axis=-1)), None)

    row_max, _ = lax.scan(
        max_step,
        jnp.full((HEADS, row_count), -1e30, jnp.float32),
        (split_blocks(keys_all), key_positions),
    )

    def sum_step(running, pieces):
        key_piece, value_piece, pos_piece = pieces
        scores, allowed = block_scores(key_piece, pos_piece)
        expon = jnp.where(
            allowed, jnp.exp(jnp.where(allowed, scores, -1e30) - row_max[:, :, None]), 0.0
        )
        rounded = expon.astype(jnp.bfloat16)
        total_sum, raw_sum = running
        total_sum = total_sum + jnp.sum(rounded.astype(jnp.float32), axis=-1)
        raw_sum = raw_sum + jnp.einsum(
            "hqk,khd->qhd", rounded, value_piece, preferred_element_type=jnp.float32
        )
        return ((total_sum, raw_sum), None)

    (total_sum, raw_sum), _ = lax.scan(
        sum_step,
        (
            jnp.zeros((HEADS, row_count), jnp.float32),
            jnp.zeros((row_count, HEADS, head_size), jnp.float32),
        ),
        (split_blocks(keys_all), split_blocks(values_all), key_positions),
    )
    totals_rows = jnp.transpose(total_sum)
    attended = raw_sum / totals_rows[:, :, None]
    attended_low = attended.reshape(row_count, model_width).astype(jnp.bfloat16)
    resid = inputs_f + jnp.dot(attended_low, full_out, preferred_element_type=jnp.float32)
    h_two_f, normed_two, factor_two = norm_rows(resid, gain_two)
    h_two = h_two_f.astype(jnp.bfloat16)
    gate_proj = jnp.dot(h_two, full_gate, preferred_element_type=jnp.float32)
    up_proj = jnp.dot(h_two, full_up, preferred_element_type=jnp.float32)
    gate_sigmoid = jax.nn.sigmoid(gate_proj)
    gate_active = gate_proj * gate_sigmoid
    hidden = (gate_active * up_proj).astype(jnp.bfloat16)
    outputs = resid + jnp.dot(hidden, full_down, preferred_element_type=jnp.float32)
    latents_out = outputs.astype(jnp.bfloat16)[None]
    grad_out = d_out[0]
    grad_down = dot_left(hidden, grad_out)
    g_hidden = dot_right(grad_out, full_down)
    g_gate = (g_hidden * up_proj * gate_sigmoid * (1.0 + gate_proj * (1.0 - gate_sigmoid))).astype(
        jnp.bfloat16
    )
    g_up = (g_hidden * gate_active).astype(jnp.bfloat16)
    grad_gate = dot_left(h_two, g_gate)
    grad_up = dot_left(h_two, g_up)
    g_h_two = dot_right(g_gate, full_gate) + dot_right(g_up, full_up)
    g_norm_two, grad_gain_two = norm_back(g_h_two, normed_two, factor_two, gain_two)
    g_resid = grad_out.astype(jnp.float32) + g_norm_two
    g_branch = g_resid.astype(jnp.bfloat16)
    grad_out_proj = dot_left(attended_low, g_branch)
    g_att = dot_right(g_branch, full_out).reshape(row_count, HEADS, head_size).astype(jnp.bfloat16)
    g_att_f = g_att.astype(jnp.float32)
    g_raw = (g_att_f / totals_rows[:, :, None]).astype(jnp.bfloat16)
    g_total = jnp.transpose(-jnp.sum(g_att_f * raw_sum, axis=-1) / (totals_rows * totals_rows))
    keys_back, values_back = (
        lax.all_gather(key_proj, "seq", axis=0, tiled=True),
        lax.all_gather(value_proj, "seq", axis=0, tiled=True),
    )

    def score_grads(key_piece, value_piece, pos_piece):
        scores, allowed = block_scores(key_piece, pos_piece)
        expon = jnp.where(
            allowed, jnp.exp(jnp.where(allowed, scores, -1e30) - row_max[:, :, None]), 0.0
        )
        g_probs = jnp.einsum("qhd,khd->hqk", g_raw, value_piece, preferred_element_type=jnp.float32)
        g_scores = (expon * (g_probs + g_total[:, :, None])).astype(jnp.bfloat16)
        return (expon, g_scores)

    def grad_step(running, pieces):
        key_piece, value_piece, pos_piece = pieces
        expon, g_scores = score_grads(key_piece, value_piece, pos_piece)
        rounded = expon.astype(jnp.bfloat16)
        running = (
            running
            + jnp.einsum("hqk,khd->qhd", g_scores, key_piece, preferred_element_type=jnp.float32)
            * 0.125
        )
        g_key_piece = (
            jnp.einsum("hqk,qhd->khd", g_scores, query_heads, preferred_element_type=jnp.float32)
            * 0.125
        )
        g_value_piece = jnp.einsum(
            "hqk,qhd->khd", rounded, g_raw, preferred_element_type=jnp.float32
        )
        return (running, (g_key_piece, g_value_piece))

    g_query_f, (g_keys, g_values) = lax.scan(
        grad_step,
        jnp.zeros((row_count, HEADS, head_size), jnp.float32),
        (split_blocks(keys_back), split_blocks(values_back), key_positions),
    )
    mine_key, mine_value = (
        lax.psum_scatter(
            g_keys.reshape(group_rows, model_width).astype(jnp.bfloat16),
            "seq",
            scatter_dimension=0,
            tiled=True,
        ).astype(jnp.float32),
        lax.psum_scatter(
            g_values.reshape(group_rows, model_width).astype(jnp.bfloat16),
            "seq",
            scatter_dimension=0,
            tiled=True,
        ).astype(jnp.float32),
    )
    g_key = mine_key.astype(jnp.bfloat16)
    g_value = mine_value.astype(jnp.bfloat16)
    g_query = g_query_f.reshape(row_count, model_width).astype(jnp.bfloat16)
    grad_query = dot_left(h_one, g_query)
    grad_key = dot_left(h_one, g_key)
    grad_value = dot_left(h_one, g_value)
    g_h_one = (
        dot_right(g_query, full_query) + dot_right(g_key, full_key) + dot_right(g_value, full_value)
    )
    g_norm_one, grad_gain_one = norm_back(g_h_one, normed_one, factor_one, gain_one)
    d_latents = (g_resid + g_norm_one).astype(jnp.bfloat16)[None]
    gain_pair = jnp.stack((grad_gain_one, grad_gain_two), axis=1)
    summed = (
        lax.psum_scatter(gain_pair, ("dp", "seq"), scatter_dimension=0, tiled=True),
        lax.psum_scatter(grad_query, ("dp", "seq"), scatter_dimension=0, tiled=True),
        lax.psum_scatter(grad_key, ("dp", "seq"), scatter_dimension=0, tiled=True),
        lax.psum_scatter(grad_value, ("dp", "seq"), scatter_dimension=0, tiled=True),
        lax.psum_scatter(grad_out_proj, ("dp", "seq"), scatter_dimension=0, tiled=True),
        lax.psum_scatter(grad_gate, ("dp", "seq"), scatter_dimension=0, tiled=True),
        lax.psum_scatter(grad_up, ("dp", "seq"), scatter_dimension=0, tiled=True),
        lax.psum_scatter(grad_down, ("dp", "seq"), scatter_dimension=0, tiled=True),
    )
    return (
        latents_out,
        d_latents,
        summed[0][:, 0],
        summed[1],
        summed[2],
        summed[3],
        summed[4],
        summed[0][:, 1],
        summed[5],
        summed[6],
        summed[7],
    )


MESH = pl.DeviceIdType.MESH
BF = jnp.bfloat16
F32 = jnp.float32
DP, ZS, CORES = 4, 4, 2
RANKS = DP * CORES


def planes_fit(mesh):
    return mesh.shape["dp"] == DP and mesh.shape["seq"] == ZS * CORES


def dot_nn(left, right):
    return jnp.dot(left, right, preferred_element_type=F32)


def remote(src, dst, send_sem, recv_sem, device):
    return pltpu.make_async_remote_copy(
        src_ref=src,
        dst_ref=dst,
        send_sem=send_sem,
        recv_sem=recv_sem,
        device_id=device,
        device_id_type=MESH,
    )


def wait_for(ref, sem):
    pltpu.make_async_copy(ref, ref, sem).wait()


def layer_kernel(
    lat_in,
    dout_in,
    lens_in,
    wqkv_in,
    wgu_in,
    wd_in,
    wo_in,
    lat_o,
    dlat_o,
    gqkv_o,
    ggu_o,
    gd_o,
    go_o,
    own_l,
    lens,
    n_one,
    n_two,
    cot,
    gbr,
    wqkv,
    wgu,
    wd,
    wo,
    qkv,
    att,
    att_f,
    tot,
    probs,
    gsc,
    part_a,
    part_b,
    part_c,
    sib,
    rcv,
    hid,
    ggu,
    gatt,
    graw_two,
    q_two,
    gqkv,
    dwqkv,
    dwgu,
    dwd,
    dwo,
    zq,
    zgu,
    resid,
    gres,
    back,
    tr_s,
    tr_r,
    ln_s,
    ln_r,
    wa_s,
    wa_r,
    wz_s,
    wz_r,
    wd_s,
    wd_r,
    wo_s,
    wo_r,
    ag_s,
    ag_r,
    ag_x,
    rs_s,
    rs_r,
    rs_x,
    gz_s,
    gz_r,
    ga_s,
    ga_r,
    gd_s,
    gd_r,
    go_s,
    go_r,
    tb_s,
    tb_r,
):
    k = lax.axis_index("dp")
    s = lax.axis_index("seq")
    z = s // CORES
    c = s % CORES
    oc = 1 - c
    rank = CORES * k + c

    def dev(kk, zz, cc):
        return (kk, CORES * zz + cc)

    def peer(i):
        return 2 * ((k // 2 + i // 2) % 2) + (k % 2 + i % 2) % 2

    def zpeer(i):
        return (z + i) % ZS

    sibling = dev(k, z, oc)

    barrier = pltpu.get_barrier_semaphore()
    greeted = 0
    for di in range(4):
        for dz in range(4):
            if di or dz:
                pl.semaphore_signal(
                    barrier, inc=1, device_id=dev(peer(di), zpeer(dz), c), device_id_type=MESH
                )
                greeted += 1
            if di == 0 or dz == 0:
                pl.semaphore_signal(
                    barrier, inc=1, device_id=dev(peer(di), zpeer(dz), oc), device_id_type=MESH
                )
                greeted += 1
    pl.semaphore_wait(barrier, greeted)

    def spread(src, dst_of, which, start):
        for q in range(4):
            here = (k == q) & (z == k)
            piece = src.at[pl.ds(32 * q, 32)]

            @pl.when(here)
            def _():
                if start:
                    pltpu.make_async_copy(piece, dst_of(q), tr_r.at[which, z]).start()

            @pl.when(jnp.logical_not(here))
            def _():
                copy = remote(
                    piece, dst_of(q), tr_s.at[which, q], tr_r.at[which, z], dev(q, k, c)
                )
                if start:
                    copy.start()
                else:
                    copy.wait_send()

    def spread_lat(start):
        spread(lat_in, lambda q: own_l.at[z], 0, start)

    def spread_cot(start):
        spread(dout_in, lambda q: cot.at[q, z, c], 1, start)

    def spread_lens(start):
        here = z == k

        @pl.when(here)
        def _():
            if start:
                pltpu.make_async_copy(lens_in, lens, ln_r).start()

        @pl.when(jnp.logical_not(here))
        def _():
            copy = remote(lens_in, lens, ln_s, ln_r, dev(z, k, c))
            if start:
                copy.start()
            else:
                copy.wait_send()

    def plane_weights(src, dst, which, start):
        for i in range(4):
            for same in (True, False):
                cc = c if same else oc
                target = CORES * peer(i) + cc
                piece = src.at[target]
                place = dst.at[k, z, c]
                if i == 0 and same:
                    if start:
                        pltpu.make_async_copy(piece, place, wa_r.at[which, rank]).start()
                else:
                    copy = remote(
                        piece,
                        place,
                        wa_s.at[which, 2 * i + (0 if same else 1)],
                        wa_r.at[which, rank],
                        dev(peer(i), z, cc),
                    )
                    if start:
                        copy.start()
                    else:
                        copy.wait_send()

    def plane_weights_here(dst, which):
        for kk in range(4):
            for cc in range(2):
                wait_for(dst.at[kk, z, cc], wa_r.at[which, CORES * kk + cc])

    def line_weights(dst, which, start):
        for i in range(1, 4):
            copy = remote(
                dst.at[:, z],
                dst.at[:, z],
                wz_s.at[which, i],
                wz_r.at[which, z],
                dev(k, zpeer(i), c),
            )
            if start:
                copy.start()
            else:
                copy.wait_send()

    def line_weights_here(dst, which):
        for i in range(1, 4):
            wait_for(dst.at[:, zpeer(i)], wz_r.at[which, zpeer(i)])

    def down_weights(start):
        for i in range(4):
            if i == 0:
                if start:
                    pltpu.make_async_copy(wd_in, wd.at[z], wd_r.at[z]).start()
            else:
                copy = remote(wd_in, wd.at[z], wd_s.at[i], wd_r.at[z], dev(k, zpeer(i), c))
                if start:
                    copy.start()
                else:
                    copy.wait_send()

    def out_weights(start):
        to_core = z // 2
        slot = 2 * (z % 2) + c
        for i in range(4):

            def send():
                copy = remote(
                    wo_in, wo.at[slot], wo_s.at[i], wo_r.at[slot], dev(k, zpeer(i), to_core)
                )
                if start:
                    copy.start()
                else:
                    copy.wait_send()

            if i == 0:

                @pl.when(to_core == c)
                def _():
                    if start:
                        pltpu.make_async_copy(wo_in, wo.at[slot], wo_r.at[slot]).start()

                @pl.when(to_core != c)
                def _():
                    send()

            else:
                send()

    def ag_send(buf, which):
        own = buf.at[k, :, c]
        for i in (1, 2, 3):
            remote(
                own, own, ag_s.at[which, i], ag_r.at[which, k], dev(peer(i), z, c)
            ).start()
        remote(own, own, ag_s.at[which, 4], ag_x.at[which, k], sibling).start()

    def ag_relay(buf, which, i):
        m = peer(i)
        block = buf.at[m, :, c]
        wait_for(block, ag_r.at[which, m])
        remote(block, block, ag_s.at[which, 4 + i], ag_x.at[which, m], sibling).start()

    def ag_other(buf, which, i):
        m = peer(i)
        wait_for(buf.at[m, :, oc], ag_x.at[which, m])

    def ag_end(buf, which):
        own = buf.at[k, :, c]
        for i in (1, 2, 3):
            remote(
                own, own, ag_s.at[which, i], ag_r.at[which, k], dev(peer(i), z, c)
            ).wait_send()
        for i in range(4):
            block = buf.at[peer(i), :, c]
            remote(
                block, block, ag_s.at[which, 4 + i], ag_x.at[which, peer(i)], sibling
            ).wait_send()

    def rs_copy(part, which, i):
        m = peer(i)
        return remote(
            part.at[m, :, oc], sib.at[which, m], rs_s.at[which, i], rs_r.at[which, m], sibling
        )

    def rs_send_copy(part, which, i):
        m = peer(i)
        return remote(
            part.at[m, :, c],
            rcv.at[which, k],
            rs_s.at[which, 4 + i],
            rs_x.at[which, k],
            dev(m, z, c),
        )

    def rs_pair(part, which, i):
        m = peer(i)
        wait_for(sib.at[which, m], rs_r.at[which, m])
        return part[m, :, c].astype(F32) + sib[which, m].astype(F32)

    def rs_forward(part, which):
        for i in (3, 1, 2):
            part[peer(i), :, c] = rs_pair(part, which, i).astype(BF)
            rs_send_copy(part, which, i).start()

    def rs_sum(part, which):
        total = rs_pair(part, which, 0)
        for i in (1, 2, 3):
            m = peer(i)
            wait_for(rcv.at[which, m], rs_x.at[which, m])
            total = total + rcv[which, m].astype(F32)
        return total.reshape(128, 1024)

    def rs_end(part, which):
        for i in range(4):
            rs_copy(part, which, i).wait_send()
        for i in (1, 2, 3):
            rs_send_copy(part, which, i).wait_send()

    spread_lat(True)
    spread_lens(True)
    plane_weights(wqkv_in, wqkv, 0, True)
    spread_cot(True)
    plane_weights(wgu_in, wgu, 1, True)
    plane_weights_here(wqkv, 0)
    line_weights(wqkv, 0, True)
    for b in range(4):
        wait_for(own_l.at[b], tr_r.at[0, b])
    lat_f = own_l[...].reshape(128, 1024).astype(F32)
    r_one = lax.rsqrt(jnp.mean(lat_f * lat_f, axis=-1, keepdims=True) + EPS)
    n_one[k, :, c] = (lat_f * r_one).astype(BF).reshape(4, 32, 1024)
    ag_send(n_one, 0)
    out_weights(True)
    plane_weights_here(wgu, 1)
    line_weights(wgu, 1, True)
    down_weights(True)
    for b in range(4):
        wait_for(cot.at[k, b, c], tr_r.at[1, b])
    ag_send(cot, 1)

    line_weights_here(wqkv, 0)

    @pl.loop(0, 4)
    def _(i):
        @pl.when(i > 0)
        def _():
            ag_relay(n_one, 0, i)

        ag_other(n_one, 0, i)
        m = peer(i)
        block = n_one[m].reshape(256, 1024)
        out = dot_nn(block, wqkv[...].reshape(1024, 384))
        qkv[:, m] = out.astype(BF).reshape(8, 32, 384)

    wait_for(lens, ln_r)
    lane = lax.broadcasted_iota(jnp.int32, (128, 128), 1)
    row = lax.broadcasted_iota(jnp.int32, (128, 128), 0)
    first = lane < 64

    def two_heads(v):
        zero = jnp.zeros_like(v)
        return jnp.concatenate(
            [jnp.where(first, v, zero), jnp.where(first, zero, v)], axis=0
        )

    def one_of_two(v):
        return jnp.where(first, v[:128], v[128:])

    def part_of(t0, t1, col):
        return qkv[t0:t1, :, :, col * 128 : (col + 1) * 128].reshape((t1 - t0) * 128, 128)

    for t in range(8):
        span = (t + 1) * 128
        q = two_heads(part_of(t, t + 1, 0).astype(F32) * 0.125).astype(BF)
        keys = part_of(0, t + 1, 1)
        vals = part_of(0, t + 1, 2)
        pos = row + t * 128
        begin = jnp.zeros((128, 128), jnp.int32)
        end = jnp.zeros((1, 128), jnp.int32)
        for g in range(4):
            length = lens[g : g + 1, :]
            end = end + length
            begin = begin + jnp.where(end <= pos, length, 0)
        allowed = []
        for u in range(t + 1):
            ok = begin <= lane + u * 128
            if u == t:
                ok = ok & (lane <= row)
            allowed.append(ok)
        allowed = jnp.concatenate(allowed, axis=1)
        scores = dot_right(q, keys)
        sums = []
        raws = []
        for h in range(2):
            sc = jnp.where(allowed, scores[h * 128 : (h + 1) * 128], -1e30)
            top = jnp.max(sc, axis=-1, keepdims=True)
            expo = jnp.exp(sc - top)
            low = expo.astype(BF)
            probs[t, h * 128 : (h + 1) * 128, 0:span] = low
            sums.append(jnp.sum(low.astype(F32), axis=-1, keepdims=True))
        raw = dot_nn(probs[t, :, 0:span], vals)
        both = jnp.where(first, sums[0], sums[1])
        attended = one_of_two(raw) / both
        tot[t] = both
        att_f[t] = attended
        att[:, t] = attended.astype(BF).reshape(4, 32, 128)

    for i in (1, 2, 3):
        ag_relay(cot, 1, i)
    for slot in range(4):
        wait_for(wo.at[slot], wo_r.at[slot])

    @pl.loop(0, 4)
    def _(j):
        i = 3 - j
        m = peer(i)
        out = dot_nn(att[m].reshape(256, 128), wo[...].reshape(128, 1024))
        part_a[m] = out.astype(BF).reshape(4, 2, 32, 1024)
        rs_copy(part_a, 0, i).start()

    rs_forward(part_a, 0)
    res = own_l[...].reshape(128, 1024).astype(F32) + rs_sum(part_a, 0)
    resid[...] = res
    r_two = lax.rsqrt(jnp.mean(res * res, axis=-1, keepdims=True) + EPS)
    n_two[k, :, c] = (res * r_two).astype(BF).reshape(4, 32, 1024)
    ag_send(n_two, 2)

    for i in range(4):
        ag_other(cot, 1, i)
    line_weights_here(wgu, 1)
    for b in range(4):
        wait_for(wd.at[b], wd_r.at[b])

    @pl.loop(0, 4)
    def _(i):
        @pl.when(i > 0)
        def _():
            ag_relay(n_two, 2, i)

        ag_other(n_two, 2, i)
        m = peer(i)
        gu = dot_nn(n_two[m].reshape(256, 1024), wgu[...].reshape(1024, 768))
        gate = gu[:, :384]
        up = gu[:, 384:]
        sig = jax.nn.sigmoid(gate)
        active = gate * sig
        hid[m] = (active * up).astype(BF)
        g_hid = dot_right(cot[m].reshape(256, 1024), wd[...].reshape(384, 1024))
        ggu[m, :, :384] = (g_hid * up * sig * (1.0 + gate * (1.0 - sig))).astype(BF)
        ggu[m, :, 384:] = (g_hid * active).astype(BF)
        out = dot_right(ggu[m], wgu[...].reshape(1024, 768))
        part_b[m] = out.astype(BF).reshape(4, 2, 32, 1024)
        rs_copy(part_b, 1, i).start()

    rs_forward(part_b, 1)

    @pl.loop(0, 4)
    def _(i):
        m = peer(i)
        out = dot_nn(hid[m], wd[...].reshape(384, 1024))
        part_c[m] = out.astype(BF).reshape(4, 2, 32, 1024)
        rs_copy(part_c, 2, i).start()

    scaled = rs_sum(part_b, 1)
    res = resid[...]
    r_two = lax.rsqrt(jnp.mean(res * res, axis=-1, keepdims=True) + EPS)
    normed = res * r_two
    inner = jnp.mean(scaled * normed, axis=-1, keepdims=True)
    g_res = cot[k, :, c].reshape(128, 1024).astype(F32) + r_two * (scaled - normed * inner)
    gres[...] = g_res
    gbr[k, :, c] = g_res.astype(BF).reshape(4, 32, 1024)
    ag_send(gbr, 3)
    rs_forward(part_c, 2)

    @pl.loop(0, 4)
    def _(d):
        cols = pl.ds(pl.multiple_of(d * 256, 256), 256)
        left = n_two[:, :, :, :, cols].reshape(1024, 256)
        out = dot_left(left, ggu[...].reshape(1024, 768))
        dwgu[d] = out.astype(BF).reshape(4, 2, 32, 768)

    def line_grads(grad, land, which, start):
        for i in range(1, 4):
            copy = remote(
                grad.at[:, zpeer(i)],
                land.at[z],
                gz_s.at[which, i],
                gz_r.at[which, z],
                dev(k, zpeer(i), c),
            )
            if start:
                copy.start()
            else:
                copy.wait_send()

    line_grads(dwgu, zgu, 1, True)

    @pl.loop(0, 4)
    def _(n):
        cols = pl.ds(pl.multiple_of(n * 256, 256), 256)
        right = cot[:, :, :, :, cols].reshape(1024, 256)
        out = dot_left(hid[...].reshape(1024, 384), right)
        dwd[:, :, cols] = out.astype(BF).reshape(4, 96, 256)

    def down_grads(start):
        for i in range(4):
            src = dwd.at[zpeer(i)]
            if i == 0:
                if start:
                    pltpu.make_async_copy(src, gd_o.at[z], gd_r.at[z]).start()
            else:
                copy = remote(src, gd_o.at[z], gd_s.at[i], gd_r.at[z], dev(k, zpeer(i), c))
                if start:
                    copy.start()
                else:
                    copy.wait_send()

    down_grads(True)

    @pl.loop(0, 4)
    def _(i):
        @pl.when(i > 0)
        def _():
            ag_relay(gbr, 3, i)

        ag_other(gbr, 3, i)
        m = peer(i)
        out = dot_right(gbr[m].reshape(256, 1024), wo[...].reshape(128, 1024))
        gatt[:, m] = out.astype(BF).reshape(8, 32, 128)

    for t in range(8):
        span = (t + 1) * 128
        keys = part_of(0, t + 1, 1)
        vals = part_of(0, t + 1, 2)
        ratio = gatt[t].reshape(128, 128).astype(F32) / tot[t]
        g_raw = two_heads(ratio.astype(BF).astype(F32)).astype(BF)
        graw_two[t] = g_raw
        q_two[t] = two_heads(part_of(t, t + 1, 0).astype(F32)).astype(BF)
        prod = ratio * att_f[t]
        g_tot = -jnp.sum(two_heads(prod), axis=-1, keepdims=True)
        g_pr = dot_right(g_raw, vals)
        g_sc = probs[t, :, 0:span].astype(F32) * (g_pr + g_tot)
        gsc[t, :, 0:span] = g_sc.astype(BF)
        g_q = one_of_two(dot_nn(gsc[t, :, 0:span], keys)) * 0.125
        gqkv[:, t, :, 0:128] = g_q.astype(BF).reshape(4, 32, 128)
    for u in range(8):
        cols = slice(u * 128, (u + 1) * 128)
        rows = (8 - u) * 256
        g_k = dot_left(gsc[u:, :, cols].reshape(rows, 128), q_two[u:].reshape(rows, 128)) * 0.125
        g_v = dot_left(probs[u:, :, cols].reshape(rows, 128), graw_two[u:].reshape(rows, 128))
        gqkv[:, u, :, 128:256] = g_k.astype(BF).reshape(4, 32, 128)
        gqkv[:, u, :, 256:384] = g_v.astype(BF).reshape(4, 32, 128)

    rs_end(part_a, 0)

    @pl.loop(0, 4)
    def _(j):
        i = 3 - j
        m = peer(i)
        out = dot_right(gqkv[m].reshape(256, 384), wqkv[...].reshape(1024, 384))
        part_a[m] = out.astype(BF).reshape(4, 2, 32, 1024)
        rs_copy(part_a, 3, i).start()

    rs_forward(part_a, 3)

    @pl.loop(0, 4)
    def _(d):
        cols = pl.ds(pl.multiple_of(d * 256, 256), 256)
        left = n_one[:, :, :, :, cols].reshape(1024, 256)
        out = dot_left(left, gqkv[...].reshape(1024, 384))
        dwqkv[d] = out.astype(BF).reshape(4, 2, 32, 384)

    line_grads(dwqkv, zq, 0, True)

    @pl.loop(0, 4)
    def _(n):
        cols = pl.ds(pl.multiple_of(n * 256, 256), 256)
        right = gbr[:, :, :, :, cols].reshape(1024, 256)
        out = dot_left(att[...].reshape(1024, 128), right)
        dwo[:, :, cols] = out.astype(BF).reshape(4, 32, 256)

    def out_grads(start):
        for p in range(2):
            for cs in range(2):
                zz = 2 * c + p
                here = (zz == z) & (c == cs)
                src = dwo.at[2 * p + cs]

                @pl.when(here)
                def _():
                    if start:
                        pltpu.make_async_copy(src, go_o.at[z], go_r.at[z]).start()

                @pl.when(jnp.logical_not(here))
                def _():
                    copy = remote(
                        src, go_o.at[z], go_s.at[2 * p + cs], go_r.at[z], dev(k, zz, cs)
                    )
                    if start:
                        copy.start()
                    else:
                        copy.wait_send()

    out_grads(True)

    def gather_back(which, dst, start):
        for b in range(4):
            here = (z == k) & (z == b)
            src = back.at[which, b]
            place = dst.at[pl.ds(pl.multiple_of(32 * k, 32), 32)]

            @pl.when(here)
            def _():
                if start:
                    pltpu.make_async_copy(src, place, tb_r.at[which, k]).start()

            @pl.when(jnp.logical_not(here))
            def _():
                copy = remote(src, place, tb_s.at[which, b], tb_r.at[which, k], dev(z, b, c))
                if start:
                    copy.start()
                else:
                    copy.wait_send()

    out_f = resid[...] + rs_sum(part_c, 2)
    back[0] = out_f.astype(BF).reshape(4, 32, 1024)
    gather_back(0, lat_o, True)

    def line_sum(grad, land, which):
        total = grad[:, z].astype(F32)
        for i in range(1, 4):
            wait_for(land.at[zpeer(i)], gz_r.at[which, zpeer(i)])
            total = total + land[zpeer(i)].astype(F32)
        land[z] = total.astype(BF)

    def plane_grads(land, dst, which, start):
        for i in range(4):
            m = peer(i)
            for same in (True, False):
                cc = c if same else oc
                src = land.at[z, m, cc]
                place = dst.at[rank]
                if i == 0 and same:
                    if start:
                        pltpu.make_async_copy(src, place, ga_r.at[which, rank]).start()
                else:
                    copy = remote(
                        src,
                        place,
                        ga_s.at[which, 2 * i + (0 if same else 1)],
                        ga_r.at[which, rank],
                        dev(m, z, cc),
                    )
                    if start:
                        copy.start()
                    else:
                        copy.wait_send()

    line_sum(dwgu, zgu, 1)
    plane_grads(zgu, ggu_o, 1, True)

    scaled = rs_sum(part_a, 3)
    lat_f = own_l[...].reshape(128, 1024).astype(F32)
    r_one = lax.rsqrt(jnp.mean(lat_f * lat_f, axis=-1, keepdims=True) + EPS)
    normed = lat_f * r_one
    inner = jnp.mean(scaled * normed, axis=-1, keepdims=True)
    d_lat = gres[...] + r_one * (scaled - normed * inner)
    back[1] = d_lat.astype(BF).reshape(4, 32, 1024)
    gather_back(1, dlat_o, True)

    line_sum(dwqkv, zq, 0)
    plane_grads(zq, gqkv_o, 0, True)

    for b in range(4):
        wait_for(gd_o.at[b], gd_r.at[b])
        wait_for(go_o.at[b], go_r.at[b])
        for which, dst in ((0, lat_o), (1, dlat_o)):
            wait_for(dst.at[pl.ds(32 * b, 32)], tb_r.at[which, b])
    for r in range(RANKS):
        wait_for(gqkv_o.at[r], ga_r.at[0, r])
        wait_for(ggu_o.at[r], ga_r.at[1, r])
    spread_lat(False)
    spread_cot(False)
    spread_lens(False)
    plane_weights(wqkv_in, wqkv, 0, False)
    plane_weights(wgu_in, wgu, 1, False)
    line_weights(wqkv, 0, False)
    line_weights(wgu, 1, False)
    down_weights(False)
    out_weights(False)
    for which, buf in enumerate((n_one, cot, n_two, gbr)):
        ag_end(buf, which)
    rs_end(part_b, 1)
    rs_end(part_c, 2)
    rs_end(part_a, 3)
    line_grads(dwgu, zgu, 1, False)
    line_grads(dwqkv, zq, 0, False)
    plane_grads(zgu, ggu_o, 1, False)
    plane_grads(zq, gqkv_o, 0, False)
    down_grads(False)
    out_grads(False)
    gather_back(0, lat_o, False)
    gather_back(1, dlat_o, False)


def run_layer(lat, dout, lens, wqkv_src, wgu_src, wd_src, wo_src):
    vm = pltpu.VMEM
    dma = pltpu.SemaphoreType.DMA
    rows = (4, 4, 2, 32)
    return pl.pallas_call(
        layer_kernel,
        out_shape=(
            jax.ShapeDtypeStruct((128, 1024), BF),
            jax.ShapeDtypeStruct((128, 1024), BF),
            jax.ShapeDtypeStruct((RANKS, 32, 384), BF),
            jax.ShapeDtypeStruct((RANKS, 32, 768), BF),
            jax.ShapeDtypeStruct((4, 96, 1024), BF),
            jax.ShapeDtypeStruct((4, 32, 1024), BF),
        ),
        in_specs=[pl.BlockSpec(memory_space=pl.ANY)] * 7,
        out_specs=[pl.BlockSpec(memory_space=pl.ANY)] * 6,
        scratch_shapes=[
            vm((4, 32, 1024), BF),
            vm((8, 128), jnp.int32),
            vm(rows + (1024,), BF),
            vm(rows + (1024,), BF),
            vm(rows + (1024,), BF),
            vm(rows + (1024,), BF),
            vm(rows + (384,), BF),
            vm(rows + (768,), BF),
            vm((4, 96, 1024), BF),
            vm((4, 32, 1024), BF),
            vm((8, 4, 32, 384), BF),
            vm((4, 8, 32, 128), BF),
            vm((8, 128, 128), F32),
            vm((8, 128, 128), F32),
            vm((8, 256, 1024), BF),
            vm((8, 256, 1024), BF),
            vm(rows + (1024,), BF),
            vm(rows + (1024,), BF),
            vm(rows + (1024,), BF),
            vm((4, 4, 4, 32, 1024), BF),
            vm((4, 4, 4, 32, 1024), BF),
            vm((4, 256, 384), BF),
            vm((4, 256, 768), BF),
            vm((8, 4, 32, 128), BF),
            vm((8, 256, 128), BF),
            vm((8, 256, 128), BF),
            vm((4, 8, 32, 384), BF),
            vm(rows + (384,), BF),
            vm(rows + (768,), BF),
            vm((4, 96, 1024), BF),
            vm((4, 32, 1024), BF),
            vm((4, 4, 2, 32, 384), BF),
            vm((4, 4, 2, 32, 768), BF),
            vm((128, 1024), F32),
            vm((128, 1024), F32),
            vm((2, 4, 32, 1024), BF),
            dma((2, 4)),
            dma((2, 4)),
            dma,
            dma,
            dma((2, 8)),
            dma((2, 8)),
            dma((2, 4)),
            dma((2, 4)),
            dma((4,)),
            dma((4,)),
            dma((4,)),
            dma((4,)),
            dma((4, 8)),
            dma((4, 4)),
            dma((4, 4)),
            dma((4, 8)),
            dma((4, 4)),
            dma((4, 4)),
            dma((2, 4)),
            dma((2, 4)),
            dma((2, 8)),
            dma((2, 8)),
            dma((4,)),
            dma((4,)),
            dma((4,)),
            dma((4,)),
            dma((2, 4)),
            dma((2, 4)),
        ],
        compiler_params=pltpu.CompilerParams(
            collective_id=0, has_side_effects=True, vmem_limit_bytes=60 * 1024 * 1024
        ),
    )(lat, dout, lens, wqkv_src, wgu_src, wd_src, wo_src)


def plane_device(
    latents,
    d_out,
    lengths,
    gain_attn,
    w_query,
    w_key,
    w_value,
    w_out,
    gain_ffn,
    w_gate,
    w_up,
    w_down,
):
    gain_one = gain_attn.astype(F32)[:, None]
    gain_two = gain_ffn.astype(F32)[:, None]

    def heads_of(w):
        return (w.astype(F32) * gain_one).astype(BF).reshape(32, RANKS, 128)

    wqkv_src = jnp.concatenate(
        [heads_of(w) for w in (w_query, w_key, w_value)], axis=-1
    ).transpose(1, 0, 2)

    def units_of(w):
        w = (w.astype(F32) * gain_two).astype(BF).reshape(32, DP, ZS, CORES, 88)
        w = jnp.pad(w, ((0, 0), (0, 0), (0, 0), (0, 0), (0, 8)))
        return w.transpose(1, 3, 0, 2, 4).reshape(RANKS, 32, 384)

    wgu_src = jnp.concatenate([units_of(w_gate), units_of(w_up)], axis=-1)
    wd_src = jnp.pad(w_down, ((0, 8), (0, 0)))
    lens = jnp.broadcast_to(jnp.pad(lengths[0], (0, 4))[:, None], (8, 128))
    lat_o, dlat_o, gqkv, ggu, gd, go = run_layer(
        latents[0], d_out[0], lens, wqkv_src, wgu_src, wd_src, w_out
    )

    def rows_of(g):
        return g.astype(F32).transpose(1, 0, 2).reshape(32, 1024)

    def units_back(g):
        g = g.astype(F32).reshape(DP, CORES, 32, ZS, 96)[..., :88]
        return g.transpose(2, 0, 3, 1, 4).reshape(32, 2816)

    n_q, n_k, n_v = (rows_of(gqkv[:, :, i * 128 : (i + 1) * 128]) for i in range(3))
    n_g, n_u = units_back(ggu[:, :, :384]), units_back(ggu[:, :, 384:])
    g_gain_one = jnp.sum(
        n_q * w_query.astype(F32) + n_k * w_key.astype(F32) + n_v * w_value.astype(F32), axis=1
    )
    g_gain_two = jnp.sum(n_g * w_gate.astype(F32) + n_u * w_up.astype(F32), axis=1)
    g_out = jnp.sum(go.astype(F32), axis=0)
    g_down = jnp.sum(gd.astype(F32), axis=0)[:88]
    return (
        lat_o[None],
        dlat_o[None],
        g_gain_one,
        n_q * gain_one,
        n_k * gain_one,
        n_v * gain_one,
        g_out,
        g_gain_two,
        n_g * gain_two,
        n_u * gain_two,
        g_down,
    )


def solution(mesh):
    return jax.shard_map(
        plane_device if planes_fit(mesh) else per_device,
        mesh=mesh,
        in_specs=(
            P("dp", "seq", None),
            P("dp", "seq", None),
            P("dp", None),
            P(("dp", "seq")),
            P(("dp", "seq"), None),
            P(("dp", "seq"), None),
            P(("dp", "seq"), None),
            P(("dp", "seq"), None),
            P(("dp", "seq")),
            P(("dp", "seq"), None),
            P(("dp", "seq"), None),
            P(("dp", "seq"), None),
        ),
        out_specs=(
            P("dp", "seq", None),
            P("dp", "seq", None),
            P(("dp", "seq")),
            P(("dp", "seq"), None),
            P(("dp", "seq"), None),
            P(("dp", "seq"), None),
            P(("dp", "seq"), None),
            P(("dp", "seq")),
            P(("dp", "seq"), None),
            P(("dp", "seq"), None),
            P(("dp", "seq"), None),
        ),
        check_vma=False,
    )
```

```python
import functools
import math

import jax
import jax.numpy as jnp
from jax import lax
from jax.experimental import pallas as pl
from jax.experimental.pallas import tpu as pltpu
from jax.sharding import PartitionSpec as P

HEADS = 16


EPS = 1e-05


def norm_rows(values, gain_vec):
    factor = lax.rsqrt(jnp.mean(values * values, axis=-1, keepdims=True) + EPS)
    normed = values * factor
    return (normed * gain_vec, normed, factor)


def norm_back(grad_out, normed, factor, gain_vec):
    scaled = grad_out * gain_vec
    inner = jnp.mean(scaled * normed, axis=-1, keepdims=True)
    return (factor * (scaled - normed * inner), jnp.sum(grad_out * normed, axis=0))


def dot_left(left, right):
    return lax.dot_general(
        left, right, (((0,), (0,)), ((), ())), preferred_element_type=jnp.float32
    )


def dot_right(left, right):
    return lax.dot_general(
        left, right, (((1,), (1,)), ((), ())), preferred_element_type=jnp.float32
    )


def per_device(
    latents,
    d_out,
    lengths,
    gain_attn,
    w_query,
    w_key,
    w_value,
    w_out,
    gain_ffn,
    w_gate,
    w_up,
    w_down,
):
    g_attn, full_query, full_key, full_value, full_out, g_ffn, full_gate, full_up, full_down = (
        lax.all_gather(gain_attn, ("dp", "seq"), axis=0, tiled=True),
        lax.all_gather(w_query, ("dp", "seq"), axis=0, tiled=True),
        lax.all_gather(w_key, ("dp", "seq"), axis=0, tiled=True),
        lax.all_gather(w_value, ("dp", "seq"), axis=0, tiled=True),
        lax.all_gather(w_out, ("dp", "seq"), axis=0, tiled=True),
        lax.all_gather(gain_ffn, ("dp", "seq"), axis=0, tiled=True),
        lax.all_gather(w_gate, ("dp", "seq"), axis=0, tiled=True),
        lax.all_gather(w_up, ("dp", "seq"), axis=0, tiled=True),
        lax.all_gather(w_down, ("dp", "seq"), axis=0, tiled=True),
    )
    gain_one = g_attn.astype(jnp.float32)
    gain_two = g_ffn.astype(jnp.float32)
    inputs_f = latents[0].astype(jnp.float32)
    row_count, model_width = inputs_f.shape
    head_size = model_width // HEADS
    group_rows = row_count * lax.axis_size("seq")
    here = lax.axis_index("seq") * row_count + jnp.arange(row_count, dtype=jnp.int32)
    seq_lens = lengths[0]
    seq_ends = jnp.cumsum(seq_lens, dtype=jnp.int32)
    begins = jnp.sum(
        jnp.where(seq_ends[None, :] <= here[:, None], seq_lens[None, :], 0), axis=1, dtype=jnp.int32
    )
    key_block = math.gcd(group_rows, 1024)
    block_count = group_rows // key_block
    key_positions = jnp.arange(group_rows, dtype=jnp.int32).reshape(block_count, key_block)
    h_one_f, normed_one, factor_one = norm_rows(inputs_f, gain_one)
    h_one = h_one_f.astype(jnp.bfloat16)
    query_proj = jnp.dot(h_one, full_query, preferred_element_type=jnp.float32).astype(jnp.bfloat16)
    key_proj = jnp.dot(h_one, full_key, preferred_element_type=jnp.float32).astype(jnp.bfloat16)
    value_proj = jnp.dot(h_one, full_value, preferred_element_type=jnp.float32).astype(jnp.bfloat16)
    keys_all, values_all = (
        lax.all_gather(key_proj, "seq", axis=0, tiled=True),
        lax.all_gather(value_proj, "seq", axis=0, tiled=True),
    )
    query_heads = query_proj.reshape(row_count, HEADS, head_size)

    def split_blocks(array):
        return array.reshape(block_count, key_block, HEADS, head_size)

    def block_scores(key_piece, pos_piece):
        scores = (
            jnp.einsum("qhd,khd->hqk", query_heads, key_piece, preferred_element_type=jnp.float32)
            * 0.125
        )
        allowed = (pos_piece[None, :] <= here[:, None]) & (pos_piece[None, :] >= begins[:, None])
        return (scores, allowed[None])

    def max_step(running, pieces):
        key_piece, pos_piece = pieces
        scores, allowed = block_scores(key_piece, pos_piece)
        return (jnp.maximum(running, jnp.max(jnp.where(allowed, scores, -1e30), axis=-1)), None)

    row_max, _ = lax.scan(
        max_step,
        jnp.full((HEADS, row_count), -1e30, jnp.float32),
        (split_blocks(keys_all), key_positions),
    )

    def sum_step(running, pieces):
        key_piece, value_piece, pos_piece = pieces
        scores, allowed = block_scores(key_piece, pos_piece)
        expon = jnp.where(
            allowed, jnp.exp(jnp.where(allowed, scores, -1e30) - row_max[:, :, None]), 0.0
        )
        rounded = expon.astype(jnp.bfloat16)
        total_sum, raw_sum = running
        total_sum = total_sum + jnp.sum(rounded.astype(jnp.float32), axis=-1)
        raw_sum = raw_sum + jnp.einsum(
            "hqk,khd->qhd", rounded, value_piece, preferred_element_type=jnp.float32
        )
        return ((total_sum, raw_sum), None)

    (total_sum, raw_sum), _ = lax.scan(
        sum_step,
        (
            jnp.zeros((HEADS, row_count), jnp.float32),
            jnp.zeros((row_count, HEADS, head_size), jnp.float32),
        ),
        (split_blocks(keys_all), split_blocks(values_all), key_positions),
    )
    totals_rows = jnp.transpose(total_sum)
    attended = raw_sum / totals_rows[:, :, None]
    attended_low = attended.reshape(row_count, model_width).astype(jnp.bfloat16)
    resid = inputs_f + jnp.dot(attended_low, full_out, preferred_element_type=jnp.float32)
    h_two_f, normed_two, factor_two = norm_rows(resid, gain_two)
    h_two = h_two_f.astype(jnp.bfloat16)
    gate_proj = jnp.dot(h_two, full_gate, preferred_element_type=jnp.float32)
    up_proj = jnp.dot(h_two, full_up, preferred_element_type=jnp.float32)
    gate_sigmoid = jax.nn.sigmoid(gate_proj)
    gate_active = gate_proj * gate_sigmoid
    hidden = (gate_active * up_proj).astype(jnp.bfloat16)
    outputs = resid + jnp.dot(hidden, full_down, preferred_element_type=jnp.float32)
    latents_out = outputs.astype(jnp.bfloat16)[None]
    grad_out = d_out[0]
    grad_down = dot_left(hidden, grad_out)
    g_hidden = dot_right(grad_out, full_down)
    g_gate = (g_hidden * up_proj * gate_sigmoid * (1.0 + gate_proj * (1.0 - gate_sigmoid))).astype(
        jnp.bfloat16
    )
    g_up = (g_hidden * gate_active).astype(jnp.bfloat16)
    grad_gate = dot_left(h_two, g_gate)
    grad_up = dot_left(h_two, g_up)
    g_h_two = dot_right(g_gate, full_gate) + dot_right(g_up, full_up)
    g_norm_two, grad_gain_two = norm_back(g_h_two, normed_two, factor_two, gain_two)
    g_resid = grad_out.astype(jnp.float32) + g_norm_two
    g_branch = g_resid.astype(jnp.bfloat16)
    grad_out_proj = dot_left(attended_low, g_branch)
    g_att = dot_right(g_branch, full_out).reshape(row_count, HEADS, head_size).astype(jnp.bfloat16)
    g_att_f = g_att.astype(jnp.float32)
    g_raw = (g_att_f / totals_rows[:, :, None]).astype(jnp.bfloat16)
    g_total = jnp.transpose(-jnp.sum(g_att_f * raw_sum, axis=-1) / (totals_rows * totals_rows))
    keys_back, values_back = (
        lax.all_gather(key_proj, "seq", axis=0, tiled=True),
        lax.all_gather(value_proj, "seq", axis=0, tiled=True),
    )

    def score_grads(key_piece, value_piece, pos_piece):
        scores, allowed = block_scores(key_piece, pos_piece)
        expon = jnp.where(
            allowed, jnp.exp(jnp.where(allowed, scores, -1e30) - row_max[:, :, None]), 0.0
        )
        g_probs = jnp.einsum("qhd,khd->hqk", g_raw, value_piece, preferred_element_type=jnp.float32)
        g_scores = (expon * (g_probs + g_total[:, :, None])).astype(jnp.bfloat16)
        return (expon, g_scores)

    def grad_step(running, pieces):
        key_piece, value_piece, pos_piece = pieces
        expon, g_scores = score_grads(key_piece, value_piece, pos_piece)
        rounded = expon.astype(jnp.bfloat16)
        running = (
            running
            + jnp.einsum("hqk,khd->qhd", g_scores, key_piece, preferred_element_type=jnp.float32)
            * 0.125
        )
        g_key_piece = (
            jnp.einsum("hqk,qhd->khd", g_scores, query_heads, preferred_element_type=jnp.float32)
            * 0.125
        )
        g_value_piece = jnp.einsum(
            "hqk,qhd->khd", rounded, g_raw, preferred_element_type=jnp.float32
        )
        return (running, (g_key_piece, g_value_piece))

    g_query_f, (g_keys, g_values) = lax.scan(
        grad_step,
        jnp.zeros((row_count, HEADS, head_size), jnp.float32),
        (split_blocks(keys_back), split_blocks(values_back), key_positions),
    )
    mine_key, mine_value = (
        lax.psum_scatter(
            g_keys.reshape(group_rows, model_width).astype(jnp.bfloat16),
            "seq",
            scatter_dimension=0,
            tiled=True,
        ).astype(jnp.float32),
        lax.psum_scatter(
            g_values.reshape(group_rows, model_width).astype(jnp.bfloat16),
            "seq",
            scatter_dimension=0,
            tiled=True,
        ).astype(jnp.float32),
    )
    g_key = mine_key.astype(jnp.bfloat16)
    g_value = mine_value.astype(jnp.bfloat16)
    g_query = g_query_f.reshape(row_count, model_width).astype(jnp.bfloat16)
    grad_query = dot_left(h_one, g_query)
    grad_key = dot_left(h_one, g_key)
    grad_value = dot_left(h_one, g_value)
    g_h_one = (
        dot_right(g_query, full_query) + dot_right(g_key, full_key) + dot_right(g_value, full_value)
    )
    g_norm_one, grad_gain_one = norm_back(g_h_one, normed_one, factor_one, gain_one)
    d_latents = (g_resid + g_norm_one).astype(jnp.bfloat16)[None]
    gain_pair = jnp.stack((grad_gain_one, grad_gain_two), axis=1)
    summed = (
        lax.psum_scatter(gain_pair, ("dp", "seq"), scatter_dimension=0, tiled=True),
        lax.psum_scatter(grad_query, ("dp", "seq"), scatter_dimension=0, tiled=True),
        lax.psum_scatter(grad_key, ("dp", "seq"), scatter_dimension=0, tiled=True),
        lax.psum_scatter(grad_value, ("dp", "seq"), scatter_dimension=0, tiled=True),
        lax.psum_scatter(grad_out_proj, ("dp", "seq"), scatter_dimension=0, tiled=True),
        lax.psum_scatter(grad_gate, ("dp", "seq"), scatter_dimension=0, tiled=True),
        lax.psum_scatter(grad_up, ("dp", "seq"), scatter_dimension=0, tiled=True),
        lax.psum_scatter(grad_down, ("dp", "seq"), scatter_dimension=0, tiled=True),
    )
    return (
        latents_out,
        d_latents,
        summed[0][:, 0],
        summed[1],
        summed[2],
        summed[3],
        summed[4],
        summed[0][:, 1],
        summed[5],
        summed[6],
        summed[7],
    )


MESH = pl.DeviceIdType.MESH
BF = jnp.bfloat16
F32 = jnp.float32
DP, ZS, CORES = 4, 4, 2
RANKS = DP * CORES


def planes_fit(mesh):
    return mesh.shape["dp"] == DP and mesh.shape["seq"] == ZS * CORES


def dot_nn(left, right):
    return jnp.dot(left, right, preferred_element_type=F32)


def remote(src, dst, send_sem, recv_sem, device):
    return pltpu.make_async_remote_copy(
        src_ref=src,
        dst_ref=dst,
        send_sem=send_sem,
        recv_sem=recv_sem,
        device_id=device,
        device_id_type=MESH,
    )


def wait_for(ref, sem):
    pltpu.make_async_copy(ref, ref, sem).wait()


def on_diagonal(row):
    at = lax.broadcasted_iota(jnp.int32, (32, 32), 0) == lax.broadcasted_iota(jnp.int32, (32, 32), 1)
    return jnp.where(at, row.astype(F32), 0.0)


def layer_kernel(
    lat_in,
    dout_in,
    lengths_in,
    gain_one,
    gain_two,
    wq_raw,
    wk_raw,
    wv_raw,
    wg_raw,
    wu_raw,
    wd_raw,
    wo_in,
    lat_o,
    dlat_o,
    gqkv_o,
    ggu_o,
    gd_o,
    go_o,
    lens_in,
    wqkv_in,
    wgu_in,
    wd_in,
    own_l,
    stop,
    lens,
    n_one,
    n_two,
    cot,
    gbr,
    wqkv,
    wgu,
    wd,
    wo,
    qkv,
    att,
    att_f,
    tot,
    probs,
    gsc,
    part_a,
    part_b,
    part_c,
    sib,
    rcv,
    turn,
    hid,
    ggu,
    slope,
    gatt,
    graw_two,
    q_two,
    gqkv,
    dwqkv,
    dwgu,
    dwd,
    dwo,
    zq,
    zgu,
    zd,
    xq,
    xgu,
    xd,
    down_sum,
    resid,
    gres,
    back,
    tr_s,
    tr_r,
    tx_r,
    tz_s,
    ln_s,
    ln_r,
    wa_s,
    wa_r,
    wz_s,
    wz_r,
    wd_r,
    wo_s,
    wo_r,
    ag_s,
    ag_r,
    ag_x,
    ag_d,
    rs_s,
    rs_r,
    rs_x,
    rs_d,
    gz_s,
    gz_r,
    gx_r,
    ga_s,
    ga_r,
    gd_r,
    go_s,
    go_r,
    tb_s,
    tb_r,
):
    k = lax.axis_index("dp")
    s = lax.axis_index("seq")
    z = s // CORES
    c = s % CORES
    oc = 1 - c
    rank = CORES * k + c

    def dev(kk, zz, cc):
        return (kk, CORES * zz + cc)

    def peer(i):
        return 2 * ((k // 2 + i // 2) % 2) + (k % 2 + i % 2) % 2

    def zpeer(i):
        return (z + i) % ZS

    sibling = dev(k, z, oc)

    barrier = pltpu.get_barrier_semaphore()
    greeted = 0
    for di in range(4):
        for dz in range(4):
            if di or dz:
                pl.semaphore_signal(
                    barrier, inc=1, device_id=dev(peer(di), zpeer(dz), c), device_id_type=MESH
                )
                greeted += 1
            if di == 0 or dz == 0:
                pl.semaphore_signal(
                    barrier, inc=1, device_id=dev(peer(di), zpeer(dz), oc), device_id_type=MESH
                )
                greeted += 1

    def scaled_rows(w, gain):
        return dot_nn(on_diagonal(gain[...]).astype(BF), w[...])

    for i, w in enumerate((wq_raw, wk_raw, wv_raw)):
        rows = scaled_rows(w, gain_one).astype(BF)
        for r in range(RANKS):
            wqkv_in[r, :, i * 128 : (i + 1) * 128] = rows[:, r * 128 : (r + 1) * 128]
    wd_in[0:80] = wd_raw[0:80]
    wd_in[80:96] = jnp.concatenate([wd_raw[80:88], jnp.zeros((8, 1024), BF)], axis=0)
    tile_row = lax.broadcasted_iota(jnp.int32, (8, 128), 0)
    tile = jnp.zeros((8, 128), jnp.int32)
    for i in range(4):
        tile = jnp.where(tile_row == i, lengths_in[0, i], tile)
    lens_in[...] = tile

    def units_to_ranks():
        for i, w in enumerate((wg_raw, wu_raw)):
            rows = scaled_rows(w, gain_two)
            gap = jnp.zeros((32, 8), F32)
            for r in range(RANKS):
                parts = []
                for b in range(ZS):
                    at = 88 * (8 * (r // CORES) + CORES * b + r % CORES)
                    parts += [rows[:, at : at + 88], gap]
                wgu_in[r, :, i * 384 : (i + 1) * 384] = jnp.concatenate(parts, axis=1).astype(BF)

    pl.semaphore_wait(barrier, greeted)

    def spread(src, final_of, which, start):
        for q in range(4):
            piece = src.at[pl.ds(32 * q, 32)]

            @pl.when((z == k) & (k == q))
            def _():
                if start:
                    pltpu.make_async_copy(piece, final_of(q, z), tr_r.at[which, z]).start()

            @pl.when((z == k) & (k != q))
            def _():
                copy = remote(
                    piece, final_of(q, z), tr_s.at[which, q], tr_r.at[which, z], dev(q, z, c)
                )
                if start:
                    copy.start()
                else:
                    copy.wait_send()

            @pl.when((z != k) & (k != q))
            def _():
                copy = remote(
                    piece, stop.at[which, k], tr_s.at[which, q], tx_r.at[which, k], dev(q, z, c)
                )
                if start:
                    copy.start()
                else:
                    copy.wait_send()

    def spread_on(src, final_of, which, start):
        for i in range(1, 4):
            g = zpeer(i)

            def send(piece):
                copy = remote(
                    piece, final_of(k, z), tz_s.at[which, i], tr_r.at[which, z], dev(k, g, c)
                )
                if start:
                    copy.start()
                else:
                    copy.wait_send()

            @pl.when(g == k)
            def _():
                send(src.at[pl.ds(pl.multiple_of(32 * k, 32), 32)])

            @pl.when(g != k)
            def _():
                if start:
                    wait_for(stop.at[which, g], tx_r.at[which, g])
                send(stop.at[which, g])

    def lat_place(q, b):
        return own_l.at[b]

    def cot_place(q, b):
        return cot.at[q, b, c]

    def spread_lens(start):
        here = z == k

        @pl.when(here)
        def _():
            if start:
                pltpu.make_async_copy(lens_in, lens, ln_r).start()

        @pl.when(jnp.logical_not(here))
        def _():
            copy = remote(lens_in, lens, ln_s, ln_r, dev(z, k, c))
            if start:
                copy.start()
            else:
                copy.wait_send()

    def plane_weights(src, dst, which, start):
        for i in range(4):
            for same in (True, False):
                cc = c if same else oc
                target = CORES * peer(i) + cc
                piece = src.at[target]
                place = dst.at[k, z, c]
                if i == 0 and same:
                    if start:
                        pltpu.make_async_copy(piece, place, wa_r.at[which, rank]).start()
                else:
                    copy = remote(
                        piece,
                        place,
                        wa_s.at[which, 2 * i + (0 if same else 1)],
                        wa_r.at[which, rank],
                        dev(peer(i), z, cc),
                    )
                    if start:
                        copy.start()
                    else:
                        copy.wait_send()

    def plane_weights_here(dst, which):
        for kk in range(4):
            for cc in range(2):
                wait_for(dst.at[kk, z, cc], wa_r.at[which, CORES * kk + cc])

    middle = (z == 1) | (z == 2)
    near = (1 + z % 2, 2 + z // 2 - 2 * (z % 2))
    z_end = 3 * (z // 2)

    def far_of(place):
        return (3 - place, 6 - 3 * place)

    far = far_of(z)

    def line_copy(block, which, slot, b, place, src=None):
        src = block(b) if src is None else src
        return remote(src, block(b), wz_s.at[which, slot], wz_r.at[which, b], dev(k, place, c))

    def line_send(block, which, from_ends, from_middle, start=True, src=None):
        def send(slots):
            for j in slots:
                copy = line_copy(block, which, j, z, near[j], src)
                if start:
                    copy.start()
                else:
                    copy.wait_send()

        if from_ends:

            @pl.when(jnp.logical_not(middle))
            def _():
                send(from_ends)

        if from_middle:

            @pl.when(middle)
            def _():
                send(from_middle)

    def line_relay(block, which, j):
        @pl.when(middle)
        def _():
            wait_for(block(far[j]), wz_r.at[which, far[j]])
            line_copy(block, which, 2 + j, far[j], z_end).start()

    def line_sent(block, which, src=None):
        line_send(block, which, (0, 1), (0, 1), False, src)

        @pl.when(middle)
        def _():
            for j in range(2):
                line_copy(block, which, 2 + j, far[j], z_end).wait_send()

    def line_here(block, which):
        @pl.when(middle)
        def _():
            wait_for(block(z_end), wz_r.at[which, z_end])

        @pl.when(jnp.logical_not(middle))
        def _():
            for i in range(1, 4):
                wait_for(block(zpeer(i)), wz_r.at[which, zpeer(i)])

    def qkv_block(b):
        return wqkv.at[:, b]

    def gu_block(h):
        return lambda b: wgu.at[pl.ds(2 * h, 2), b]

    def down_block(b):
        return wd.at[b]

    def out_weights(start):
        to_core = z // 2
        slot = 2 * (z % 2) + c
        for i in range(4):

            def send():
                copy = remote(
                    wo_in, wo.at[slot], wo_s.at[i], wo_r.at[slot], dev(k, zpeer(i), to_core)
                )
                if start:
                    copy.start()
                else:
                    copy.wait_send()

            if i == 0:

                @pl.when(to_core == c)
                def _():
                    if start:
                        pltpu.make_async_copy(wo_in, wo.at[slot], wo_r.at[slot]).start()

                @pl.when(to_core != c)
                def _():
                    send()

            else:
                send()

    def half(j):
        return pl.ds(2 * j, 2)

    def ag_copy(buf, which, i):
        own = buf.at[k, :, c]
        return remote(own, own, ag_s.at[which, i], ag_r.at[which, k], dev(peer(i), z, c))

    def ag_turn(buf, which, i):
        block = buf.at[peer(i), half(i - 1), c]
        return remote(
            block, block, ag_s.at[which, 8 + i], ag_d.at[which, i - 1], dev(peer(3 - i), z, c)
        )

    def ag_across(buf, which, i):
        block = buf.at[peer(i), :, c]
        return remote(
            block, block, ag_s.at[which, 4 + i], ag_x.at[which, peer(i)], sibling
        )

    def ag_send(buf, which):
        for i in (1, 2):
            ag_copy(buf, which, i).start()
        ag_across(buf, which, 0).start()

    def ag_relay(buf, which, i):
        m = peer(i)
        if i < 3:
            wait_for(buf.at[m, :, c], ag_r.at[which, m])
            ag_turn(buf, which, i).start()
        else:
            for j in range(2):
                wait_for(buf.at[m, half(j), c], ag_d.at[which, j])
        ag_across(buf, which, i).start()

    def ag_other(buf, which, i):
        m = peer(i)
        wait_for(buf.at[m, :, oc], ag_x.at[which, m])

    def ag_end(buf, which):
        for i in (1, 2):
            ag_copy(buf, which, i).wait_send()
            ag_turn(buf, which, i).wait_send()
        for i in range(4):
            ag_across(buf, which, i).wait_send()

    def rs_copy(part, which, i):
        m = peer(i)
        return remote(
            part.at[m, :, oc], sib.at[which, m], rs_s.at[which, i], rs_r.at[which, m], sibling
        )

    def rs_part(part, which, i, j):
        m = peer(i)
        return remote(
            part.at[m, half(j), c],
            rcv.at[which, i - 1, half(j)],
            rs_s.at[which, 2 + 2 * i + j],
            rs_x.at[which, i - 1, j],
            dev(m, z, c),
        )

    def rs_turn(part, which, j):
        return remote(
            part.at[peer(3), half(j), c],
            turn.at[which, j],
            rs_s.at[which, 8 + j],
            rs_d.at[which, j],
            dev(peer(j + 1), z, c),
        )

    def rs_pair(part, which, i):
        m = peer(i)
        wait_for(sib.at[which, m], rs_r.at[which, m])
        return part[m, :, c].astype(F32) + sib[which, m].astype(F32)

    def rs_forward(part, which):
        part[peer(3), :, c] = rs_pair(part, which, 3).astype(BF)
        for j in range(2):
            rs_turn(part, which, j).start()
        for i in (1, 2):
            part[peer(i), :, c] = rs_pair(part, which, i).astype(BF)
            rs_part(part, which, i, i - 1).start()
        for j in range(2):
            wait_for(turn.at[which, j], rs_d.at[which, j])
            m = peer(2 - j)
            sums = part[m, half(j), c].astype(F32) + turn[which, j].astype(F32)
            part[m, half(j), c] = sums.astype(BF)
            rs_part(part, which, 2 - j, j).start()

    def rs_sum(part, which):
        total = rs_pair(part, which, 0)
        for i in (1, 2):
            for j in range(2):
                wait_for(rcv.at[which, i - 1, half(j)], rs_x.at[which, i - 1, j])
            total = total + rcv[which, i - 1].astype(F32)
        return total.reshape(128, 1024)

    def rs_end(part, which):
        for i in range(4):
            rs_copy(part, which, i).wait_send()
        for j in range(2):
            rs_turn(part, which, j).wait_send()
            for i in (1, 2):
                rs_part(part, which, i, j).wait_send()

    def grads_to_far(grad, land, which, j):
        return remote(
            grad(far[j]), land.at[z], gz_s.at[which, 1 + j], gz_r.at[which, z], dev(k, far[j], c)
        )

    def line_grads(grad, land, add, which, start):
        @pl.when(middle)
        def _():
            copy = remote(
                grad(z_end), land.at[z], gz_s.at[which, 0], gz_r.at[which, z], dev(k, z_end, c)
            )
            if start:
                copy.start()
            else:
                copy.wait_send()
                for j in range(2):
                    grads_to_far(grad, land, which, j).wait_send()

        @pl.when(jnp.logical_not(middle))
        def _():
            mid = 1 + z // 2
            for j in range(2):
                copy = remote(
                    grad(far_of(mid)[j]),
                    add.at[j],
                    gz_s.at[which, j],
                    gx_r.at[which, j],
                    dev(k, mid, c),
                )
                if start:
                    copy.start()
                else:
                    copy.wait_send()
            copy = remote(
                grad(mid), land.at[z], gz_s.at[which, 2], gz_r.at[which, z], dev(k, mid, c)
            )
            if start:
                copy.start()
            else:
                copy.wait_send()

    def line_grads_relay(grad, land, add, which, j):
        @pl.when(middle)
        def _():
            wait_for(add.at[j], gx_r.at[which, j])
            mine = grad(far[j])
            mine[...] = (mine[...].astype(F32) + add[j].astype(F32)).astype(BF)
            grads_to_far(grad, land, which, j).start()

    def line_sum(grad, land, which):
        total = grad(z)[...].astype(F32)
        for j in range(2):
            wait_for(land.at[near[j]], gz_r.at[which, near[j]])
            total = total + land[near[j]].astype(F32)
        return total

    def dwgu_block(b):
        return dwgu.at[:, b]

    def dwqkv_block(b):
        return dwqkv.at[:, b]

    def dwd_block(b):
        return dwd.at[b]

    spread(lat_in, lat_place, 0, True)
    plane_weights(wqkv_in, wqkv, 0, True)
    spread_lens(True)
    line_send(down_block, 2, (0,), (0, 1), src=wd_in)
    own_down = pltpu.make_async_copy(wd_in, wd.at[z], wd_r)
    own_down.start()
    units_to_ranks()
    spread_on(lat_in, lat_place, 0, True)
    plane_weights(wgu_in, wgu, 1, True)
    spread(dout_in, cot_place, 1, True)
    plane_weights_here(wqkv, 0)
    line_send(qkv_block, 0, (0, 1), (0, 1))
    for b in range(4):
        wait_for(own_l.at[b], tr_r.at[0, b])
    lat_f = own_l[...].reshape(128, 1024).astype(F32)
    r_one = lax.rsqrt(jnp.mean(lat_f * lat_f, axis=-1, keepdims=True) + EPS)
    n_one[k, :, c] = (lat_f * r_one).astype(BF).reshape(4, 32, 1024)
    ag_send(n_one, 0)
    line_relay(down_block, 2, 0)
    spread_on(dout_in, cot_place, 1, True)
    line_relay(qkv_block, 0, 0)
    ag_relay(n_one, 0, 1)
    ag_relay(n_one, 0, 2)
    line_relay(qkv_block, 0, 1)
    line_send(down_block, 2, (1,), (), src=wd_in)
    out_weights(True)
    ag_relay(n_one, 0, 3)
    plane_weights_here(wgu, 1)
    line_send(gu_block(0), 1, (0, 1), (0, 1))
    line_send(gu_block(1), 3, (0, 1), (0, 1))

    line_here(qkv_block, 0)

    @pl.loop(0, 4)
    def _(i):
        ag_other(n_one, 0, i)
        m = peer(i)
        block = n_one[m].reshape(256, 1024)
        out = dot_nn(block, wqkv[...].reshape(1024, 384))
        qkv[:, m] = out.astype(BF).reshape(8, 32, 384)

    for b in range(4):
        wait_for(cot.at[k, b, c], tr_r.at[1, b])
    ag_send(cot, 1)

    wait_for(lens, ln_r)
    lane = lax.broadcasted_iota(jnp.int32, (128, 128), 1)
    row = lax.broadcasted_iota(jnp.int32, (128, 128), 0)
    first = lane < 64

    def two_heads(v):
        zero = jnp.zeros_like(v)
        return jnp.concatenate(
            [jnp.where(first, v, zero), jnp.where(first, zero, v)], axis=0
        )

    def one_of_two(v):
        return jnp.where(first, v[:128], v[128:])

    def part_of(t0, t1, col):
        return qkv[t0:t1, :, :, col * 128 : (col + 1) * 128].reshape((t1 - t0) * 128, 128)

    for t in range(8):
        span = (t + 1) * 128
        q = two_heads(part_of(t, t + 1, 0).astype(F32) * 0.125).astype(BF)
        keys = part_of(0, t + 1, 1)
        vals = part_of(0, t + 1, 2)
        pos = row + t * 128
        begin = jnp.zeros((128, 128), jnp.int32)
        end = jnp.zeros((1, 128), jnp.int32)
        for g in range(4):
            length = lens[g : g + 1, :]
            end = end + length
            begin = begin + jnp.where(end <= pos, length, 0)
        allowed = []
        for u in range(t + 1):
            ok = begin <= lane + u * 128
            if u == t:
                ok = ok & (lane <= row)
            allowed.append(ok)
        allowed = jnp.concatenate(allowed, axis=1)
        scores = dot_right(q, keys)
        sums = []
        raws = []
        for h in range(2):
            sc = jnp.where(allowed, scores[h * 128 : (h + 1) * 128], -1e30)
            top = jnp.max(sc, axis=-1, keepdims=True)
            expo = jnp.exp(sc - top)
            low = expo.astype(BF)
            probs[t, h * 128 : (h + 1) * 128, 0:span] = low
            sums.append(jnp.sum(low.astype(F32), axis=-1, keepdims=True))
        raw = dot_nn(probs[t, :, 0:span], vals)
        both = jnp.where(first, sums[0], sums[1])
        attended = one_of_two(raw) / both
        tot[t] = both
        att_f[t] = attended
        att[:, t] = attended.astype(BF).reshape(4, 32, 128)

    for slot in range(4):
        wait_for(wo.at[slot], wo_r.at[slot])

    @pl.loop(0, 4)
    def _(j):
        i = 3 - j
        m = peer(i)
        out = dot_nn(att[m].reshape(256, 128), wo[...].reshape(128, 1024))
        part_a[m] = out.astype(BF).reshape(4, 2, 32, 1024)
        rs_copy(part_a, 0, i).start()

    line_relay(down_block, 2, 1)
    ag_relay(cot, 1, 1)
    ag_relay(cot, 1, 2)
    rs_forward(part_a, 0)
    line_relay(gu_block(0), 1, 0)
    line_relay(gu_block(0), 1, 1)
    ag_relay(cot, 1, 3)
    res = own_l[...].reshape(128, 1024).astype(F32) + rs_sum(part_a, 0)
    resid[...] = res
    r_two = lax.rsqrt(jnp.mean(res * res, axis=-1, keepdims=True) + EPS)
    n_two[k, :, c] = (res * r_two).astype(BF).reshape(4, 32, 1024)
    ag_send(n_two, 2)
    line_relay(gu_block(1), 3, 0)
    line_relay(gu_block(1), 3, 1)

    for i in range(4):
        ag_other(cot, 1, i)
    ag_relay(n_two, 2, 1)
    ag_relay(n_two, 2, 2)
    ag_relay(n_two, 2, 3)
    line_here(down_block, 2)
    own_down.wait()
    line_here(gu_block(0), 1)
    line_here(gu_block(1), 3)

    @pl.loop(0, 4)
    def _(i):
        ag_other(n_two, 2, i)
        m = peer(i)
        gu = dot_nn(n_two[m].reshape(256, 1024), wgu[...].reshape(1024, 768))
        gate = gu[:, :384]
        up = gu[:, 384:]
        sig = jax.nn.sigmoid(gate)
        active = gate * sig
        hid[m] = (active * up).astype(BF)
        slope[m, :, :384] = up * sig * (1.0 + gate * (1.0 - sig))
        slope[m, :, 384:] = active

    @pl.loop(0, 4)
    def _(n):
        cols = pl.ds(pl.multiple_of(n * 256, 256), 256)
        right = cot[:, :, :, :, cols].reshape(1024, 256)
        out = dot_left(hid[...].reshape(1024, 384), right)
        dwd[:, :, cols] = out.astype(BF).reshape(4, 96, 256)

    line_grads(dwd_block, zd, xd, 2, True)

    @pl.loop(0, 4)
    def _(i):
        m = peer(i)
        g_hid = dot_right(cot[m].reshape(256, 1024), wd[...].reshape(384, 1024))
        ggu[m, :, :384] = (g_hid * slope[m, :, :384]).astype(BF)
        ggu[m, :, 384:] = (g_hid * slope[m, :, 384:]).astype(BF)
        out = dot_right(ggu[m], wgu[...].reshape(1024, 768))
        part_b[m] = out.astype(BF).reshape(4, 2, 32, 1024)
        rs_copy(part_b, 1, i).start()

    rs_forward(part_b, 1)

    @pl.loop(0, 4)
    def _(d):
        cols = pl.ds(pl.multiple_of(d * 256, 256), 256)
        left = n_two[:, :, :, :, cols].reshape(1024, 256)
        out = dot_left(left, ggu[...].reshape(1024, 768))
        dwgu[d] = out.astype(BF).reshape(4, 2, 32, 768)

    line_grads(dwgu_block, zgu, xgu, 1, True)
    line_grads_relay(dwd_block, zd, xd, 2, 0)
    line_grads_relay(dwd_block, zd, xd, 2, 1)

    @pl.loop(0, 4)
    def _(i):
        m = peer(i)
        out = dot_nn(hid[m], wd[...].reshape(384, 1024))
        part_c[m] = out.astype(BF).reshape(4, 2, 32, 1024)
        rs_copy(part_c, 2, i).start()

    scaled = rs_sum(part_b, 1)
    res = resid[...]
    r_two = lax.rsqrt(jnp.mean(res * res, axis=-1, keepdims=True) + EPS)
    normed = res * r_two
    inner = jnp.mean(scaled * normed, axis=-1, keepdims=True)
    g_res = cot[k, :, c].reshape(128, 1024).astype(F32) + r_two * (scaled - normed * inner)
    gres[...] = g_res
    gbr[k, :, c] = g_res.astype(BF).reshape(4, 32, 1024)
    ag_send(gbr, 3)

    ag_relay(gbr, 3, 1)
    ag_relay(gbr, 3, 2)
    ag_relay(gbr, 3, 3)
    line_grads_relay(dwgu_block, zgu, xgu, 1, 0)
    rs_forward(part_c, 2)

    @pl.loop(0, 4)
    def _(i):
        ag_other(gbr, 3, i)
        m = peer(i)
        out = dot_right(gbr[m].reshape(256, 1024), wo[...].reshape(128, 1024))
        gatt[:, m] = out.astype(BF).reshape(8, 32, 128)

    for t in range(8):
        span = (t + 1) * 128
        keys = part_of(0, t + 1, 1)
        vals = part_of(0, t + 1, 2)
        ratio = gatt[t].reshape(128, 128).astype(F32) / tot[t]
        g_raw = two_heads(ratio.astype(BF).astype(F32)).astype(BF)
        graw_two[t] = g_raw
        q_two[t] = two_heads(part_of(t, t + 1, 0).astype(F32)).astype(BF)
        prod = ratio * att_f[t]
        g_tot = -jnp.sum(two_heads(prod), axis=-1, keepdims=True)
        g_pr = dot_right(g_raw, vals)
        g_sc = probs[t, :, 0:span].astype(F32) * (g_pr + g_tot)
        gsc[t, :, 0:span] = g_sc.astype(BF)
        g_q = one_of_two(dot_nn(gsc[t, :, 0:span], keys)) * 0.125
        gqkv[:, t, :, 0:128] = g_q.astype(BF).reshape(4, 32, 128)
    line_grads_relay(dwgu_block, zgu, xgu, 1, 1)
    for u in range(8):
        cols = slice(u * 128, (u + 1) * 128)
        rows = (8 - u) * 256
        g_k = dot_left(gsc[u:, :, cols].reshape(rows, 128), q_two[u:].reshape(rows, 128)) * 0.125
        g_v = dot_left(probs[u:, :, cols].reshape(rows, 128), graw_two[u:].reshape(rows, 128))
        gqkv[:, u, :, 128:256] = g_k.astype(BF).reshape(4, 32, 128)
        gqkv[:, u, :, 256:384] = g_v.astype(BF).reshape(4, 32, 128)

    rs_end(part_a, 0)

    @pl.loop(0, 4)
    def _(j):
        i = 3 - j
        m = peer(i)
        out = dot_right(gqkv[m].reshape(256, 384), wqkv[...].reshape(1024, 384))
        part_a[m] = out.astype(BF).reshape(4, 2, 32, 1024)
        rs_copy(part_a, 3, i).start()


    @pl.loop(0, 4)
    def _(d):
        cols = pl.ds(pl.multiple_of(d * 256, 256), 256)
        left = n_one[:, :, :, :, cols].reshape(1024, 256)
        out = dot_left(left, gqkv[...].reshape(1024, 384))
        dwqkv[d] = out.astype(BF).reshape(4, 2, 32, 384)

    line_grads(dwqkv_block, zq, xq, 0, True)
    rs_forward(part_a, 3)
    line_grads_relay(dwqkv_block, zq, xq, 0, 0)
    line_grads_relay(dwqkv_block, zq, xq, 0, 1)

    @pl.loop(0, 4)
    def _(n):
        cols = pl.ds(pl.multiple_of(n * 256, 256), 256)
        right = gbr[:, :, :, :, cols].reshape(1024, 256)
        out = dot_left(att[...].reshape(1024, 128), right)
        dwo[:, :, cols] = out.astype(BF).reshape(4, 32, 256)

    def out_grads(start):
        for p in range(2):
            for cs in range(2):
                zz = 2 * c + p
                here = (zz == z) & (c == cs)
                src = dwo.at[2 * p + cs]

                @pl.when(here)
                def _():
                    if start:
                        pltpu.make_async_copy(src, go_o.at[z], go_r.at[z]).start()

                @pl.when(jnp.logical_not(here))
                def _():
                    copy = remote(
                        src, go_o.at[z], go_s.at[2 * p + cs], go_r.at[z], dev(k, zz, cs)
                    )
                    if start:
                        copy.start()
                    else:
                        copy.wait_send()

    out_grads(True)

    def gather_back(which, dst, start):
        for b in range(4):
            here = (z == k) & (z == b)
            src = back.at[which, b]
            place = dst.at[pl.ds(pl.multiple_of(32 * k, 32), 32)]

            @pl.when(here)
            def _():
                if start:
                    pltpu.make_async_copy(src, place, tb_r.at[which, k]).start()

            @pl.when(jnp.logical_not(here))
            def _():
                copy = remote(src, place, tb_s.at[which, b], tb_r.at[which, k], dev(z, b, c))
                if start:
                    copy.start()
                else:
                    copy.wait_send()

    out_f = resid[...] + rs_sum(part_c, 2)
    back[0] = out_f.astype(BF).reshape(4, 32, 1024)
    gather_back(0, lat_o, True)

    def plane_grads(land, dst, which, start):
        for i in range(4):
            m = peer(i)
            for same in (True, False):
                cc = c if same else oc
                src = land.at[z, m, cc]
                place = dst.at[rank]
                if i == 0 and same:
                    if start:
                        pltpu.make_async_copy(src, place, ga_r.at[which, rank]).start()
                else:
                    copy = remote(
                        src,
                        place,
                        ga_s.at[which, 2 * i + (0 if same else 1)],
                        ga_r.at[which, rank],
                        dev(m, z, cc),
                    )
                    if start:
                        copy.start()
                    else:
                        copy.wait_send()

    scaled = rs_sum(part_a, 3)
    lat_f = own_l[...].reshape(128, 1024).astype(F32)
    r_one = lax.rsqrt(jnp.mean(lat_f * lat_f, axis=-1, keepdims=True) + EPS)
    normed = lat_f * r_one
    inner = jnp.mean(scaled * normed, axis=-1, keepdims=True)
    d_lat = gres[...] + r_one * (scaled - normed * inner)
    back[1] = d_lat.astype(BF).reshape(4, 32, 1024)
    gather_back(1, dlat_o, True)
    zgu[z] = line_sum(dwgu_block, zgu, 1).astype(BF)
    plane_grads(zgu, ggu_o, 1, True)


    down_sum[...] = line_sum(dwd_block, zd, 2)
    down_out = pltpu.make_async_copy(down_sum, gd_o, gd_r)
    down_out.start()
    zq[z] = line_sum(dwqkv_block, zq, 0).astype(BF)
    plane_grads(zq, gqkv_o, 0, True)

    for which, dst in ((0, lat_o), (1, dlat_o)):
        for b in range(4):
            wait_for(dst.at[pl.ds(32 * b, 32)], tb_r.at[which, b])
    for b in range(4):
        wait_for(go_o.at[b], go_r.at[b])
    for which, dst in ((1, ggu_o), (0, gqkv_o)):
        for r in range(RANKS):
            wait_for(dst.at[r], ga_r.at[which, r])
    spread(lat_in, lat_place, 0, False)
    spread_on(lat_in, lat_place, 0, False)
    spread(dout_in, cot_place, 1, False)
    spread_on(dout_in, cot_place, 1, False)
    spread_lens(False)
    plane_weights(wqkv_in, wqkv, 0, False)
    plane_weights(wgu_in, wgu, 1, False)
    line_sent(qkv_block, 0)
    line_sent(gu_block(0), 1)
    line_sent(gu_block(1), 3)
    line_sent(down_block, 2, wd_in)
    down_out.wait()
    out_weights(False)
    for which, buf in enumerate((n_one, cot, n_two, gbr)):
        ag_end(buf, which)
    rs_end(part_b, 1)
    rs_end(part_c, 2)
    rs_end(part_a, 3)
    line_grads(dwgu_block, zgu, xgu, 1, False)
    line_grads(dwqkv_block, zq, xq, 0, False)
    line_grads(dwd_block, zd, xd, 2, False)
    plane_grads(zgu, ggu_o, 1, False)
    plane_grads(zq, gqkv_o, 0, False)
    out_grads(False)
    gather_back(0, lat_o, False)
    gather_back(1, dlat_o, False)


def run_layer(lat, dout, lengths, gain_one, gain_two, weights):
    vm = pltpu.VMEM
    dma = pltpu.SemaphoreType.DMA
    rows = (4, 4, 2, 32)
    return pl.pallas_call(
        layer_kernel,
        out_shape=(
            jax.ShapeDtypeStruct((128, 1024), BF),
            jax.ShapeDtypeStruct((128, 1024), BF),
            jax.ShapeDtypeStruct((RANKS, 32, 384), BF),
            jax.ShapeDtypeStruct((RANKS, 32, 768), BF),
            jax.ShapeDtypeStruct((96, 1024), F32),
            jax.ShapeDtypeStruct((4, 32, 1024), BF),
        ),
        in_specs=[pl.BlockSpec(memory_space=pl.ANY)] * 2
        + [pl.BlockSpec(memory_space=pltpu.SMEM)]
        + [pl.BlockSpec(memory_space=pltpu.VMEM)] * 9,
        out_specs=[pl.BlockSpec(memory_space=pl.ANY)] * 6,
        scratch_shapes=[
            vm((8, 128), jnp.int32),
            vm((RANKS, 32, 384), BF),
            vm((RANKS, 32, 768), BF),
            vm((96, 1024), BF),
            vm((4, 32, 1024), BF),
            vm((2, 4, 32, 1024), BF),
            vm((8, 128), jnp.int32),
            vm(rows + (1024,), BF),
            vm(rows + (1024,), BF),
            vm(rows + (1024,), BF),
            vm(rows + (1024,), BF),
            vm(rows + (384,), BF),
            vm(rows + (768,), BF),
            vm((4, 96, 1024), BF),
            vm((4, 32, 1024), BF),
            vm((8, 4, 32, 384), BF),
            vm((4, 8, 32, 128), BF),
            vm((8, 128, 128), F32),
            vm((8, 128, 128), F32),
            vm((8, 256, 1024), BF),
            vm((8, 256, 1024), BF),
            vm(rows + (1024,), BF),
            vm(rows + (1024,), BF),
            vm(rows + (1024,), BF),
            vm((4, 4, 4, 32, 1024), BF),
            vm((4, 2, 4, 32, 1024), BF),
            vm((4, 2, 2, 32, 1024), BF),
            vm((4, 256, 384), BF),
            vm((4, 256, 768), BF),
            vm((4, 256, 768), F32),
            vm((8, 4, 32, 128), BF),
            vm((8, 256, 128), BF),
            vm((8, 256, 128), BF),
            vm((4, 8, 32, 384), BF),
            vm(rows + (384,), BF),
            vm(rows + (768,), BF),
            vm((4, 96, 1024), BF),
            vm((4, 32, 1024), BF),
            vm((4, 4, 2, 32, 384), BF),
            vm((4, 4, 2, 32, 768), BF),
            vm((4, 96, 1024), BF),
            vm((2, 4, 2, 32, 384), BF),
            vm((2, 4, 2, 32, 768), BF),
            vm((2, 96, 1024), BF),
            vm((96, 1024), F32),
            vm((128, 1024), F32),
            vm((128, 1024), F32),
            vm((2, 4, 32, 1024), BF),
            dma((2, 4)),
            dma((2, 4)),
            dma((2, 4)),
            dma((2, 4)),
            dma,
            dma,
            dma((2, 8)),
            dma((2, 8)),
            dma((4, 4)),
            dma((4, 4)),
            dma,
            dma((4,)),
            dma((4,)),
            dma((4, 12)),
            dma((4, 4)),
            dma((4, 4)),
            dma((4, 2)),
            dma((4, 12)),
            dma((4, 4)),
            dma((4, 2, 2)),
            dma((4, 2)),
            dma((3, 4)),
            dma((3, 4)),
            dma((3, 2)),
            dma((2, 8)),
            dma((2, 8)),
            dma,
            dma((4,)),
            dma((4,)),
            dma((2, 4)),
            dma((2, 4)),
        ],
        compiler_params=pltpu.CompilerParams(
            collective_id=0, has_side_effects=True, vmem_limit_bytes=60 * 1024 * 1024
        ),
    )(lat, dout, lengths, gain_one, gain_two, *weights)


def finish_kernel(
    lat,
    dlat,
    gqkv,
    ggu,
    gd,
    go,
    gain_one,
    gain_two,
    wq,
    wk,
    wv,
    wg,
    wu,
    lat_o,
    dlat_o,
    g_one_o,
    gq_o,
    gk_o,
    gv_o,
    go_o,
    g_two_o,
    gg_o,
    gu_o,
    gd_o,
):
    lat_o[0] = lat[...]
    dlat_o[0] = dlat[...]
    go_o[...] = (go[0].astype(F32) + go[1].astype(F32)) + (go[2].astype(F32) + go[3].astype(F32))
    gd_o[...] = gd[0:88]
    col_one = jnp.sum(on_diagonal(gain_one[...]), axis=1, keepdims=True)
    col_two = jnp.sum(on_diagonal(gain_two[...]), axis=1, keepdims=True)

    def as_row(acc):
        return jnp.sum(on_diagonal(jnp.sum(acc, axis=1, keepdims=True)), axis=0, keepdims=True)

    acc = jnp.zeros((32, 128), F32)
    for i, (w, out) in enumerate(((wq, gq_o), (wk, gk_o), (wv, gv_o))):
        for r in range(RANKS):
            cols = slice(r * 128, (r + 1) * 128)
            part = gqkv[r, :, i * 128 : (i + 1) * 128].astype(F32)
            out[:, cols] = part * col_one
            acc = acc + part * w[:, cols].astype(F32)
    g_one_o[...] = as_row(acc)
    acc = jnp.zeros((32, 256), F32)
    for i, (w, out) in enumerate(((wg, gg_o), (wu, gu_o))):
        parts = [None] * 32
        for r in range(RANKS):
            whole = ggu[r, :, i * 384 : (i + 1) * 384].astype(F32)
            for b in range(ZS):
                parts[8 * (r // CORES) + CORES * b + r % CORES] = whole[:, b * 96 : b * 96 + 88]
        rows = jnp.concatenate(parts, axis=1)
        out[...] = rows * col_two
        prod = rows * w[...].astype(F32)
        for n in range(11):
            acc = acc + prod[:, n * 256 : (n + 1) * 256]
    g_two_o[...] = as_row(acc)


def finish(*arrays):
    outs = (
        ((1, 128, 1024), BF),
        ((1, 128, 1024), BF),
        ((1, 32), F32),
        ((32, 1024), F32),
        ((32, 1024), F32),
        ((32, 1024), F32),
        ((32, 1024), F32),
        ((1, 32), F32),
        ((32, 2816), F32),
        ((32, 2816), F32),
        ((88, 1024), F32),
    )
    return pl.pallas_call(
        finish_kernel,
        out_shape=tuple(jax.ShapeDtypeStruct(*o) for o in outs),
        in_specs=[pl.BlockSpec(memory_space=pltpu.VMEM)] * len(arrays),
        out_specs=[pl.BlockSpec(memory_space=pltpu.VMEM)] * len(outs),
        compiler_params=pltpu.CompilerParams(vmem_limit_bytes=32 * 1024 * 1024),
    )(*arrays)


def plane_device(
    latents,
    d_out,
    lengths,
    gain_attn,
    w_query,
    w_key,
    w_value,
    w_out,
    gain_ffn,
    w_gate,
    w_up,
    w_down,
):
    gains = gain_attn.reshape(1, 32), gain_ffn.reshape(1, 32)
    weights = w_query, w_key, w_value, w_gate, w_up, w_down, w_out
    parts = run_layer(latents[0], d_out[0], lengths, *gains, weights)
    outs = finish(*parts, *gains, w_query, w_key, w_value, w_gate, w_up)
    return tuple(o.reshape(32) if o.shape == (1, 32) else o for o in outs)


def solution(mesh):
    return jax.shard_map(
        plane_device if planes_fit(mesh) else per_device,
        mesh=mesh,
        in_specs=(
            P("dp", "seq", None),
            P("dp", "seq", None),
            P("dp", None),
            P(("dp", "seq")),
            P(("dp", "seq"), None),
            P(("dp", "seq"), None),
            P(("dp", "seq"), None),
            P(("dp", "seq"), None),
            P(("dp", "seq")),
            P(("dp", "seq"), None),
            P(("dp", "seq"), None),
            P(("dp", "seq"), None),
        ),
        out_specs=(
            P("dp", "seq", None),
            P("dp", "seq", None),
            P(("dp", "seq")),
            P(("dp", "seq"), None),
            P(("dp", "seq"), None),
            P(("dp", "seq"), None),
            P(("dp", "seq"), None),
            P(("dp", "seq")),
            P(("dp", "seq"), None),
            P(("dp", "seq"), None),
            P(("dp", "seq"), None),
        ),
        check_vma=False,
    )
```

```python
import functools
import math

import jax
import jax.numpy as jnp
from jax import lax
from jax.experimental import pallas as pl
from jax.experimental.pallas import tpu as pltpu
from jax.sharding import PartitionSpec as P

HEADS = 16


EPS = 1e-05


def norm_rows(values, gain_vec):
    factor = lax.rsqrt(jnp.mean(values * values, axis=-1, keepdims=True) + EPS)
    normed = values * factor
    return (normed * gain_vec, normed, factor)


def norm_back(grad_out, normed, factor, gain_vec):
    scaled = grad_out * gain_vec
    inner = jnp.mean(scaled * normed, axis=-1, keepdims=True)
    return (factor * (scaled - normed * inner), jnp.sum(grad_out * normed, axis=0))


def dot_left(left, right):
    return lax.dot_general(
        left, right, (((0,), (0,)), ((), ())), preferred_element_type=jnp.float32
    )


def dot_right(left, right):
    return lax.dot_general(
        left, right, (((1,), (1,)), ((), ())), preferred_element_type=jnp.float32
    )


def per_device(
    latents,
    d_out,
    lengths,
    gain_attn,
    w_query,
    w_key,
    w_value,
    w_out,
    gain_ffn,
    w_gate,
    w_up,
    w_down,
):
    g_attn, full_query, full_key, full_value, full_out, g_ffn, full_gate, full_up, full_down = (
        lax.all_gather(gain_attn, ("dp", "seq"), axis=0, tiled=True),
        lax.all_gather(w_query, ("dp", "seq"), axis=0, tiled=True),
        lax.all_gather(w_key, ("dp", "seq"), axis=0, tiled=True),
        lax.all_gather(w_value, ("dp", "seq"), axis=0, tiled=True),
        lax.all_gather(w_out, ("dp", "seq"), axis=0, tiled=True),
        lax.all_gather(gain_ffn, ("dp", "seq"), axis=0, tiled=True),
        lax.all_gather(w_gate, ("dp", "seq"), axis=0, tiled=True),
        lax.all_gather(w_up, ("dp", "seq"), axis=0, tiled=True),
        lax.all_gather(w_down, ("dp", "seq"), axis=0, tiled=True),
    )
    gain_one = g_attn.astype(jnp.float32)
    gain_two = g_ffn.astype(jnp.float32)
    inputs_f = latents[0].astype(jnp.float32)
    row_count, model_width = inputs_f.shape
    head_size = model_width // HEADS
    group_rows = row_count * lax.axis_size("seq")
    here = lax.axis_index("seq") * row_count + jnp.arange(row_count, dtype=jnp.int32)
    seq_lens = lengths[0]
    seq_ends = jnp.cumsum(seq_lens, dtype=jnp.int32)
    begins = jnp.sum(
        jnp.where(seq_ends[None, :] <= here[:, None], seq_lens[None, :], 0), axis=1, dtype=jnp.int32
    )
    key_block = math.gcd(group_rows, 1024)
    block_count = group_rows // key_block
    key_positions = jnp.arange(group_rows, dtype=jnp.int32).reshape(block_count, key_block)
    h_one_f, normed_one, factor_one = norm_rows(inputs_f, gain_one)
    h_one = h_one_f.astype(jnp.bfloat16)
    query_proj = jnp.dot(h_one, full_query, preferred_element_type=jnp.float32).astype(jnp.bfloat16)
    key_proj = jnp.dot(h_one, full_key, preferred_element_type=jnp.float32).astype(jnp.bfloat16)
    value_proj = jnp.dot(h_one, full_value, preferred_element_type=jnp.float32).astype(jnp.bfloat16)
    keys_all, values_all = (
        lax.all_gather(key_proj, "seq", axis=0, tiled=True),
        lax.all_gather(value_proj, "seq", axis=0, tiled=True),
    )
    query_heads = query_proj.reshape(row_count, HEADS, head_size)

    def split_blocks(array):
        return array.reshape(block_count, key_block, HEADS, head_size)

    def block_scores(key_piece, pos_piece):
        scores = (
            jnp.einsum("qhd,khd->hqk", query_heads, key_piece, preferred_element_type=jnp.float32)
            * 0.125
        )
        allowed = (pos_piece[None, :] <= here[:, None]) & (pos_piece[None, :] >= begins[:, None])
        return (scores, allowed[None])

    def max_step(running, pieces):
        key_piece, pos_piece = pieces
        scores, allowed = block_scores(key_piece, pos_piece)
        return (jnp.maximum(running, jnp.max(jnp.where(allowed, scores, -1e30), axis=-1)), None)

    row_max, _ = lax.scan(
        max_step,
        jnp.full((HEADS, row_count), -1e30, jnp.float32),
        (split_blocks(keys_all), key_positions),
    )

    def sum_step(running, pieces):
        key_piece, value_piece, pos_piece = pieces
        scores, allowed = block_scores(key_piece, pos_piece)
        expon = jnp.where(
            allowed, jnp.exp(jnp.where(allowed, scores, -1e30) - row_max[:, :, None]), 0.0
        )
        rounded = expon.astype(jnp.bfloat16)
        total_sum, raw_sum = running
        total_sum = total_sum + jnp.sum(rounded.astype(jnp.float32), axis=-1)
        raw_sum = raw_sum + jnp.einsum(
            "hqk,khd->qhd", rounded, value_piece, preferred_element_type=jnp.float32
        )
        return ((total_sum, raw_sum), None)

    (total_sum, raw_sum), _ = lax.scan(
        sum_step,
        (
            jnp.zeros((HEADS, row_count), jnp.float32),
            jnp.zeros((row_count, HEADS, head_size), jnp.float32),
        ),
        (split_blocks(keys_all), split_blocks(values_all), key_positions),
    )
    totals_rows = jnp.transpose(total_sum)
    attended = raw_sum / totals_rows[:, :, None]
    attended_low = attended.reshape(row_count, model_width).astype(jnp.bfloat16)
    resid = inputs_f + jnp.dot(attended_low, full_out, preferred_element_type=jnp.float32)
    h_two_f, normed_two, factor_two = norm_rows(resid, gain_two)
    h_two = h_two_f.astype(jnp.bfloat16)
    gate_proj = jnp.dot(h_two, full_gate, preferred_element_type=jnp.float32)
    up_proj = jnp.dot(h_two, full_up, preferred_element_type=jnp.float32)
    gate_sigmoid = jax.nn.sigmoid(gate_proj)
    gate_active = gate_proj * gate_sigmoid
    hidden = (gate_active * up_proj).astype(jnp.bfloat16)
    outputs = resid + jnp.dot(hidden, full_down, preferred_element_type=jnp.float32)
    latents_out = outputs.astype(jnp.bfloat16)[None]
    grad_out = d_out[0]
    grad_down = dot_left(hidden, grad_out)
    g_hidden = dot_right(grad_out, full_down)
    g_gate = (g_hidden * up_proj * gate_sigmoid * (1.0 + gate_proj * (1.0 - gate_sigmoid))).astype(
        jnp.bfloat16
    )
    g_up = (g_hidden * gate_active).astype(jnp.bfloat16)
    grad_gate = dot_left(h_two, g_gate)
    grad_up = dot_left(h_two, g_up)
    g_h_two = dot_right(g_gate, full_gate) + dot_right(g_up, full_up)
    g_norm_two, grad_gain_two = norm_back(g_h_two, normed_two, factor_two, gain_two)
    g_resid = grad_out.astype(jnp.float32) + g_norm_two
    g_branch = g_resid.astype(jnp.bfloat16)
    grad_out_proj = dot_left(attended_low, g_branch)
    g_att = dot_right(g_branch, full_out).reshape(row_count, HEADS, head_size).astype(jnp.bfloat16)
    g_att_f = g_att.astype(jnp.float32)
    g_raw = (g_att_f / totals_rows[:, :, None]).astype(jnp.bfloat16)
    g_total = jnp.transpose(-jnp.sum(g_att_f * raw_sum, axis=-1) / (totals_rows * totals_rows))
    keys_back, values_back = (
        lax.all_gather(key_proj, "seq", axis=0, tiled=True),
        lax.all_gather(value_proj, "seq", axis=0, tiled=True),
    )

    def score_grads(key_piece, value_piece, pos_piece):
        scores, allowed = block_scores(key_piece, pos_piece)
        expon = jnp.where(
            allowed, jnp.exp(jnp.where(allowed, scores, -1e30) - row_max[:, :, None]), 0.0
        )
        g_probs = jnp.einsum("qhd,khd->hqk", g_raw, value_piece, preferred_element_type=jnp.float32)
        g_scores = (expon * (g_probs + g_total[:, :, None])).astype(jnp.bfloat16)
        return (expon, g_scores)

    def grad_step(running, pieces):
        key_piece, value_piece, pos_piece = pieces
        expon, g_scores = score_grads(key_piece, value_piece, pos_piece)
        rounded = expon.astype(jnp.bfloat16)
        running = (
            running
            + jnp.einsum("hqk,khd->qhd", g_scores, key_piece, preferred_element_type=jnp.float32)
            * 0.125
        )
        g_key_piece = (
            jnp.einsum("hqk,qhd->khd", g_scores, query_heads, preferred_element_type=jnp.float32)
            * 0.125
        )
        g_value_piece = jnp.einsum(
            "hqk,qhd->khd", rounded, g_raw, preferred_element_type=jnp.float32
        )
        return (running, (g_key_piece, g_value_piece))

    g_query_f, (g_keys, g_values) = lax.scan(
        grad_step,
        jnp.zeros((row_count, HEADS, head_size), jnp.float32),
        (split_blocks(keys_back), split_blocks(values_back), key_positions),
    )
    mine_key, mine_value = (
        lax.psum_scatter(
            g_keys.reshape(group_rows, model_width).astype(jnp.bfloat16),
            "seq",
            scatter_dimension=0,
            tiled=True,
        ).astype(jnp.float32),
        lax.psum_scatter(
            g_values.reshape(group_rows, model_width).astype(jnp.bfloat16),
            "seq",
            scatter_dimension=0,
            tiled=True,
        ).astype(jnp.float32),
    )
    g_key = mine_key.astype(jnp.bfloat16)
    g_value = mine_value.astype(jnp.bfloat16)
    g_query = g_query_f.reshape(row_count, model_width).astype(jnp.bfloat16)
    grad_query = dot_left(h_one, g_query)
    grad_key = dot_left(h_one, g_key)
    grad_value = dot_left(h_one, g_value)
    g_h_one = (
        dot_right(g_query, full_query) + dot_right(g_key, full_key) + dot_right(g_value, full_value)
    )
    g_norm_one, grad_gain_one = norm_back(g_h_one, normed_one, factor_one, gain_one)
    d_latents = (g_resid + g_norm_one).astype(jnp.bfloat16)[None]
    gain_pair = jnp.stack((grad_gain_one, grad_gain_two), axis=1)
    summed = (
        lax.psum_scatter(gain_pair, ("dp", "seq"), scatter_dimension=0, tiled=True),
        lax.psum_scatter(grad_query, ("dp", "seq"), scatter_dimension=0, tiled=True),
        lax.psum_scatter(grad_key, ("dp", "seq"), scatter_dimension=0, tiled=True),
        lax.psum_scatter(grad_value, ("dp", "seq"), scatter_dimension=0, tiled=True),
        lax.psum_scatter(grad_out_proj, ("dp", "seq"), scatter_dimension=0, tiled=True),
        lax.psum_scatter(grad_gate, ("dp", "seq"), scatter_dimension=0, tiled=True),
        lax.psum_scatter(grad_up, ("dp", "seq"), scatter_dimension=0, tiled=True),
        lax.psum_scatter(grad_down, ("dp", "seq"), scatter_dimension=0, tiled=True),
    )
    return (
        latents_out,
        d_latents,
        summed[0][:, 0],
        summed[1],
        summed[2],
        summed[3],
        summed[4],
        summed[0][:, 1],
        summed[5],
        summed[6],
        summed[7],
    )


MESH = pl.DeviceIdType.MESH
BF = jnp.bfloat16
F32 = jnp.float32
DP, ZS, CORES = 4, 4, 2
RANKS = DP * CORES


def planes_fit(mesh):
    return mesh.shape["dp"] == DP and mesh.shape["seq"] == ZS * CORES


def dot_nn(left, right):
    return jnp.dot(left, right, preferred_element_type=F32)


def remote(src, dst, send_sem, recv_sem, device):
    return pltpu.make_async_remote_copy(
        src_ref=src,
        dst_ref=dst,
        send_sem=send_sem,
        recv_sem=recv_sem,
        device_id=device,
        device_id_type=MESH,
    )


def wait_for(ref, sem):
    pltpu.make_async_copy(ref, ref, sem).wait()


def on_diagonal(row):
    at = lax.broadcasted_iota(jnp.int32, (32, 32), 0) == lax.broadcasted_iota(jnp.int32, (32, 32), 1)
    return jnp.where(at, row.astype(F32), 0.0)


def layer_kernel(
    lat_in,
    dout_in,
    lengths_in,
    gain_one,
    gain_two,
    wq_raw,
    wk_raw,
    wv_raw,
    wg_raw,
    wu_raw,
    wd_raw,
    wo_in,
    lat_o,
    dlat_o,
    gqkv_o,
    ggu_o,
    gd_o,
    go_o,
    lens_in,
    wqkv_in,
    wgu_in,
    wd_in,
    own_l,
    stop,
    lens,
    n_one,
    n_two,
    cot,
    gbr,
    wqkv,
    wgu,
    wd,
    wo,
    qkv,
    att,
    att_f,
    tot,
    probs,
    gsc,
    part_a,
    part_b,
    part_c,
    sib,
    rcv,
    turn,
    hid,
    ggu,
    slope,
    gatt,
    graw_two,
    q_two,
    gqkv,
    dwqkv,
    dwgu,
    dwd,
    dwo,
    zq,
    zgu,
    zd,
    xq,
    xgu,
    xd,
    down_sum,
    resid,
    gres,
    back,
    tr_s,
    tr_r,
    tx_r,
    tz_s,
    ln_s,
    ln_r,
    wa_s,
    wa_r,
    wz_s,
    wz_r,
    wd_r,
    wo_s,
    wo_r,
    ag_s,
    ag_r,
    ag_x,
    ag_d,
    rs_s,
    rs_r,
    rs_x,
    rs_d,
    gz_s,
    gz_r,
    gx_r,
    ga_s,
    ga_r,
    gd_r,
    go_s,
    go_r,
    tb_s,
    tb_r,
):
    k = lax.axis_index("dp")
    s = lax.axis_index("seq")
    z = s // CORES
    c = s % CORES
    oc = 1 - c
    rank = CORES * k + c

    def dev(kk, zz, cc):
        return (kk, CORES * zz + cc)

    def peer(i):
        return 2 * ((k // 2 + i // 2) % 2) + (k % 2 + i % 2) % 2

    def zpeer(i):
        return (z + i) % ZS

    sibling = dev(k, z, oc)

    barrier = pltpu.get_barrier_semaphore()
    greeted = 0
    for di in range(4):
        for dz in range(4):
            if di or dz:
                pl.semaphore_signal(
                    barrier, inc=1, device_id=dev(peer(di), zpeer(dz), c), device_id_type=MESH
                )
                greeted += 1
            if di == 0 or dz == 0:
                pl.semaphore_signal(
                    barrier, inc=1, device_id=dev(peer(di), zpeer(dz), oc), device_id_type=MESH
                )
                greeted += 1

    def scaled_rows(w, gain):
        return dot_nn(on_diagonal(gain[...]).astype(BF), w[...])

    for i, w in enumerate((wq_raw, wk_raw, wv_raw)):
        rows = scaled_rows(w, gain_one).astype(BF)
        for r in range(RANKS):
            wqkv_in[r, :, i * 128 : (i + 1) * 128] = rows[:, r * 128 : (r + 1) * 128]
    wd_in[0:80] = wd_raw[0:80]
    wd_in[80:96] = jnp.concatenate([wd_raw[80:88], jnp.zeros((8, 1024), BF)], axis=0)
    tile_row = lax.broadcasted_iota(jnp.int32, (8, 128), 0)
    tile = jnp.zeros((8, 128), jnp.int32)
    for i in range(4):
        tile = jnp.where(tile_row == i, lengths_in[0, i], tile)
    lens_in[...] = tile

    def units_to_ranks():
        for i, w in enumerate((wg_raw, wu_raw)):
            rows = scaled_rows(w, gain_two)
            gap = jnp.zeros((32, 8), F32)
            for r in range(RANKS):
                parts = []
                for b in range(ZS):
                    at = 88 * (8 * (r // CORES) + CORES * b + r % CORES)
                    parts += [rows[:, at : at + 88], gap]
                wgu_in[r, :, i * 384 : (i + 1) * 384] = jnp.concatenate(parts, axis=1).astype(BF)

    pl.semaphore_wait(barrier, greeted)

    def spread(src, final_of, which, start):
        for q in range(4):
            piece = src.at[pl.ds(32 * q, 32)]

            @pl.when((z == k) & (k == q))
            def _():
                if start:
                    pltpu.make_async_copy(piece, final_of(q, z), tr_r.at[which, z]).start()

            @pl.when((z == k) & (k != q))
            def _():
                copy = remote(
                    piece, final_of(q, z), tr_s.at[which, q], tr_r.at[which, z], dev(q, z, c)
                )
                if start:
                    copy.start()
                else:
                    copy.wait_send()

            @pl.when((z != k) & (k != q))
            def _():
                copy = remote(
                    piece, stop.at[which, k], tr_s.at[which, q], tx_r.at[which, k], dev(q, z, c)
                )
                if start:
                    copy.start()
                else:
                    copy.wait_send()

    def spread_on(src, final_of, which, start):
        for i in range(1, 4):
            g = zpeer(i)

            def send(piece):
                copy = remote(
                    piece, final_of(k, z), tz_s.at[which, i], tr_r.at[which, z], dev(k, g, c)
                )
                if start:
                    copy.start()
                else:
                    copy.wait_send()

            @pl.when(g == k)
            def _():
                send(src.at[pl.ds(pl.multiple_of(32 * k, 32), 32)])

            @pl.when(g != k)
            def _():
                if start:
                    wait_for(stop.at[which, g], tx_r.at[which, g])
                send(stop.at[which, g])

    def lat_place(q, b):
        return own_l.at[b]

    def cot_place(q, b):
        return cot.at[q, b, c]

    def spread_lens(start):
        here = z == k

        @pl.when(here)
        def _():
            if start:
                pltpu.make_async_copy(lens_in, lens, ln_r).start()

        @pl.when(jnp.logical_not(here))
        def _():
            copy = remote(lens_in, lens, ln_s, ln_r, dev(z, k, c))
            if start:
                copy.start()
            else:
                copy.wait_send()

    def plane_weights(src, dst, which, start):
        for i in range(4):
            for same in (True, False):
                cc = c if same else oc
                target = CORES * peer(i) + cc
                piece = src.at[target]
                place = dst.at[k, z, c]
                if i == 0 and same:
                    if start:
                        pltpu.make_async_copy(piece, place, wa_r.at[which, rank]).start()
                else:
                    copy = remote(
                        piece,
                        place,
                        wa_s.at[which, 2 * i + (0 if same else 1)],
                        wa_r.at[which, rank],
                        dev(peer(i), z, cc),
                    )
                    if start:
                        copy.start()
                    else:
                        copy.wait_send()

    def plane_weights_here(dst, which):
        for kk in range(4):
            for cc in range(2):
                wait_for(dst.at[kk, z, cc], wa_r.at[which, CORES * kk + cc])

    middle = (z == 1) | (z == 2)
    near = (1 + z % 2, 2 + z // 2 - 2 * (z % 2))
    z_end = 3 * (z // 2)

    def far_of(place):
        return (3 - place, 6 - 3 * place)

    far = far_of(z)

    def line_copy(block, which, slot, b, place, src=None):
        src = block(b) if src is None else src
        return remote(src, block(b), wz_s.at[which, slot], wz_r.at[which, b], dev(k, place, c))

    def line_send(block, which, from_ends, from_middle, start=True, src=None):
        def send(slots):
            for j in slots:
                copy = line_copy(block, which, j, z, near[j], src)
                if start:
                    copy.start()
                else:
                    copy.wait_send()

        if from_ends:

            @pl.when(jnp.logical_not(middle))
            def _():
                send(from_ends)

        if from_middle:

            @pl.when(middle)
            def _():
                send(from_middle)

    def line_relay(block, which, j):
        @pl.when(middle)
        def _():
            wait_for(block(far[j]), wz_r.at[which, far[j]])
            line_copy(block, which, 2 + j, far[j], z_end).start()

    def line_sent(block, which, src=None):
        line_send(block, which, (0, 1), (0, 1), False, src)

        @pl.when(middle)
        def _():
            for j in range(2):
                line_copy(block, which, 2 + j, far[j], z_end).wait_send()

    def line_here(block, which):
        @pl.when(middle)
        def _():
            wait_for(block(z_end), wz_r.at[which, z_end])

        @pl.when(jnp.logical_not(middle))
        def _():
            for i in range(1, 4):
                wait_for(block(zpeer(i)), wz_r.at[which, zpeer(i)])

    def qkv_block(b):
        return wqkv.at[:, b]

    def gu_block(h):
        return lambda b: wgu.at[pl.ds(2 * h, 2), b]

    def down_block(b):
        return wd.at[b]

    def out_weights(start):
        to_core = z // 2
        slot = 2 * (z % 2) + c
        for i in range(4):

            def send():
                copy = remote(
                    wo_in, wo.at[slot], wo_s.at[i], wo_r.at[slot], dev(k, zpeer(i), to_core)
                )
                if start:
                    copy.start()
                else:
                    copy.wait_send()

            if i == 0:

                @pl.when(to_core == c)
                def _():
                    if start:
                        pltpu.make_async_copy(wo_in, wo.at[slot], wo_r.at[slot]).start()

                @pl.when(to_core != c)
                def _():
                    send()

            else:
                send()

    def half(j):
        return pl.ds(2 * j, 2)

    def ag_copy(buf, which, i, j):
        own = buf.at[k, half(j), c]
        return remote(
            own, own, ag_s.at[which, 2 * i + j], ag_r.at[which, k, j], dev(peer(i), z, c)
        )

    def ag_turn(buf, which, i):
        block = buf.at[peer(i), half(i - 1), c]
        return remote(
            block, block, ag_s.at[which, 9 + i], ag_d.at[which, i - 1], dev(peer(3 - i), z, c)
        )

    def ag_across(buf, which, i):
        block = buf.at[peer(i), :, c]
        return remote(
            block, block, ag_s.at[which, 6 + i], ag_x.at[which, peer(i)], sibling
        )

    def ag_send(buf, which):
        for i, j in ((1, 0), (2, 1), (1, 1), (2, 0)):
            ag_copy(buf, which, i, j).start()
        ag_across(buf, which, 0).start()

    def ag_corner(buf, which):
        for i in (1, 2):
            m = peer(i)
            wait_for(buf.at[m, half(i - 1), c], ag_r.at[which, m, i - 1])
            ag_turn(buf, which, i).start()

    def ag_relay(buf, which, i):
        m = peer(i)
        if i < 3:
            wait_for(buf.at[m, half(2 - i), c], ag_r.at[which, m, 2 - i])
        else:
            for j in range(2):
                wait_for(buf.at[m, half(j), c], ag_d.at[which, j])
        ag_across(buf, which, i).start()

    def ag_other(buf, which, i):
        m = peer(i)
        wait_for(buf.at[m, :, oc], ag_x.at[which, m])

    def ag_end(buf, which):
        for i in (1, 2):
            for j in range(2):
                ag_copy(buf, which, i, j).wait_send()
            ag_turn(buf, which, i).wait_send()
        for i in range(4):
            ag_across(buf, which, i).wait_send()

    def rs_copy(part, which, i):
        m = peer(i)
        return remote(
            part.at[m, :, oc], sib.at[which, m], rs_s.at[which, i], rs_r.at[which, m], sibling
        )

    def rs_part(part, which, i, j):
        m = peer(i)
        return remote(
            part.at[m, half(j), c],
            rcv.at[which, i - 1, half(j)],
            rs_s.at[which, 2 + 2 * i + j],
            rs_x.at[which, i - 1, j],
            dev(m, z, c),
        )

    def rs_turn(part, which, j):
        return remote(
            part.at[peer(3), half(j), c],
            turn.at[which, j],
            rs_s.at[which, 8 + j],
            rs_d.at[which, j],
            dev(peer(j + 1), z, c),
        )

    def rs_pair(part, which, i):
        m = peer(i)
        wait_for(sib.at[which, m], rs_r.at[which, m])
        return part[m, :, c].astype(F32) + sib[which, m].astype(F32)

    def rs_halves(part, which, i):
        m = peer(i)
        part[m, :, c] = rs_pair(part, which, i).astype(BF)
        if i == 3:
            for j in range(2):
                rs_turn(part, which, j).start()
        else:
            rs_part(part, which, i, i - 1).start()

    def rs_start(part, which, compute):
        for i, ready in ((3, None), (1, 3), (2, 1), (0, 2)):
            compute(i)
            rs_copy(part, which, i).start()
            if ready:
                rs_halves(part, which, ready)

    def rs_corner(part, which):
        for j in range(2):
            wait_for(turn.at[which, j], rs_d.at[which, j])
            m = peer(2 - j)
            sums = part[m, half(j), c].astype(F32) + turn[which, j].astype(F32)
            part[m, half(j), c] = sums.astype(BF)
            rs_part(part, which, 2 - j, j).start()

    def rs_sum(part, which):
        total = rs_pair(part, which, 0)
        for i in (1, 2):
            for j in range(2):
                wait_for(rcv.at[which, i - 1, half(j)], rs_x.at[which, i - 1, j])
            total = total + rcv[which, i - 1].astype(F32)
        return total.reshape(128, 1024)

    def rs_end(part, which):
        for i in range(4):
            rs_copy(part, which, i).wait_send()
        for j in range(2):
            rs_turn(part, which, j).wait_send()
            for i in (1, 2):
                rs_part(part, which, i, j).wait_send()

    def grads_to_far(grad, land, which, j):
        return remote(
            grad(far[j]), land.at[z], gz_s.at[which, 1 + j], gz_r.at[which, z], dev(k, far[j], c)
        )

    def line_grads(grad, land, add, which, start):
        @pl.when(middle)
        def _():
            copy = remote(
                grad(z_end), land.at[z], gz_s.at[which, 0], gz_r.at[which, z], dev(k, z_end, c)
            )
            if start:
                copy.start()
            else:
                copy.wait_send()
                for j in range(2):
                    grads_to_far(grad, land, which, j).wait_send()

        @pl.when(jnp.logical_not(middle))
        def _():
            mid = 1 + z // 2
            for j in range(2):
                copy = remote(
                    grad(far_of(mid)[j]),
                    add.at[j],
                    gz_s.at[which, j],
                    gx_r.at[which, j],
                    dev(k, mid, c),
                )
                if start:
                    copy.start()
                else:
                    copy.wait_send()
            copy = remote(
                grad(mid), land.at[z], gz_s.at[which, 2], gz_r.at[which, z], dev(k, mid, c)
            )
            if start:
                copy.start()
            else:
                copy.wait_send()

    def line_grads_relay(grad, land, add, which, j):
        @pl.when(middle)
        def _():
            wait_for(add.at[j], gx_r.at[which, j])
            mine = grad(far[j])
            mine[...] = (mine[...].astype(F32) + add[j].astype(F32)).astype(BF)
            grads_to_far(grad, land, which, j).start()

    def line_sum(grad, land, which):
        total = grad(z)[...].astype(F32)
        for j in range(2):
            wait_for(land.at[near[j]], gz_r.at[which, near[j]])
            total = total + land[near[j]].astype(F32)
        return total

    def dwgu_block(b):
        return dwgu.at[:, b]

    def dwqkv_block(b):
        return dwqkv.at[:, b]

    def dwd_block(b):
        return dwd.at[b]

    spread(lat_in, lat_place, 0, True)
    plane_weights(wqkv_in, wqkv, 0, True)
    spread_lens(True)
    line_send(down_block, 2, (0,), (0, 1), src=wd_in)
    own_down = pltpu.make_async_copy(wd_in, wd.at[z], wd_r)
    own_down.start()
    units_to_ranks()
    spread_on(lat_in, lat_place, 0, True)
    plane_weights(wgu_in, wgu, 1, True)
    spread(dout_in, cot_place, 1, True)
    plane_weights_here(wqkv, 0)
    line_send(qkv_block, 0, (0, 1), (0, 1))
    for b in range(4):
        wait_for(own_l.at[b], tr_r.at[0, b])
    lat_f = own_l[...].reshape(128, 1024).astype(F32)
    r_one = lax.rsqrt(jnp.mean(lat_f * lat_f, axis=-1, keepdims=True) + EPS)
    n_one[k, :, c] = (lat_f * r_one).astype(BF).reshape(4, 32, 1024)
    ag_send(n_one, 0)
    line_relay(qkv_block, 0, 0)
    ag_corner(n_one, 0)
    ag_relay(n_one, 0, 1)
    ag_relay(n_one, 0, 2)
    line_relay(qkv_block, 0, 1)
    spread_on(dout_in, cot_place, 1, True)
    out_weights(True)
    line_send(down_block, 2, (1,), (), src=wd_in)
    ag_relay(n_one, 0, 3)
    plane_weights_here(wgu, 1)
    line_send(gu_block(0), 1, (0, 1), (0, 1))
    line_send(gu_block(1), 3, (0, 1), (0, 1))

    line_here(qkv_block, 0)

    @pl.loop(0, 4)
    def _(i):
        ag_other(n_one, 0, i)
        m = peer(i)
        block = n_one[m].reshape(256, 1024)
        out = dot_nn(block, wqkv[...].reshape(1024, 384))
        qkv[:, m] = out.astype(BF).reshape(8, 32, 384)

    line_relay(down_block, 2, 0)

    wait_for(lens, ln_r)
    lane = lax.broadcasted_iota(jnp.int32, (128, 128), 1)
    row = lax.broadcasted_iota(jnp.int32, (128, 128), 0)
    first = lane < 64

    def two_heads(v):
        zero = jnp.zeros_like(v)
        return jnp.concatenate(
            [jnp.where(first, v, zero), jnp.where(first, zero, v)], axis=0
        )

    def one_of_two(v):
        return jnp.where(first, v[:128], v[128:])

    def part_of(t0, t1, col):
        return qkv[t0:t1, :, :, col * 128 : (col + 1) * 128].reshape((t1 - t0) * 128, 128)

    for t in range(8):
        span = (t + 1) * 128
        q = two_heads(part_of(t, t + 1, 0).astype(F32) * 0.125).astype(BF)
        keys = part_of(0, t + 1, 1)
        vals = part_of(0, t + 1, 2)
        pos = row + t * 128
        begin = jnp.zeros((128, 128), jnp.int32)
        end = jnp.zeros((1, 128), jnp.int32)
        for g in range(4):
            length = lens[g : g + 1, :]
            end = end + length
            begin = begin + jnp.where(end <= pos, length, 0)
        allowed = []
        for u in range(t + 1):
            ok = begin <= lane + u * 128
            if u == t:
                ok = ok & (lane <= row)
            allowed.append(ok)
        allowed = jnp.concatenate(allowed, axis=1)
        scores = dot_right(q, keys)
        sums = []
        raws = []
        for h in range(2):
            sc = jnp.where(allowed, scores[h * 128 : (h + 1) * 128], -1e30)
            top = jnp.max(sc, axis=-1, keepdims=True)
            expo = jnp.exp(sc - top)
            low = expo.astype(BF)
            probs[t, h * 128 : (h + 1) * 128, 0:span] = low
            sums.append(jnp.sum(low.astype(F32), axis=-1, keepdims=True))
        raw = dot_nn(probs[t, :, 0:span], vals)
        both = jnp.where(first, sums[0], sums[1])
        attended = one_of_two(raw) / both
        tot[t] = both
        att_f[t] = attended
        att[:, t] = attended.astype(BF).reshape(4, 32, 128)

    for b in range(4):
        wait_for(cot.at[k, b, c], tr_r.at[1, b])
    ag_send(cot, 1)
    for slot in range(4):
        wait_for(wo.at[slot], wo_r.at[slot])

    def project_out(i):
        m = peer(i)
        out = dot_nn(att[m].reshape(256, 128), wo[...].reshape(128, 1024))
        part_a[m] = out.astype(BF).reshape(4, 2, 32, 1024)

    rs_start(part_a, 0, project_out)
    line_relay(down_block, 2, 1)
    ag_corner(cot, 1)
    ag_relay(cot, 1, 1)
    ag_relay(cot, 1, 2)
    rs_corner(part_a, 0)
    line_relay(gu_block(0), 1, 0)
    line_relay(gu_block(0), 1, 1)
    res = own_l[...].reshape(128, 1024).astype(F32) + rs_sum(part_a, 0)
    resid[...] = res
    r_two = lax.rsqrt(jnp.mean(res * res, axis=-1, keepdims=True) + EPS)
    n_two[k, :, c] = (res * r_two).astype(BF).reshape(4, 32, 1024)
    ag_send(n_two, 2)
    ag_relay(cot, 1, 3)
    line_relay(gu_block(1), 3, 0)

    ag_corner(n_two, 2)
    ag_relay(n_two, 2, 1)
    ag_relay(n_two, 2, 2)
    line_relay(gu_block(1), 3, 1)
    line_here(gu_block(0), 1)
    line_here(gu_block(1), 3)

    def feed_forward(i):
        ag_other(n_two, 2, i)
        m = peer(i)
        gu = dot_nn(n_two[m].reshape(256, 1024), wgu[...].reshape(1024, 768))
        gate = gu[:, :384]
        up = gu[:, 384:]
        sig = jax.nn.sigmoid(gate)
        active = gate * sig
        hid[m] = (active * up).astype(BF)
        slope[m, :, :384] = up * sig * (1.0 + gate * (1.0 - sig))
        slope[m, :, 384:] = active

    @pl.loop(0, 3)
    def _(i):
        feed_forward(i)

    ag_relay(n_two, 2, 3)
    line_here(down_block, 2)
    own_down.wait()
    for i in range(4):
        ag_other(cot, 1, i)
    feed_forward(3)

    @pl.loop(0, 4)
    def _(n):
        cols = pl.ds(pl.multiple_of(n * 256, 256), 256)
        right = cot[:, :, :, :, cols].reshape(1024, 256)
        out = dot_left(hid[...].reshape(1024, 384), right)
        dwd[:, :, cols] = out.astype(BF).reshape(4, 96, 256)

    line_grads(dwd_block, zd, xd, 2, True)

    def feed_back(i):
        m = peer(i)
        g_hid = dot_right(cot[m].reshape(256, 1024), wd[...].reshape(384, 1024))
        ggu[m, :, :384] = (g_hid * slope[m, :, :384]).astype(BF)
        ggu[m, :, 384:] = (g_hid * slope[m, :, 384:]).astype(BF)
        out = dot_right(ggu[m], wgu[...].reshape(1024, 768))
        part_b[m] = out.astype(BF).reshape(4, 2, 32, 1024)

    rs_start(part_b, 1, feed_back)

    def units_grad(d):
        cols = pl.ds(pl.multiple_of(d * 256, 256), 256)
        left = n_two[:, :, :, :, cols].reshape(1024, 256)
        out = dot_left(left, ggu[...].reshape(1024, 768))
        dwgu[d] = out.astype(BF).reshape(4, 2, 32, 768)

    @pl.loop(0, 2)
    def _(d):
        units_grad(d)

    rs_corner(part_b, 1)

    @pl.loop(2, 4)
    def _(d):
        units_grad(d)

    line_grads(dwgu_block, zgu, xgu, 1, True)
    line_grads_relay(dwd_block, zd, xd, 2, 0)
    line_grads_relay(dwd_block, zd, xd, 2, 1)

    @pl.loop(0, 4)
    def _(i):
        m = peer(i)
        out = dot_nn(hid[m], wd[...].reshape(384, 1024))
        part_c[m] = out.astype(BF).reshape(4, 2, 32, 1024)
        rs_copy(part_c, 2, i).start()

    scaled = rs_sum(part_b, 1)
    res = resid[...]
    r_two = lax.rsqrt(jnp.mean(res * res, axis=-1, keepdims=True) + EPS)
    normed = res * r_two
    inner = jnp.mean(scaled * normed, axis=-1, keepdims=True)
    g_res = cot[k, :, c].reshape(128, 1024).astype(F32) + r_two * (scaled - normed * inner)
    gres[...] = g_res
    gbr[k, :, c] = g_res.astype(BF).reshape(4, 32, 1024)
    ag_send(gbr, 3)

    ag_corner(gbr, 3)
    ag_relay(gbr, 3, 1)
    ag_relay(gbr, 3, 2)

    def attended_grad(i):
        ag_other(gbr, 3, i)
        m = peer(i)
        out = dot_right(gbr[m].reshape(256, 1024), wo[...].reshape(128, 1024))
        gatt[:, m] = out.astype(BF).reshape(8, 32, 128)

    @pl.loop(0, 3)
    def _(i):
        attended_grad(i)

    ag_relay(gbr, 3, 3)
    for i in (3, 1, 2):
        rs_halves(part_c, 2, i)
    line_grads_relay(dwgu_block, zgu, xgu, 1, 0)
    attended_grad(3)

    for t in range(8):
        span = (t + 1) * 128
        keys = part_of(0, t + 1, 1)
        vals = part_of(0, t + 1, 2)
        ratio = gatt[t].reshape(128, 128).astype(F32) / tot[t]
        g_raw = two_heads(ratio.astype(BF).astype(F32)).astype(BF)
        graw_two[t] = g_raw
        q_two[t] = two_heads(part_of(t, t + 1, 0).astype(F32)).astype(BF)
        prod = ratio * att_f[t]
        g_tot = -jnp.sum(two_heads(prod), axis=-1, keepdims=True)
        g_pr = dot_right(g_raw, vals)
        g_sc = probs[t, :, 0:span].astype(F32) * (g_pr + g_tot)
        gsc[t, :, 0:span] = g_sc.astype(BF)
        g_q = one_of_two(dot_nn(gsc[t, :, 0:span], keys)) * 0.125
        gqkv[:, t, :, 0:128] = g_q.astype(BF).reshape(4, 32, 128)
    line_grads_relay(dwgu_block, zgu, xgu, 1, 1)
    rs_corner(part_c, 2)
    for u in range(8):
        cols = slice(u * 128, (u + 1) * 128)
        rows = (8 - u) * 256
        g_k = dot_left(gsc[u:, :, cols].reshape(rows, 128), q_two[u:].reshape(rows, 128)) * 0.125
        g_v = dot_left(probs[u:, :, cols].reshape(rows, 128), graw_two[u:].reshape(rows, 128))
        gqkv[:, u, :, 128:256] = g_k.astype(BF).reshape(4, 32, 128)
        gqkv[:, u, :, 256:384] = g_v.astype(BF).reshape(4, 32, 128)

    rs_end(part_a, 0)

    def heads_back(i):
        m = peer(i)
        out = dot_right(gqkv[m].reshape(256, 384), wqkv[...].reshape(1024, 384))
        part_a[m] = out.astype(BF).reshape(4, 2, 32, 1024)

    rs_start(part_a, 3, heads_back)

    @pl.loop(0, 4)
    def _(d):
        cols = pl.ds(pl.multiple_of(d * 256, 256), 256)
        left = n_one[:, :, :, :, cols].reshape(1024, 256)
        out = dot_left(left, gqkv[...].reshape(1024, 384))
        dwqkv[d] = out.astype(BF).reshape(4, 2, 32, 384)

    line_grads(dwqkv_block, zq, xq, 0, True)
    rs_corner(part_a, 3)

    def gather_back(which, dst, start):
        for b in range(4):
            here = (z == k) & (z == b)
            src = back.at[which, b]
            place = dst.at[pl.ds(pl.multiple_of(32 * k, 32), 32)]

            @pl.when(here)
            def _():
                if start:
                    pltpu.make_async_copy(src, place, tb_r.at[which, k]).start()

            @pl.when(jnp.logical_not(here))
            def _():
                copy = remote(src, place, tb_s.at[which, b], tb_r.at[which, k], dev(z, b, c))
                if start:
                    copy.start()
                else:
                    copy.wait_send()

    out_f = resid[...] + rs_sum(part_c, 2)
    back[0] = out_f.astype(BF).reshape(4, 32, 1024)
    gather_back(0, lat_o, True)

    def plane_grads(land, dst, which, start):
        for i in range(4):
            m = peer(i)
            for same in (True, False):
                cc = c if same else oc
                src = land.at[z, m, cc]
                place = dst.at[rank]
                if i == 0 and same:
                    if start:
                        pltpu.make_async_copy(src, place, ga_r.at[which, rank]).start()
                else:
                    copy = remote(
                        src,
                        place,
                        ga_s.at[which, 2 * i + (0 if same else 1)],
                        ga_r.at[which, rank],
                        dev(m, z, cc),
                    )
                    if start:
                        copy.start()
                    else:
                        copy.wait_send()

    zgu[z] = line_sum(dwgu_block, zgu, 1).astype(BF)
    plane_grads(zgu, ggu_o, 1, True)
    line_grads_relay(dwqkv_block, zq, xq, 0, 0)
    line_grads_relay(dwqkv_block, zq, xq, 0, 1)
    scaled = rs_sum(part_a, 3)
    lat_f = own_l[...].reshape(128, 1024).astype(F32)
    r_one = lax.rsqrt(jnp.mean(lat_f * lat_f, axis=-1, keepdims=True) + EPS)
    normed = lat_f * r_one
    inner = jnp.mean(scaled * normed, axis=-1, keepdims=True)
    d_lat = gres[...] + r_one * (scaled - normed * inner)
    back[1] = d_lat.astype(BF).reshape(4, 32, 1024)
    gather_back(1, dlat_o, True)

    @pl.loop(0, 4)
    def _(n):
        cols = pl.ds(pl.multiple_of(n * 256, 256), 256)
        right = gbr[:, :, :, :, cols].reshape(1024, 256)
        out = dot_left(att[...].reshape(1024, 128), right)
        dwo[:, :, cols] = out.astype(BF).reshape(4, 32, 256)

    def out_grads(start):
        for p in range(2):
            for cs in range(2):
                zz = 2 * c + p
                here = (zz == z) & (c == cs)
                src = dwo.at[2 * p + cs]

                @pl.when(here)
                def _():
                    if start:
                        pltpu.make_async_copy(src, go_o.at[z], go_r.at[z]).start()

                @pl.when(jnp.logical_not(here))
                def _():
                    copy = remote(
                        src, go_o.at[z], go_s.at[2 * p + cs], go_r.at[z], dev(k, zz, cs)
                    )
                    if start:
                        copy.start()
                    else:
                        copy.wait_send()

    out_grads(True)
    down_sum[...] = line_sum(dwd_block, zd, 2)
    down_out = pltpu.make_async_copy(down_sum.at[pl.ds(0, 88)], gd_o, gd_r)
    down_out.start()
    zq[z] = line_sum(dwqkv_block, zq, 0).astype(BF)
    plane_grads(zq, gqkv_o, 0, True)

    for which, dst in ((0, lat_o), (1, dlat_o)):
        for b in range(4):
            wait_for(dst.at[pl.ds(32 * b, 32)], tb_r.at[which, b])
    for b in range(4):
        wait_for(go_o.at[b], go_r.at[b])
    for which, dst in ((1, ggu_o), (0, gqkv_o)):
        for r in range(RANKS):
            wait_for(dst.at[r], ga_r.at[which, r])
    spread(lat_in, lat_place, 0, False)
    spread_on(lat_in, lat_place, 0, False)
    spread(dout_in, cot_place, 1, False)
    spread_on(dout_in, cot_place, 1, False)
    spread_lens(False)
    plane_weights(wqkv_in, wqkv, 0, False)
    plane_weights(wgu_in, wgu, 1, False)
    line_sent(qkv_block, 0)
    line_sent(gu_block(0), 1)
    line_sent(gu_block(1), 3)
    line_sent(down_block, 2, wd_in)
    down_out.wait()
    out_weights(False)
    for which, buf in enumerate((n_one, cot, n_two, gbr)):
        ag_end(buf, which)
    rs_end(part_b, 1)
    rs_end(part_c, 2)
    rs_end(part_a, 3)
    line_grads(dwgu_block, zgu, xgu, 1, False)
    line_grads(dwqkv_block, zq, xq, 0, False)
    line_grads(dwd_block, zd, xd, 2, False)
    plane_grads(zgu, ggu_o, 1, False)
    plane_grads(zq, gqkv_o, 0, False)
    out_grads(False)
    gather_back(0, lat_o, False)
    gather_back(1, dlat_o, False)


def run_layer(lat, dout, lengths, gain_one, gain_two, weights):
    vm = pltpu.VMEM
    dma = pltpu.SemaphoreType.DMA
    rows = (4, 4, 2, 32)
    return pl.pallas_call(
        layer_kernel,
        out_shape=(
            jax.ShapeDtypeStruct((128, 1024), BF),
            jax.ShapeDtypeStruct((128, 1024), BF),
            jax.ShapeDtypeStruct((RANKS, 32, 384), BF),
            jax.ShapeDtypeStruct((RANKS, 32, 768), BF),
            jax.ShapeDtypeStruct((88, 1024), F32),
            jax.ShapeDtypeStruct((4, 32, 1024), BF),
        ),
        in_specs=[pl.BlockSpec(memory_space=pl.ANY)] * 2
        + [pl.BlockSpec(memory_space=pltpu.SMEM)]
        + [pl.BlockSpec(memory_space=pltpu.VMEM)] * 9,
        out_specs=[pl.BlockSpec(memory_space=pl.ANY)] * 6,
        scratch_shapes=[
            vm((8, 128), jnp.int32),
            vm((RANKS, 32, 384), BF),
            vm((RANKS, 32, 768), BF),
            vm((96, 1024), BF),
            vm((4, 32, 1024), BF),
            vm((2, 4, 32, 1024), BF),
            vm((8, 128), jnp.int32),
            vm(rows + (1024,), BF),
            vm(rows + (1024,), BF),
            vm(rows + (1024,), BF),
            vm(rows + (1024,), BF),
            vm(rows + (384,), BF),
            vm(rows + (768,), BF),
            vm((4, 96, 1024), BF),
            vm((4, 32, 1024), BF),
            vm((8, 4, 32, 384), BF),
            vm((4, 8, 32, 128), BF),
            vm((8, 128, 128), F32),
            vm((8, 128, 128), F32),
            vm((8, 256, 1024), BF),
            vm((8, 256, 1024), BF),
            vm(rows + (1024,), BF),
            vm(rows + (1024,), BF),
            vm(rows + (1024,), BF),
            vm((4, 4, 4, 32, 1024), BF),
            vm((4, 2, 4, 32, 1024), BF),
            vm((4, 2, 2, 32, 1024), BF),
            vm((4, 256, 384), BF),
            vm((4, 256, 768), BF),
            vm((4, 256, 768), F32),
            vm((8, 4, 32, 128), BF),
            vm((8, 256, 128), BF),
            vm((8, 256, 128), BF),
            vm((4, 8, 32, 384), BF),
            vm(rows + (384,), BF),
            vm(rows + (768,), BF),
            vm((4, 96, 1024), BF),
            vm((4, 32, 1024), BF),
            vm((4, 4, 2, 32, 384), BF),
            vm((4, 4, 2, 32, 768), BF),
            vm((4, 96, 1024), BF),
            vm((2, 4, 2, 32, 384), BF),
            vm((2, 4, 2, 32, 768), BF),
            vm((2, 96, 1024), BF),
            vm((96, 1024), F32),
            vm((128, 1024), F32),
            vm((128, 1024), F32),
            vm((2, 4, 32, 1024), BF),
            dma((2, 4)),
            dma((2, 4)),
            dma((2, 4)),
            dma((2, 4)),
            dma,
            dma,
            dma((2, 8)),
            dma((2, 8)),
            dma((4, 4)),
            dma((4, 4)),
            dma,
            dma((4,)),
            dma((4,)),
            dma((4, 12)),
            dma((4, 4, 2)),
            dma((4, 4)),
            dma((4, 2)),
            dma((4, 12)),
            dma((4, 4)),
            dma((4, 2, 2)),
            dma((4, 2)),
            dma((3, 4)),
            dma((3, 4)),
            dma((3, 2)),
            dma((2, 8)),
            dma((2, 8)),
            dma,
            dma((4,)),
            dma((4,)),
            dma((2, 4)),
            dma((2, 4)),
        ],
        compiler_params=pltpu.CompilerParams(
            collective_id=0, has_side_effects=True, vmem_limit_bytes=60 * 1024 * 1024
        ),
    )(lat, dout, lengths, gain_one, gain_two, *weights)


def finish_kernel(
    lat,
    dlat,
    gqkv_in,
    ggu_in,
    gd,
    go_in,
    gain_one,
    gain_two,
    wq,
    wk,
    wv,
    wg,
    wu,
    lat_o,
    dlat_o,
    g_one_o,
    gq_o,
    gk_o,
    gv_o,
    go_o,
    g_two_o,
    gg_o,
    gu_o,
    gd_o,
    gqkv,
    ggu,
    go,
    sems,
):
    moves = ((gqkv_in, gqkv), (ggu_in, ggu), (go_in, go))
    moves += ((lat, lat_o.at[0]), (dlat, dlat_o.at[0]), (gd, gd_o))
    copies = [pltpu.make_async_copy(src, dst, sems.at[i]) for i, (src, dst) in enumerate(moves)]
    for copy in copies:
        copy.start()
    col_one = jnp.sum(on_diagonal(gain_one[...]), axis=1, keepdims=True)
    col_two = jnp.sum(on_diagonal(gain_two[...]), axis=1, keepdims=True)

    def as_row(acc):
        return jnp.sum(on_diagonal(jnp.sum(acc, axis=1, keepdims=True)), axis=0, keepdims=True)

    copies[0].wait()
    acc = jnp.zeros((32, 128), F32)
    for i, (w, out) in enumerate(((wq, gq_o), (wk, gk_o), (wv, gv_o))):
        for r in range(RANKS):
            cols = slice(r * 128, (r + 1) * 128)
            part = gqkv[r, :, i * 128 : (i + 1) * 128].astype(F32)
            out[:, cols] = part * col_one
            acc = acc + part * w[:, cols].astype(F32)
    g_one_o[...] = as_row(acc)
    copies[1].wait()
    acc = jnp.zeros((32, 256), F32)
    for i, (w, out) in enumerate(((wg, gg_o), (wu, gu_o))):
        parts = [None] * 32
        for r in range(RANKS):
            whole = ggu[r, :, i * 384 : (i + 1) * 384].astype(F32)
            for b in range(ZS):
                parts[8 * (r // CORES) + CORES * b + r % CORES] = whole[:, b * 96 : b * 96 + 88]
        rows = jnp.concatenate(parts, axis=1)
        out[...] = rows * col_two
        prod = rows * w[...].astype(F32)
        for n in range(11):
            acc = acc + prod[:, n * 256 : (n + 1) * 256]
    g_two_o[...] = as_row(acc)
    copies[2].wait()
    go_o[...] = (go[0].astype(F32) + go[1].astype(F32)) + (go[2].astype(F32) + go[3].astype(F32))
    for copy in copies[3:]:
        copy.wait()


def finish(*arrays):
    outs = (
        ((1, 128, 1024), BF),
        ((1, 128, 1024), BF),
        ((1, 32), F32),
        ((32, 1024), F32),
        ((32, 1024), F32),
        ((32, 1024), F32),
        ((32, 1024), F32),
        ((1, 32), F32),
        ((32, 2816), F32),
        ((32, 2816), F32),
        ((88, 1024), F32),
    )
    hbm = pl.BlockSpec(memory_space=pltpu.HBM)
    vmem = pl.BlockSpec(memory_space=pltpu.VMEM)
    return pl.pallas_call(
        finish_kernel,
        out_shape=tuple(jax.ShapeDtypeStruct(*o) for o in outs),
        in_specs=[hbm] * 6 + [vmem] * 7,
        out_specs=[vmem] * len(outs),
        scratch_shapes=[
            pltpu.VMEM((RANKS, 32, 384), BF),
            pltpu.VMEM((RANKS, 32, 768), BF),
            pltpu.VMEM((4, 32, 1024), BF),
            pltpu.SemaphoreType.DMA((6,)),
        ],
        compiler_params=pltpu.CompilerParams(vmem_limit_bytes=60 * 1024 * 1024),
    )(*arrays)


def plane_device(
    latents,
    d_out,
    lengths,
    gain_attn,
    w_query,
    w_key,
    w_value,
    w_out,
    gain_ffn,
    w_gate,
    w_up,
    w_down,
):
    gains = gain_attn.reshape(1, 32), gain_ffn.reshape(1, 32)
    weights = w_query, w_key, w_value, w_gate, w_up, w_down, w_out
    parts = run_layer(latents[0], d_out[0], lengths, *gains, weights)
    outs = finish(*parts, *gains, w_query, w_key, w_value, w_gate, w_up)
    return tuple(o.reshape(32) if o.shape == (1, 32) else o for o in outs)


def solution(mesh):
    return jax.shard_map(
        plane_device if planes_fit(mesh) else per_device,
        mesh=mesh,
        in_specs=(
            P("dp", "seq", None),
            P("dp", "seq", None),
            P("dp", None),
            P(("dp", "seq")),
            P(("dp", "seq"), None),
            P(("dp", "seq"), None),
            P(("dp", "seq"), None),
            P(("dp", "seq"), None),
            P(("dp", "seq")),
            P(("dp", "seq"), None),
            P(("dp", "seq"), None),
            P(("dp", "seq"), None),
        ),
        out_specs=(
            P("dp", "seq", None),
            P("dp", "seq", None),
            P(("dp", "seq")),
            P(("dp", "seq"), None),
            P(("dp", "seq"), None),
            P(("dp", "seq"), None),
            P(("dp", "seq"), None),
            P(("dp", "seq")),
            P(("dp", "seq"), None),
            P(("dp", "seq"), None),
            P(("dp", "seq"), None),
        ),
        check_vma=False,
    )
```

```python
import functools
import math

import jax
import jax.numpy as jnp
from jax import lax
from jax.experimental import pallas as pl
from jax.experimental.pallas import tpu as pltpu
from jax.sharding import PartitionSpec as P

HEADS = 16


EPS = 1e-05


def norm_rows(values, gain_vec):
    factor = lax.rsqrt(jnp.mean(values * values, axis=-1, keepdims=True) + EPS)
    normed = values * factor
    return (normed * gain_vec, normed, factor)


def norm_back(grad_out, normed, factor, gain_vec):
    scaled = grad_out * gain_vec
    inner = jnp.mean(scaled * normed, axis=-1, keepdims=True)
    return (factor * (scaled - normed * inner), jnp.sum(grad_out * normed, axis=0))


def dot_left(left, right):
    return lax.dot_general(
        left, right, (((0,), (0,)), ((), ())), preferred_element_type=jnp.float32
    )


def dot_right(left, right):
    return lax.dot_general(
        left, right, (((1,), (1,)), ((), ())), preferred_element_type=jnp.float32
    )


def per_device(
    latents,
    d_out,
    lengths,
    gain_attn,
    w_query,
    w_key,
    w_value,
    w_out,
    gain_ffn,
    w_gate,
    w_up,
    w_down,
):
    g_attn, full_query, full_key, full_value, full_out, g_ffn, full_gate, full_up, full_down = (
        lax.all_gather(gain_attn, ("dp", "seq"), axis=0, tiled=True),
        lax.all_gather(w_query, ("dp", "seq"), axis=0, tiled=True),
        lax.all_gather(w_key, ("dp", "seq"), axis=0, tiled=True),
        lax.all_gather(w_value, ("dp", "seq"), axis=0, tiled=True),
        lax.all_gather(w_out, ("dp", "seq"), axis=0, tiled=True),
        lax.all_gather(gain_ffn, ("dp", "seq"), axis=0, tiled=True),
        lax.all_gather(w_gate, ("dp", "seq"), axis=0, tiled=True),
        lax.all_gather(w_up, ("dp", "seq"), axis=0, tiled=True),
        lax.all_gather(w_down, ("dp", "seq"), axis=0, tiled=True),
    )
    gain_one = g_attn.astype(jnp.float32)
    gain_two = g_ffn.astype(jnp.float32)
    inputs_f = latents[0].astype(jnp.float32)
    row_count, model_width = inputs_f.shape
    head_size = model_width // HEADS
    group_rows = row_count * lax.axis_size("seq")
    here = lax.axis_index("seq") * row_count + jnp.arange(row_count, dtype=jnp.int32)
    seq_lens = lengths[0]
    seq_ends = jnp.cumsum(seq_lens, dtype=jnp.int32)
    begins = jnp.sum(
        jnp.where(seq_ends[None, :] <= here[:, None], seq_lens[None, :], 0), axis=1, dtype=jnp.int32
    )
    key_block = math.gcd(group_rows, 1024)
    block_count = group_rows // key_block
    key_positions = jnp.arange(group_rows, dtype=jnp.int32).reshape(block_count, key_block)
    h_one_f, normed_one, factor_one = norm_rows(inputs_f, gain_one)
    h_one = h_one_f.astype(jnp.bfloat16)
    query_proj = jnp.dot(h_one, full_query, preferred_element_type=jnp.float32).astype(jnp.bfloat16)
    key_proj = jnp.dot(h_one, full_key, preferred_element_type=jnp.float32).astype(jnp.bfloat16)
    value_proj = jnp.dot(h_one, full_value, preferred_element_type=jnp.float32).astype(jnp.bfloat16)
    keys_all, values_all = (
        lax.all_gather(key_proj, "seq", axis=0, tiled=True),
        lax.all_gather(value_proj, "seq", axis=0, tiled=True),
    )
    query_heads = query_proj.reshape(row_count, HEADS, head_size)

    def split_blocks(array):
        return array.reshape(block_count, key_block, HEADS, head_size)

    def block_scores(key_piece, pos_piece):
        scores = (
            jnp.einsum("qhd,khd->hqk", query_heads, key_piece, preferred_element_type=jnp.float32)
            * 0.125
        )
        allowed = (pos_piece[None, :] <= here[:, None]) & (pos_piece[None, :] >= begins[:, None])
        return (scores, allowed[None])

    def max_step(running, pieces):
        key_piece, pos_piece = pieces
        scores, allowed = block_scores(key_piece, pos_piece)
        return (jnp.maximum(running, jnp.max(jnp.where(allowed, scores, -1e30), axis=-1)), None)

    row_max, _ = lax.scan(
        max_step,
        jnp.full((HEADS, row_count), -1e30, jnp.float32),
        (split_blocks(keys_all), key_positions),
    )

    def sum_step(running, pieces):
        key_piece, value_piece, pos_piece = pieces
        scores, allowed = block_scores(key_piece, pos_piece)
        expon = jnp.where(
            allowed, jnp.exp(jnp.where(allowed, scores, -1e30) - row_max[:, :, None]), 0.0
        )
        rounded = expon.astype(jnp.bfloat16)
        total_sum, raw_sum = running
        total_sum = total_sum + jnp.sum(rounded.astype(jnp.float32), axis=-1)
        raw_sum = raw_sum + jnp.einsum(
            "hqk,khd->qhd", rounded, value_piece, preferred_element_type=jnp.float32
        )
        return ((total_sum, raw_sum), None)

    (total_sum, raw_sum), _ = lax.scan(
        sum_step,
        (
            jnp.zeros((HEADS, row_count), jnp.float32),
            jnp.zeros((row_count, HEADS, head_size), jnp.float32),
        ),
        (split_blocks(keys_all), split_blocks(values_all), key_positions),
    )
    totals_rows = jnp.transpose(total_sum)
    attended = raw_sum / totals_rows[:, :, None]
    attended_low = attended.reshape(row_count, model_width).astype(jnp.bfloat16)
    resid = inputs_f + jnp.dot(attended_low, full_out, preferred_element_type=jnp.float32)
    h_two_f, normed_two, factor_two = norm_rows(resid, gain_two)
    h_two = h_two_f.astype(jnp.bfloat16)
    gate_proj = jnp.dot(h_two, full_gate, preferred_element_type=jnp.float32)
    up_proj = jnp.dot(h_two, full_up, preferred_element_type=jnp.float32)
    gate_sigmoid = jax.nn.sigmoid(gate_proj)
    gate_active = gate_proj * gate_sigmoid
    hidden = (gate_active * up_proj).astype(jnp.bfloat16)
    outputs = resid + jnp.dot(hidden, full_down, preferred_element_type=jnp.float32)
    latents_out = outputs.astype(jnp.bfloat16)[None]
    grad_out = d_out[0]
    grad_down = dot_left(hidden, grad_out)
    g_hidden = dot_right(grad_out, full_down)
    g_gate = (g_hidden * up_proj * gate_sigmoid * (1.0 + gate_proj * (1.0 - gate_sigmoid))).astype(
        jnp.bfloat16
    )
    g_up = (g_hidden * gate_active).astype(jnp.bfloat16)
    grad_gate = dot_left(h_two, g_gate)
    grad_up = dot_left(h_two, g_up)
    g_h_two = dot_right(g_gate, full_gate) + dot_right(g_up, full_up)
    g_norm_two, grad_gain_two = norm_back(g_h_two, normed_two, factor_two, gain_two)
    g_resid = grad_out.astype(jnp.float32) + g_norm_two
    g_branch = g_resid.astype(jnp.bfloat16)
    grad_out_proj = dot_left(attended_low, g_branch)
    g_att = dot_right(g_branch, full_out).reshape(row_count, HEADS, head_size).astype(jnp.bfloat16)
    g_att_f = g_att.astype(jnp.float32)
    g_raw = (g_att_f / totals_rows[:, :, None]).astype(jnp.bfloat16)
    g_total = jnp.transpose(-jnp.sum(g_att_f * raw_sum, axis=-1) / (totals_rows * totals_rows))
    keys_back, values_back = (
        lax.all_gather(key_proj, "seq", axis=0, tiled=True),
        lax.all_gather(value_proj, "seq", axis=0, tiled=True),
    )

    def score_grads(key_piece, value_piece, pos_piece):
        scores, allowed = block_scores(key_piece, pos_piece)
        expon = jnp.where(
            allowed, jnp.exp(jnp.where(allowed, scores, -1e30) - row_max[:, :, None]), 0.0
        )
        g_probs = jnp.einsum("qhd,khd->hqk", g_raw, value_piece, preferred_element_type=jnp.float32)
        g_scores = (expon * (g_probs + g_total[:, :, None])).astype(jnp.bfloat16)
        return (expon, g_scores)

    def grad_step(running, pieces):
        key_piece, value_piece, pos_piece = pieces
        expon, g_scores = score_grads(key_piece, value_piece, pos_piece)
        rounded = expon.astype(jnp.bfloat16)
        running = (
            running
            + jnp.einsum("hqk,khd->qhd", g_scores, key_piece, preferred_element_type=jnp.float32)
            * 0.125
        )
        g_key_piece = (
            jnp.einsum("hqk,qhd->khd", g_scores, query_heads, preferred_element_type=jnp.float32)
            * 0.125
        )
        g_value_piece = jnp.einsum(
            "hqk,qhd->khd", rounded, g_raw, preferred_element_type=jnp.float32
        )
        return (running, (g_key_piece, g_value_piece))

    g_query_f, (g_keys, g_values) = lax.scan(
        grad_step,
        jnp.zeros((row_count, HEADS, head_size), jnp.float32),
        (split_blocks(keys_back), split_blocks(values_back), key_positions),
    )
    mine_key, mine_value = (
        lax.psum_scatter(
            g_keys.reshape(group_rows, model_width).astype(jnp.bfloat16),
            "seq",
            scatter_dimension=0,
            tiled=True,
        ).astype(jnp.float32),
        lax.psum_scatter(
            g_values.reshape(group_rows, model_width).astype(jnp.bfloat16),
            "seq",
            scatter_dimension=0,
            tiled=True,
        ).astype(jnp.float32),
    )
    g_key = mine_key.astype(jnp.bfloat16)
    g_value = mine_value.astype(jnp.bfloat16)
    g_query = g_query_f.reshape(row_count, model_width).astype(jnp.bfloat16)
    grad_query = dot_left(h_one, g_query)
    grad_key = dot_left(h_one, g_key)
    grad_value = dot_left(h_one, g_value)
    g_h_one = (
        dot_right(g_query, full_query) + dot_right(g_key, full_key) + dot_right(g_value, full_value)
    )
    g_norm_one, grad_gain_one = norm_back(g_h_one, normed_one, factor_one, gain_one)
    d_latents = (g_resid + g_norm_one).astype(jnp.bfloat16)[None]
    gain_pair = jnp.stack((grad_gain_one, grad_gain_two), axis=1)
    summed = (
        lax.psum_scatter(gain_pair, ("dp", "seq"), scatter_dimension=0, tiled=True),
        lax.psum_scatter(grad_query, ("dp", "seq"), scatter_dimension=0, tiled=True),
        lax.psum_scatter(grad_key, ("dp", "seq"), scatter_dimension=0, tiled=True),
        lax.psum_scatter(grad_value, ("dp", "seq"), scatter_dimension=0, tiled=True),
        lax.psum_scatter(grad_out_proj, ("dp", "seq"), scatter_dimension=0, tiled=True),
        lax.psum_scatter(grad_gate, ("dp", "seq"), scatter_dimension=0, tiled=True),
        lax.psum_scatter(grad_up, ("dp", "seq"), scatter_dimension=0, tiled=True),
        lax.psum_scatter(grad_down, ("dp", "seq"), scatter_dimension=0, tiled=True),
    )
    return (
        latents_out,
        d_latents,
        summed[0][:, 0],
        summed[1],
        summed[2],
        summed[3],
        summed[4],
        summed[0][:, 1],
        summed[5],
        summed[6],
        summed[7],
    )


MESH = pl.DeviceIdType.MESH
BF = jnp.bfloat16
F32 = jnp.float32
DP, ZS, CORES = 4, 4, 2
RANKS = DP * CORES
GU = (1, 3, 4)


def units_of(rank):
    return [8 * (rank // CORES) + CORES * b + rank % CORES for b in range(ZS)]


def planes_fit(mesh):
    return mesh.shape["dp"] == DP and mesh.shape["seq"] == ZS * CORES


def dot_nn(left, right):
    return jnp.dot(left, right, preferred_element_type=F32)


def remote(src, dst, send_sem, recv_sem, device):
    return pltpu.make_async_remote_copy(
        src_ref=src,
        dst_ref=dst,
        send_sem=send_sem,
        recv_sem=recv_sem,
        device_id=device,
        device_id_type=MESH,
    )


def wait_for(ref, sem):
    pltpu.make_async_copy(ref, ref, sem).wait()


def on_diagonal(row):
    at = lax.broadcasted_iota(jnp.int32, (32, 32), 0) == lax.broadcasted_iota(jnp.int32, (32, 32), 1)
    return jnp.where(at, row.astype(F32), 0.0)


def layer_kernel(
    lat_in,
    dout_in,
    lengths_in,
    gain_one,
    gain_two,
    wq_raw,
    wk_raw,
    wv_raw,
    wg_raw,
    wu_raw,
    wd_raw,
    wo_in,
    lat_o,
    dlat_o,
    gqkv_o,
    ggu_o,
    gd_o,
    go_o,
    lens_in,
    wqkv_in,
    wgu_in,
    wd_in,
    own_l,
    stop,
    lens,
    n_one,
    n_two,
    cot,
    gbr,
    wqkv,
    wgu,
    wd,
    wo,
    qkv,
    att,
    att_f,
    tot,
    probs,
    gsc,
    part_a,
    part_b,
    part_c,
    sib,
    rcv,
    turn,
    hid,
    ggu,
    slope,
    gatt,
    graw_two,
    q_two,
    gqkv,
    dwqkv,
    dwgu,
    dwd,
    dwo,
    zq,
    zgu,
    zd,
    xq,
    xgu,
    xd,
    down_sum,
    resid,
    gres,
    back,
    tr_s,
    tr_r,
    tx_r,
    tz_s,
    ln_s,
    ln_r,
    wa_s,
    wa_r,
    wz_s,
    wz_r,
    wd_r,
    wo_s,
    wo_r,
    ag_s,
    ag_r,
    ag_x,
    ag_d,
    rs_s,
    rs_r,
    rs_x,
    rs_d,
    gz_s,
    gz_r,
    gx_r,
    ga_s,
    ga_r,
    gd_r,
    go_s,
    go_r,
    tb_s,
    tb_r,
):
    k = lax.axis_index("dp")
    s = lax.axis_index("seq")
    z = s // CORES
    c = s % CORES
    oc = 1 - c
    rank = CORES * k + c

    def dev(kk, zz, cc):
        return (kk, CORES * zz + cc)

    def peer(i):
        return 2 * ((k // 2 + i // 2) % 2) + (k % 2 + i % 2) % 2

    def zpeer(i):
        return (z + i) % ZS

    sibling = dev(k, z, oc)

    barrier = pltpu.get_barrier_semaphore()
    greeted = 0
    for di in range(4):
        for dz in range(4):
            if di or dz:
                pl.semaphore_signal(
                    barrier, inc=1, device_id=dev(peer(di), zpeer(dz), c), device_id_type=MESH
                )
                greeted += 1
            if di == 0 or dz == 0:
                pl.semaphore_signal(
                    barrier, inc=1, device_id=dev(peer(di), zpeer(dz), oc), device_id_type=MESH
                )
                greeted += 1

    def scaled_rows(w, gain):
        return dot_nn(on_diagonal(gain[...]).astype(BF), w[...])

    for i, w in enumerate((wq_raw, wk_raw, wv_raw)):
        rows = scaled_rows(w, gain_one).astype(BF)
        for r in range(RANKS):
            wqkv_in[r, :, i * 128 : (i + 1) * 128] = rows[:, r * 128 : (r + 1) * 128]
    wd_in[0] = wd_raw[0:32]
    wd_in[1] = wd_raw[32:64]
    wd_in[2, 0:16] = wd_raw[64:80]
    wd_in[2, 16:32] = jnp.concatenate([wd_raw[80:88], jnp.zeros((8, 1024), BF)], axis=0)
    tile_row = lax.broadcasted_iota(jnp.int32, (8, 128), 0)
    tile = jnp.zeros((8, 128), jnp.int32)
    for i in range(4):
        tile = jnp.where(tile_row == i, lengths_in[0, i], tile)
    lens_in[...] = tile

    def units_to_ranks():
        both = [scaled_rows(w, gain_two) for w in (wg_raw, wu_raw)]
        gap = jnp.zeros((32, 8), F32)
        for r in range(RANKS):
            for j in range(3):
                for i, rows in enumerate(both):
                    parts = []
                    for unit in units_of(r):
                        at = 88 * unit + 32 * j
                        parts += [rows[:, at : at + 32]] if j < 2 else [rows[:, at : at + 24], gap]
                    lo = 256 * j + 128 * i
                    wgu_in[r, :, lo : lo + 128] = jnp.concatenate(parts, axis=1).astype(BF)

    pl.semaphore_wait(barrier, greeted)

    def spread(src, final_of, which, start):
        for q in range(4):
            piece = src.at[pl.ds(32 * q, 32)]

            @pl.when((z == k) & (k == q))
            def _():
                if start:
                    pltpu.make_async_copy(piece, final_of(q, z), tr_r.at[which, z]).start()

            @pl.when((z == k) & (k != q))
            def _():
                copy = remote(
                    piece, final_of(q, z), tr_s.at[which, q], tr_r.at[which, z], dev(q, z, c)
                )
                if start:
                    copy.start()
                else:
                    copy.wait_send()

            @pl.when((z != k) & (k != q))
            def _():
                copy = remote(
                    piece, stop.at[which, k], tr_s.at[which, q], tx_r.at[which, k], dev(q, z, c)
                )
                if start:
                    copy.start()
                else:
                    copy.wait_send()

    def spread_on(src, final_of, which, start):
        for i in range(1, 4):
            g = zpeer(i)

            def send(piece):
                copy = remote(
                    piece, final_of(k, z), tz_s.at[which, i], tr_r.at[which, z], dev(k, g, c)
                )
                if start:
                    copy.start()
                else:
                    copy.wait_send()

            @pl.when(g == k)
            def _():
                send(src.at[pl.ds(pl.multiple_of(32 * k, 32), 32)])

            @pl.when(g != k)
            def _():
                if start:
                    wait_for(stop.at[which, g], tx_r.at[which, g])
                send(stop.at[which, g])

    def lat_place(q, b):
        return own_l.at[b]

    def cot_place(q, b):
        return cot.at[q, b, c]

    def spread_lens(start):
        here = z == k

        @pl.when(here)
        def _():
            if start:
                pltpu.make_async_copy(lens_in, lens, ln_r).start()

        @pl.when(jnp.logical_not(here))
        def _():
            copy = remote(lens_in, lens, ln_s, ln_r, dev(z, k, c))
            if start:
                copy.start()
            else:
                copy.wait_send()

    def plane_weights(src, dst, which, start):
        for i in range(4):
            for same in (True, False):
                cc = c if same else oc
                target = CORES * peer(i) + cc
                piece = src.at[target]
                place = dst.at[k, z, c]
                if i == 0 and same:
                    if start:
                        pltpu.make_async_copy(piece, place, wa_r.at[which, rank]).start()
                else:
                    copy = remote(
                        piece,
                        place,
                        wa_s.at[which, 2 * i + (0 if same else 1)],
                        wa_r.at[which, rank],
                        dev(peer(i), z, cc),
                    )
                    if start:
                        copy.start()
                    else:
                        copy.wait_send()

    def plane_weights_here(dst, which):
        for kk in range(4):
            for cc in range(2):
                wait_for(dst.at[kk, z, cc], wa_r.at[which, CORES * kk + cc])

    middle = (z == 1) | (z == 2)
    near = (1 + z % 2, 2 + z // 2 - 2 * (z % 2))
    z_end = 3 * (z // 2)

    def far_of(place):
        return (6 - 3 * place, 3 - place)

    far = far_of(z)

    def line_copy(block, which, slot, b, place, src=None):
        src = block(b) if src is None else src
        return remote(src, block(b), wz_s.at[which, slot], wz_r.at[which, b], dev(k, place, c))

    def line_send(block, which, from_ends, from_middle, start=True, src=None):
        def send(slots):
            for j in slots:
                copy = line_copy(block, which, j, z, near[j], src)
                if start:
                    copy.start()
                else:
                    copy.wait_send()

        if from_ends:

            @pl.when(jnp.logical_not(middle))
            def _():
                send(from_ends)

        if from_middle:

            @pl.when(middle)
            def _():
                send(from_middle)

    def line_relay(block, which, j):
        @pl.when(middle)
        def _():
            wait_for(block(far[j]), wz_r.at[which, far[j]])
            line_copy(block, which, 2 + j, far[j], z_end).start()

    def line_sent(block, which, src=None):
        line_send(block, which, (0, 1), (0, 1), False, src)

        @pl.when(middle)
        def _():
            for j in range(2):
                line_copy(block, which, 2 + j, far[j], z_end).wait_send()

    def line_here(block, which):
        @pl.when(middle)
        def _():
            wait_for(block(z_end), wz_r.at[which, z_end])

        @pl.when(jnp.logical_not(middle))
        def _():
            for i in range(1, 4):
                wait_for(block(zpeer(i)), wz_r.at[which, zpeer(i)])

    def qkv_block(b):
        return wqkv.at[:, b]

    def gu_block(j):
        return lambda b: wgu.at[:, b, :, :, 256 * j : 256 * j + 256]

    def down_block(b):
        return wd.at[:, b]

    def out_weights(start):
        to_core = z // 2
        slot = 2 * (z % 2) + c
        for i in range(4):

            def send():
                copy = remote(
                    wo_in, wo.at[slot], wo_s.at[i], wo_r.at[slot], dev(k, zpeer(i), to_core)
                )
                if start:
                    copy.start()
                else:
                    copy.wait_send()

            if i == 0:

                @pl.when(to_core == c)
                def _():
                    if start:
                        pltpu.make_async_copy(wo_in, wo.at[slot], wo_r.at[slot]).start()

                @pl.when(to_core != c)
                def _():
                    send()

            else:
                send()

    def half(j):
        return pl.ds(2 * j, 2)

    def ag_copy(buf, which, i, j):
        own = buf.at[k, half(j), c]
        return remote(
            own, own, ag_s.at[which, 2 * i + j], ag_r.at[which, k, j], dev(peer(i), z, c)
        )

    def ag_turn(buf, which, i):
        block = buf.at[peer(i), half(i - 1), c]
        return remote(
            block, block, ag_s.at[which, 9 + i], ag_d.at[which, i - 1], dev(peer(3 - i), z, c)
        )

    def ag_across(buf, which, i):
        block = buf.at[peer(i), :, c]
        return remote(
            block, block, ag_s.at[which, 6 + i], ag_x.at[which, peer(i)], sibling
        )

    def ag_send(buf, which):
        for i, j in ((1, 0), (2, 1), (1, 1), (2, 0)):
            ag_copy(buf, which, i, j).start()
        ag_across(buf, which, 0).start()

    def ag_corner(buf, which):
        for i in (1, 2):
            m = peer(i)
            wait_for(buf.at[m, half(i - 1), c], ag_r.at[which, m, i - 1])
            ag_turn(buf, which, i).start()

    def ag_relay(buf, which, i):
        m = peer(i)
        if i < 3:
            wait_for(buf.at[m, half(2 - i), c], ag_r.at[which, m, 2 - i])
        else:
            for j in range(2):
                wait_for(buf.at[m, half(j), c], ag_d.at[which, j])
        ag_across(buf, which, i).start()

    def ag_other(buf, which, i):
        m = peer(i)
        wait_for(buf.at[m, :, oc], ag_x.at[which, m])

    def ag_end(buf, which):
        for i in (1, 2):
            for j in range(2):
                ag_copy(buf, which, i, j).wait_send()
            ag_turn(buf, which, i).wait_send()
        for i in range(4):
            ag_across(buf, which, i).wait_send()

    def rs_copy(part, which, i):
        m = peer(i)
        return remote(
            part.at[m, :, oc], sib.at[which, m], rs_s.at[which, i], rs_r.at[which, m], sibling
        )

    def rs_part(part, which, i, j):
        m = peer(i)
        return remote(
            part.at[m, half(j), c],
            rcv.at[which, i - 1, half(j)],
            rs_s.at[which, 2 + 2 * i + j],
            rs_x.at[which, i - 1, j],
            dev(m, z, c),
        )

    def rs_turn(part, which, j):
        return remote(
            part.at[peer(3), half(j), c],
            turn.at[which, j],
            rs_s.at[which, 8 + j],
            rs_d.at[which, j],
            dev(peer(j + 1), z, c),
        )

    def rs_pair(part, which, i):
        m = peer(i)
        wait_for(sib.at[which, m], rs_r.at[which, m])
        return part[m, :, c].astype(F32) + sib[which, m].astype(F32)

    def rs_halves(part, which, i):
        m = peer(i)
        part[m, :, c] = rs_pair(part, which, i).astype(BF)
        if i == 3:
            for j in range(2):
                rs_turn(part, which, j).start()
        else:
            rs_part(part, which, i, i - 1).start()

    def rs_start(part, which, compute):
        for i, ready in ((3, None), (1, 3), (2, 1), (0, 2)):
            compute(i)
            rs_copy(part, which, i).start()
            if ready:
                rs_halves(part, which, ready)

    def rs_corner(part, which):
        for j in range(2):
            wait_for(turn.at[which, j], rs_d.at[which, j])
            m = peer(2 - j)
            sums = part[m, half(j), c].astype(F32) + turn[which, j].astype(F32)
            part[m, half(j), c] = sums.astype(BF)
            rs_part(part, which, 2 - j, j).start()

    def rs_sum(part, which):
        total = rs_pair(part, which, 0)
        for i in (1, 2):
            for j in range(2):
                wait_for(rcv.at[which, i - 1, half(j)], rs_x.at[which, i - 1, j])
            total = total + rcv[which, i - 1].astype(F32)
        return total.reshape(128, 1024)

    def rs_end(part, which):
        for i in range(4):
            rs_copy(part, which, i).wait_send()
        for j in range(2):
            rs_turn(part, which, j).wait_send()
            for i in (1, 2):
                rs_part(part, which, i, j).wait_send()

    def grads_to_far(grad, land, which, j):
        return remote(
            grad(far[j]), land.at[z], gz_s.at[which, 1 + j], gz_r.at[which, z], dev(k, far[j], c)
        )

    def line_adds(grad, land, add, which, start):
        @pl.when(jnp.logical_not(middle))
        def _():
            mid = 1 + z // 2
            for j in range(2):
                copy = remote(
                    grad(far_of(mid)[j]),
                    add.at[j],
                    gz_s.at[which, j],
                    gx_r.at[which, j],
                    dev(k, mid, c),
                )
                if start:
                    copy.start()
                else:
                    copy.wait_send()

    def line_near(grad, land, add, which, start):
        @pl.when(middle)
        def _():
            copy = remote(
                grad(z_end), land.at[z], gz_s.at[which, 0], gz_r.at[which, z], dev(k, z_end, c)
            )
            if start:
                copy.start()
            else:
                copy.wait_send()
                for j in range(2):
                    grads_to_far(grad, land, which, j).wait_send()

        @pl.when(jnp.logical_not(middle))
        def _():
            mid = 1 + z // 2
            copy = remote(
                grad(mid), land.at[z], gz_s.at[which, 2], gz_r.at[which, z], dev(k, mid, c)
            )
            if start:
                copy.start()
            else:
                copy.wait_send()

    def line_grads(grad, land, add, which, start):
        line_adds(grad, land, add, which, start)
        line_near(grad, land, add, which, start)

    def line_grads_relay(grad, land, add, which, j):
        @pl.when(middle)
        def _():
            wait_for(add.at[j], gx_r.at[which, j])
            mine = grad(far[j])
            mine[...] = (mine[...].astype(F32) + add[j].astype(F32)).astype(BF)
            grads_to_far(grad, land, which, j).start()

    def line_sum(grad, land, which):
        total = grad(z)[...].astype(F32)
        for j in range(2):
            wait_for(land.at[near[j]], gz_r.at[which, near[j]])
            total = total + land[near[j]].astype(F32)
        return total

    def dwgu_block(j):
        return lambda b: dwgu.at[pl.ds(2 * j, 2), b]

    def units_line(j):
        return dwgu_block(j), zgu.at[:, pl.ds(2 * j, 2)], xgu.at[:, pl.ds(2 * j, 2)], (1, 5)[j]

    def dwqkv_block(b):
        return dwqkv.at[:, b]

    def dwd_block(j):
        return lambda b: dwd.at[j, b]

    spread(lat_in, lat_place, 0, True)
    plane_weights(wqkv_in, wqkv, 0, True)
    spread_lens(True)
    out_weights(True)
    own_down = pltpu.make_async_copy(wd_in, wd.at[:, z], wd_r)
    own_down.start()
    units_to_ranks()
    spread_on(lat_in, lat_place, 0, True)
    plane_weights(wgu_in, wgu, 1, True)
    spread(dout_in, cot_place, 1, True)
    plane_weights_here(wqkv, 0)
    line_send(qkv_block, 0, (1, 0), (0, 1))
    for b in range(4):
        wait_for(own_l.at[b], tr_r.at[0, b])
    lat_f = own_l[...].reshape(128, 1024).astype(F32)
    r_one = lax.rsqrt(jnp.mean(lat_f * lat_f, axis=-1, keepdims=True) + EPS)
    n_one[k, :, c] = (lat_f * r_one).astype(BF).reshape(4, 32, 1024)
    ag_send(n_one, 0)
    line_relay(qkv_block, 0, 0)
    ag_corner(n_one, 0)
    line_relay(qkv_block, 0, 1)
    plane_weights_here(wgu, 1)
    for j in range(2):
        line_send(gu_block(j), GU[j], (1, 0), (0, 1))
    ag_relay(n_one, 0, 1)
    ag_relay(n_one, 0, 2)
    ag_relay(n_one, 0, 3)

    line_here(qkv_block, 0)

    @pl.loop(0, 4)
    def _(i):
        ag_other(n_one, 0, i)
        m = peer(i)
        block = n_one[m].reshape(256, 1024)
        out = dot_nn(block, wqkv[...].reshape(1024, 384))
        qkv[:, m] = out.astype(BF).reshape(8, 32, 384)

    spread_on(dout_in, cot_place, 1, True)
    line_send(gu_block(2), GU[2], (1, 0), (0, 1))
    line_send(down_block, 2, (1, 0), (0, 1), src=wd_in)

    wait_for(lens, ln_r)
    lane = lax.broadcasted_iota(jnp.int32, (128, 128), 1)
    row = lax.broadcasted_iota(jnp.int32, (128, 128), 0)
    first = lane < 64

    def two_heads(v):
        zero = jnp.zeros_like(v)
        return jnp.concatenate(
            [jnp.where(first, v, zero), jnp.where(first, zero, v)], axis=0
        )

    def one_of_two(v):
        return jnp.where(first, v[:128], v[128:])

    def part_of(t0, t1, col):
        return qkv[t0:t1, :, :, col * 128 : (col + 1) * 128].reshape((t1 - t0) * 128, 128)

    for t in range(8):
        span = (t + 1) * 128
        q = two_heads(part_of(t, t + 1, 0).astype(F32) * 0.125).astype(BF)
        keys = part_of(0, t + 1, 1)
        vals = part_of(0, t + 1, 2)
        pos = row + t * 128
        begin = jnp.zeros((128, 128), jnp.int32)
        end = jnp.zeros((1, 128), jnp.int32)
        for g in range(4):
            length = lens[g : g + 1, :]
            end = end + length
            begin = begin + jnp.where(end <= pos, length, 0)
        allowed = []
        for u in range(t + 1):
            ok = begin <= lane + u * 128
            if u == t:
                ok = ok & (lane <= row)
            allowed.append(ok)
        allowed = jnp.concatenate(allowed, axis=1)
        scores = dot_right(q, keys)
        sums = []
        raws = []
        for h in range(2):
            sc = jnp.where(allowed, scores[h * 128 : (h + 1) * 128], -1e30)
            top = jnp.max(sc, axis=-1, keepdims=True)
            expo = jnp.exp(sc - top)
            low = expo.astype(BF)
            probs[t, h * 128 : (h + 1) * 128, 0:span] = low
            sums.append(jnp.sum(low.astype(F32), axis=-1, keepdims=True))
        raw = dot_nn(probs[t, :, 0:span], vals)
        both = jnp.where(first, sums[0], sums[1])
        attended = one_of_two(raw) / both
        tot[t] = both
        att_f[t] = attended
        att[:, t] = attended.astype(BF).reshape(4, 32, 128)

    line_relay(gu_block(0), GU[0], 0)
    for slot in range(4):
        wait_for(wo.at[slot], wo_r.at[slot])

    def project_out(i):
        m = peer(i)
        out = dot_nn(att[m].reshape(256, 128), wo[...].reshape(128, 1024))
        part_a[m] = out.astype(BF).reshape(4, 2, 32, 1024)

    rs_start(part_a, 0, project_out)
    line_relay(gu_block(0), GU[0], 1)
    line_relay(gu_block(1), GU[1], 0)
    rs_corner(part_a, 0)
    line_relay(gu_block(1), GU[1], 1)
    line_relay(gu_block(2), GU[2], 0)
    res = own_l[...].reshape(128, 1024).astype(F32) + rs_sum(part_a, 0)
    resid[...] = res
    r_two = lax.rsqrt(jnp.mean(res * res, axis=-1, keepdims=True) + EPS)
    n_two[k, :, c] = (res * r_two).astype(BF).reshape(4, 32, 1024)
    ag_send(n_two, 2)
    for b in range(4):
        wait_for(cot.at[k, b, c], tr_r.at[1, b])
    ag_send(cot, 1)
    line_relay(gu_block(2), GU[2], 1)

    ag_corner(n_two, 2)
    line_relay(down_block, 2, 0)
    ag_relay(n_two, 2, 1)
    ag_relay(n_two, 2, 2)
    line_relay(down_block, 2, 1)
    ag_corner(cot, 1)

    def feed_forward(j, i):
        m = peer(i)
        lo, mid, hi = 256 * j, 256 * j + 128, 256 * j + 256
        gu = dot_nn(n_two[m].reshape(256, 1024), wgu[:, :, :, :, lo:hi].reshape(1024, 256))
        gate = gu[:, :128]
        up = gu[:, 128:]
        sig = jax.nn.sigmoid(gate)
        active = gate * sig
        hid[m, :, 128 * j : 128 * j + 128] = (active * up).astype(BF)
        slope[m, :, lo:mid] = up * sig * (1.0 + gate * (1.0 - sig))
        slope[m, :, mid:hi] = active

    def down_grad(j):
        left = hid[:, :, 128 * j : 128 * j + 128].reshape(1024, 128)

        @pl.loop(0, 4)
        def _(n):
            cols = pl.ds(pl.multiple_of(n * 256, 256), 256)
            right = cot[:, :, :, :, cols].reshape(1024, 256)
            dwd[j, :, :, cols] = dot_left(left, right).astype(BF).reshape(4, 32, 256)

        line_grads(dwd_block(j), zd.at[j], xd.at[j], 2 + j, True)

    line_here(gu_block(0), GU[0])

    @pl.loop(0, 3)
    def _(i):
        ag_other(n_two, 2, i)
        feed_forward(0, i)

    ag_relay(n_two, 2, 3)
    ag_other(n_two, 2, 3)
    feed_forward(0, 3)
    for i in (1, 2):
        ag_relay(cot, 1, i)
    line_here(gu_block(1), GU[1])

    @pl.loop(0, 4)
    def _(i):
        feed_forward(1, i)

    ag_relay(cot, 1, 3)
    for i in range(4):
        ag_other(cot, 1, i)
    down_grad(0)
    down_grad(1)
    line_here(gu_block(2), GU[2])

    @pl.loop(0, 4)
    def _(i):
        feed_forward(2, i)

    down_grad(2)
    line_here(down_block, 2)
    own_down.wait()

    def feed_back(i):
        m = peer(i)
        g_hid = dot_right(cot[m].reshape(256, 1024), wd[...].reshape(384, 1024))
        for j in range(6):
            cols = slice(128 * j, 128 * j + 128)
            part = g_hid[:, 128 * (j // 2) : 128 * (j // 2) + 128]
            ggu[m, :, cols] = (part * slope[m, :, cols]).astype(BF)
        out = dot_right(ggu[m], wgu[...].reshape(1024, 768))
        part_b[m] = out.astype(BF).reshape(4, 2, 32, 1024)

    def down_relay(j):
        for i in range(2):
            line_grads_relay(dwd_block(j), zd.at[j], xd.at[j], 2 + j, i)

    rs_start(part_b, 1, feed_back)
    down_relay(0)

    def units_grad(d):
        cols = pl.ds(pl.multiple_of(d * 256, 256), 256)
        left = n_two[:, :, :, :, cols].reshape(1024, 256)
        out = dot_left(left, ggu[...].reshape(1024, 768))
        dwgu[d] = out.astype(BF).reshape(4, 2, 32, 768)

    @pl.loop(0, 2)
    def _(d):
        units_grad(d)

    rs_corner(part_b, 1)
    down_relay(1)

    @pl.loop(2, 4)
    def _(d):
        units_grad(d)

    for j in range(2):
        line_adds(*units_line(j), True)
    for j in range(2):
        line_near(*units_line(j), True)
    down_relay(2)

    @pl.loop(0, 4)
    def _(i):
        m = peer(i)
        out = dot_nn(hid[m], wd[...].reshape(384, 1024))
        part_c[m] = out.astype(BF).reshape(4, 2, 32, 1024)
        rs_copy(part_c, 2, i).start()

    scaled = rs_sum(part_b, 1)
    res = resid[...]
    r_two = lax.rsqrt(jnp.mean(res * res, axis=-1, keepdims=True) + EPS)
    normed = res * r_two
    inner = jnp.mean(scaled * normed, axis=-1, keepdims=True)
    g_res = cot[k, :, c].reshape(128, 1024).astype(F32) + r_two * (scaled - normed * inner)
    gres[...] = g_res
    gbr[k, :, c] = g_res.astype(BF).reshape(4, 32, 1024)
    ag_send(gbr, 3)

    ag_corner(gbr, 3)
    ag_relay(gbr, 3, 1)
    ag_relay(gbr, 3, 2)
    line_grads_relay(*units_line(0), 0)

    def attended_grad(i):
        ag_other(gbr, 3, i)
        m = peer(i)
        out = dot_right(gbr[m].reshape(256, 1024), wo[...].reshape(128, 1024))
        gatt[:, m] = out.astype(BF).reshape(8, 32, 128)

    @pl.loop(0, 3)
    def _(i):
        attended_grad(i)

    ag_relay(gbr, 3, 3)
    for i in (3, 1, 2):
        rs_halves(part_c, 2, i)
    line_grads_relay(*units_line(0), 1)
    attended_grad(3)
    line_grads_relay(*units_line(1), 0)

    for t in range(8):
        span = (t + 1) * 128
        keys = part_of(0, t + 1, 1)
        vals = part_of(0, t + 1, 2)
        ratio = gatt[t].reshape(128, 128).astype(F32) / tot[t]
        g_raw = two_heads(ratio.astype(BF).astype(F32)).astype(BF)
        graw_two[t] = g_raw
        q_two[t] = two_heads(part_of(t, t + 1, 0).astype(F32)).astype(BF)
        prod = ratio * att_f[t]
        g_tot = -jnp.sum(two_heads(prod), axis=-1, keepdims=True)
        g_pr = dot_right(g_raw, vals)
        g_sc = probs[t, :, 0:span].astype(F32) * (g_pr + g_tot)
        gsc[t, :, 0:span] = g_sc.astype(BF)
        g_q = one_of_two(dot_nn(gsc[t, :, 0:span], keys)) * 0.125
        gqkv[:, t, :, 0:128] = g_q.astype(BF).reshape(4, 32, 128)
    @pl.loop(0, 4)
    def _(n):
        cols = pl.ds(pl.multiple_of(n * 256, 256), 256)
        right = gbr[:, :, :, :, cols].reshape(1024, 256)
        out = dot_left(att[...].reshape(1024, 128), right)
        dwo[:, :, cols] = out.astype(BF).reshape(4, 32, 256)

    def out_grads(start):
        for p in range(2):
            for cs in range(2):
                zz = 2 * c + p
                here = (zz == z) & (c == cs)
                src = dwo.at[2 * p + cs]

                @pl.when(here)
                def _():
                    if start:
                        pltpu.make_async_copy(src, go_o.at[z], go_r.at[z]).start()

                @pl.when(jnp.logical_not(here))
                def _():
                    copy = remote(
                        src, go_o.at[z], go_s.at[2 * p + cs], go_r.at[z], dev(k, zz, cs)
                    )
                    if start:
                        copy.start()
                    else:
                        copy.wait_send()

    line_grads_relay(*units_line(1), 1)
    rs_corner(part_c, 2)
    for u in range(8):
        cols = slice(u * 128, (u + 1) * 128)
        rows = (8 - u) * 256
        g_k = dot_left(gsc[u:, :, cols].reshape(rows, 128), q_two[u:].reshape(rows, 128)) * 0.125
        g_v = dot_left(probs[u:, :, cols].reshape(rows, 128), graw_two[u:].reshape(rows, 128))
        gqkv[:, u, :, 128:256] = g_k.astype(BF).reshape(4, 32, 128)
        gqkv[:, u, :, 256:384] = g_v.astype(BF).reshape(4, 32, 128)

    rs_end(part_a, 0)

    def heads_back(i):
        m = peer(i)
        out = dot_right(gqkv[m].reshape(256, 384), wqkv[...].reshape(1024, 384))
        part_a[m] = out.astype(BF).reshape(4, 2, 32, 1024)

    rs_start(part_a, 3, heads_back)

    @pl.loop(0, 4)
    def _(d):
        cols = pl.ds(pl.multiple_of(d * 256, 256), 256)
        left = n_one[:, :, :, :, cols].reshape(1024, 256)
        out = dot_left(left, gqkv[...].reshape(1024, 384))
        dwqkv[d] = out.astype(BF).reshape(4, 2, 32, 384)

    line_grads(dwqkv_block, zq, xq, 0, True)
    out_grads(True)
    rs_corner(part_a, 3)


    def gather_back(which, dst, start):
        for b in range(4):
            here = (z == k) & (z == b)
            src = back.at[which, b]
            place = dst.at[pl.ds(pl.multiple_of(32 * k, 32), 32)]

            @pl.when(here)
            def _():
                if start:
                    pltpu.make_async_copy(src, place, tb_r.at[which, k]).start()

            @pl.when(jnp.logical_not(here))
            def _():
                copy = remote(src, place, tb_s.at[which, b], tb_r.at[which, k], dev(z, b, c))
                if start:
                    copy.start()
                else:
                    copy.wait_send()

    out_f = resid[...] + rs_sum(part_c, 2)
    back[0] = out_f.astype(BF).reshape(4, 32, 1024)
    gather_back(0, lat_o, True)

    def plane_grads(land, dst, which, start):
        for i in range(4):
            m = peer(i)
            for same in (True, False):
                cc = c if same else oc
                src = land.at[z, m, cc]
                place = dst.at[rank]
                if i == 0 and same:
                    if start:
                        pltpu.make_async_copy(src, place, ga_r.at[which, rank]).start()
                else:
                    copy = remote(
                        src,
                        place,
                        ga_s.at[which, 2 * i + (0 if same else 1)],
                        ga_r.at[which, rank],
                        dev(m, z, cc),
                    )
                    if start:
                        copy.start()
                    else:
                        copy.wait_send()

    for j in range(2):
        grad, land, _, which = units_line(j)
        land[z] = line_sum(grad, land, which).astype(BF)
    plane_grads(zgu, ggu_o, 1, True)
    line_grads_relay(dwqkv_block, zq, xq, 0, 0)
    line_grads_relay(dwqkv_block, zq, xq, 0, 1)
    scaled = rs_sum(part_a, 3)
    lat_f = own_l[...].reshape(128, 1024).astype(F32)
    r_one = lax.rsqrt(jnp.mean(lat_f * lat_f, axis=-1, keepdims=True) + EPS)
    normed = lat_f * r_one
    inner = jnp.mean(scaled * normed, axis=-1, keepdims=True)
    d_lat = gres[...] + r_one * (scaled - normed * inner)
    back[1] = d_lat.astype(BF).reshape(4, 32, 1024)
    gather_back(1, dlat_o, True)

    for j in range(3):
        down_sum[32 * j : 32 * j + 32] = line_sum(dwd_block(j), zd.at[j], 2 + j)
    down_out = pltpu.make_async_copy(down_sum.at[pl.ds(0, 88)], gd_o, gd_r)
    down_out.start()
    zq[z] = line_sum(dwqkv_block, zq, 0).astype(BF)
    plane_grads(zq, gqkv_o, 0, True)

    for which, dst in ((0, lat_o), (1, dlat_o)):
        for b in range(4):
            wait_for(dst.at[pl.ds(32 * b, 32)], tb_r.at[which, b])
    for b in range(4):
        wait_for(go_o.at[b], go_r.at[b])
    for which, dst in ((1, ggu_o), (0, gqkv_o)):
        for r in range(RANKS):
            wait_for(dst.at[r], ga_r.at[which, r])
    spread(lat_in, lat_place, 0, False)
    spread_on(lat_in, lat_place, 0, False)
    spread(dout_in, cot_place, 1, False)
    spread_on(dout_in, cot_place, 1, False)
    spread_lens(False)
    plane_weights(wqkv_in, wqkv, 0, False)
    plane_weights(wgu_in, wgu, 1, False)
    line_sent(qkv_block, 0)
    for j in range(3):
        line_sent(gu_block(j), GU[j])
    line_sent(down_block, 2, wd_in)
    down_out.wait()
    out_weights(False)
    for which, buf in enumerate((n_one, cot, n_two, gbr)):
        ag_end(buf, which)
    rs_end(part_b, 1)
    rs_end(part_c, 2)
    rs_end(part_a, 3)
    for j in range(2):
        line_grads(*units_line(j), False)
    line_grads(dwqkv_block, zq, xq, 0, False)
    for j in range(3):
        line_grads(dwd_block(j), zd.at[j], xd.at[j], 2 + j, False)
    plane_grads(zgu, ggu_o, 1, False)
    plane_grads(zq, gqkv_o, 0, False)
    out_grads(False)
    gather_back(0, lat_o, False)
    gather_back(1, dlat_o, False)


def run_layer(lat, dout, lengths, gain_one, gain_two, weights):
    vm = pltpu.VMEM
    dma = pltpu.SemaphoreType.DMA
    rows = (4, 4, 2, 32)
    return pl.pallas_call(
        layer_kernel,
        out_shape=(
            jax.ShapeDtypeStruct((128, 1024), BF),
            jax.ShapeDtypeStruct((128, 1024), BF),
            jax.ShapeDtypeStruct((RANKS, 32, 384), BF),
            jax.ShapeDtypeStruct((RANKS, 32, 768), BF),
            jax.ShapeDtypeStruct((88, 1024), F32),
            jax.ShapeDtypeStruct((4, 32, 1024), BF),
        ),
        in_specs=[pl.BlockSpec(memory_space=pl.ANY)] * 2
        + [pl.BlockSpec(memory_space=pltpu.SMEM)]
        + [pl.BlockSpec(memory_space=pltpu.VMEM)] * 9,
        out_specs=[pl.BlockSpec(memory_space=pl.ANY)] * 6,
        scratch_shapes=[
            vm((8, 128), jnp.int32),
            vm((RANKS, 32, 384), BF),
            vm((RANKS, 32, 768), BF),
            vm((3, 32, 1024), BF),
            vm((4, 32, 1024), BF),
            vm((2, 4, 32, 1024), BF),
            vm((8, 128), jnp.int32),
            vm(rows + (1024,), BF),
            vm(rows + (1024,), BF),
            vm(rows + (1024,), BF),
            vm(rows + (1024,), BF),
            vm(rows + (384,), BF),
            vm(rows + (768,), BF),
            vm((3, 4, 32, 1024), BF),
            vm((4, 32, 1024), BF),
            vm((8, 4, 32, 384), BF),
            vm((4, 8, 32, 128), BF),
            vm((8, 128, 128), F32),
            vm((8, 128, 128), F32),
            vm((8, 256, 1024), BF),
            vm((8, 256, 1024), BF),
            vm(rows + (1024,), BF),
            vm(rows + (1024,), BF),
            vm(rows + (1024,), BF),
            vm((4, 4, 4, 32, 1024), BF),
            vm((4, 2, 4, 32, 1024), BF),
            vm((4, 2, 2, 32, 1024), BF),
            vm((4, 256, 384), BF),
            vm((4, 256, 768), BF),
            vm((4, 256, 768), F32),
            vm((8, 4, 32, 128), BF),
            vm((8, 256, 128), BF),
            vm((8, 256, 128), BF),
            vm((4, 8, 32, 384), BF),
            vm(rows + (384,), BF),
            vm(rows + (768,), BF),
            vm((3, 4, 32, 1024), BF),
            vm((4, 32, 1024), BF),
            vm((4, 4, 2, 32, 384), BF),
            vm((4, 4, 2, 32, 768), BF),
            vm((3, 4, 32, 1024), BF),
            vm((2, 4, 2, 32, 384), BF),
            vm((2, 4, 2, 32, 768), BF),
            vm((3, 2, 32, 1024), BF),
            vm((96, 1024), F32),
            vm((128, 1024), F32),
            vm((128, 1024), F32),
            vm((2, 4, 32, 1024), BF),
            dma((2, 4)),
            dma((2, 4)),
            dma((2, 4)),
            dma((2, 4)),
            dma,
            dma,
            dma((2, 8)),
            dma((2, 8)),
            dma((5, 4)),
            dma((5, 4)),
            dma,
            dma((4,)),
            dma((4,)),
            dma((4, 12)),
            dma((4, 4, 2)),
            dma((4, 4)),
            dma((4, 2)),
            dma((4, 12)),
            dma((4, 4)),
            dma((4, 2, 2)),
            dma((4, 2)),
            dma((6, 4)),
            dma((6, 4)),
            dma((6, 2)),
            dma((2, 8)),
            dma((2, 8)),
            dma,
            dma((4,)),
            dma((4,)),
            dma((2, 4)),
            dma((2, 4)),
        ],
        compiler_params=pltpu.CompilerParams(
            collective_id=0, has_side_effects=True, vmem_limit_bytes=60 * 1024 * 1024
        ),
    )(lat, dout, lengths, gain_one, gain_two, *weights)


def finish_kernel(
    lat,
    dlat,
    gqkv_in,
    ggu_in,
    gd,
    go_in,
    gain_one,
    gain_two,
    wq,
    wk,
    wv,
    wg,
    wu,
    lat_o,
    dlat_o,
    g_one_o,
    gq_o,
    gk_o,
    gv_o,
    go_o,
    g_two_o,
    gg_o,
    gu_o,
    gd_o,
    gqkv,
    ggu,
    go,
    sems,
):
    moves = ((gqkv_in, gqkv), (ggu_in, ggu), (go_in, go))
    moves += ((lat, lat_o.at[0]), (dlat, dlat_o.at[0]), (gd, gd_o))
    copies = [pltpu.make_async_copy(src, dst, sems.at[i]) for i, (src, dst) in enumerate(moves)]
    for copy in copies:
        copy.start()
    col_one = jnp.sum(on_diagonal(gain_one[...]), axis=1, keepdims=True)
    col_two = jnp.sum(on_diagonal(gain_two[...]), axis=1, keepdims=True)

    def as_row(acc):
        return jnp.sum(on_diagonal(jnp.sum(acc, axis=1, keepdims=True)), axis=0, keepdims=True)

    copies[0].wait()
    acc = jnp.zeros((32, 128), F32)
    for i, (w, out) in enumerate(((wq, gq_o), (wk, gk_o), (wv, gv_o))):
        for r in range(RANKS):
            cols = slice(r * 128, (r + 1) * 128)
            part = gqkv[r, :, i * 128 : (i + 1) * 128].astype(F32)
            out[:, cols] = part * col_one
            acc = acc + part * w[:, cols].astype(F32)
    g_one_o[...] = as_row(acc)
    copies[1].wait()
    acc = jnp.zeros((32, 256), F32)
    for i, (w, out) in enumerate(((wg, gg_o), (wu, gu_o))):
        parts = [None] * 96
        for r in range(RANKS):
            for j in range(3):
                third = ggu[r, :, 256 * j + 128 * i : 256 * j + 128 * i + 128].astype(F32)
                for b, unit in enumerate(units_of(r)):
                    parts[3 * unit + j] = third[:, 32 * b : 32 * b + (24 if j == 2 else 32)]
        rows = jnp.concatenate(parts, axis=1)
        out[...] = rows * col_two
        prod = rows * w[...].astype(F32)
        for n in range(11):
            acc = acc + prod[:, n * 256 : (n + 1) * 256]
    g_two_o[...] = as_row(acc)
    copies[2].wait()
    go_o[...] = (go[0].astype(F32) + go[1].astype(F32)) + (go[2].astype(F32) + go[3].astype(F32))
    for copy in copies[3:]:
        copy.wait()


def finish(*arrays):
    outs = (
        ((1, 128, 1024), BF),
        ((1, 128, 1024), BF),
        ((1, 32), F32),
        ((32, 1024), F32),
        ((32, 1024), F32),
        ((32, 1024), F32),
        ((32, 1024), F32),
        ((1, 32), F32),
        ((32, 2816), F32),
        ((32, 2816), F32),
        ((88, 1024), F32),
    )
    hbm = pl.BlockSpec(memory_space=pltpu.HBM)
    vmem = pl.BlockSpec(memory_space=pltpu.VMEM)
    return pl.pallas_call(
        finish_kernel,
        out_shape=tuple(jax.ShapeDtypeStruct(*o) for o in outs),
        in_specs=[hbm] * 6 + [vmem] * 7,
        out_specs=[vmem] * len(outs),
        scratch_shapes=[
            pltpu.VMEM((RANKS, 32, 384), BF),
            pltpu.VMEM((RANKS, 32, 768), BF),
            pltpu.VMEM((4, 32, 1024), BF),
            pltpu.SemaphoreType.DMA((6,)),
        ],
        compiler_params=pltpu.CompilerParams(vmem_limit_bytes=60 * 1024 * 1024),
    )(*arrays)


def plane_device(
    latents,
    d_out,
    lengths,
    gain_attn,
    w_query,
    w_key,
    w_value,
    w_out,
    gain_ffn,
    w_gate,
    w_up,
    w_down,
):
    gains = gain_attn.reshape(1, 32), gain_ffn.reshape(1, 32)
    weights = w_query, w_key, w_value, w_gate, w_up, w_down, w_out
    parts = run_layer(latents[0], d_out[0], lengths, *gains, weights)
    outs = finish(*parts, *gains, w_query, w_key, w_value, w_gate, w_up)
    return tuple(o.reshape(32) if o.shape == (1, 32) else o for o in outs)


def solution(mesh):
    return jax.shard_map(
        plane_device if planes_fit(mesh) else per_device,
        mesh=mesh,
        in_specs=(
            P("dp", "seq", None),
            P("dp", "seq", None),
            P("dp", None),
            P(("dp", "seq")),
            P(("dp", "seq"), None),
            P(("dp", "seq"), None),
            P(("dp", "seq"), None),
            P(("dp", "seq"), None),
            P(("dp", "seq")),
            P(("dp", "seq"), None),
            P(("dp", "seq"), None),
            P(("dp", "seq"), None),
        ),
        out_specs=(
            P("dp", "seq", None),
            P("dp", "seq", None),
            P(("dp", "seq")),
            P(("dp", "seq"), None),
            P(("dp", "seq"), None),
            P(("dp", "seq"), None),
            P(("dp", "seq"), None),
            P(("dp", "seq")),
            P(("dp", "seq"), None),
            P(("dp", "seq"), None),
            P(("dp", "seq"), None),
        ),
        check_vma=False,
    )
```

```python
import functools
import math

import jax
import jax.numpy as jnp
from jax import lax
from jax.experimental import pallas as pl
from jax.experimental.pallas import tpu as pltpu
from jax.sharding import PartitionSpec as P

HEADS = 16


EPS = 1e-05


def norm_rows(values, gain_vec):
    factor = lax.rsqrt(jnp.mean(values * values, axis=-1, keepdims=True) + EPS)
    normed = values * factor
    return (normed * gain_vec, normed, factor)


def norm_back(grad_out, normed, factor, gain_vec):
    scaled = grad_out * gain_vec
    inner = jnp.mean(scaled * normed, axis=-1, keepdims=True)
    return (factor * (scaled - normed * inner), jnp.sum(grad_out * normed, axis=0))


def dot_left(left, right):
    return lax.dot_general(
        left, right, (((0,), (0,)), ((), ())), preferred_element_type=jnp.float32
    )


def dot_right(left, right):
    return lax.dot_general(
        left, right, (((1,), (1,)), ((), ())), preferred_element_type=jnp.float32
    )


def per_device(
    latents,
    d_out,
    lengths,
    gain_attn,
    w_query,
    w_key,
    w_value,
    w_out,
    gain_ffn,
    w_gate,
    w_up,
    w_down,
):
    g_attn, full_query, full_key, full_value, full_out, g_ffn, full_gate, full_up, full_down = (
        lax.all_gather(gain_attn, ("dp", "seq"), axis=0, tiled=True),
        lax.all_gather(w_query, ("dp", "seq"), axis=0, tiled=True),
        lax.all_gather(w_key, ("dp", "seq"), axis=0, tiled=True),
        lax.all_gather(w_value, ("dp", "seq"), axis=0, tiled=True),
        lax.all_gather(w_out, ("dp", "seq"), axis=0, tiled=True),
        lax.all_gather(gain_ffn, ("dp", "seq"), axis=0, tiled=True),
        lax.all_gather(w_gate, ("dp", "seq"), axis=0, tiled=True),
        lax.all_gather(w_up, ("dp", "seq"), axis=0, tiled=True),
        lax.all_gather(w_down, ("dp", "seq"), axis=0, tiled=True),
    )
    gain_one = g_attn.astype(jnp.float32)
    gain_two = g_ffn.astype(jnp.float32)
    inputs_f = latents[0].astype(jnp.float32)
    row_count, model_width = inputs_f.shape
    head_size = model_width // HEADS
    group_rows = row_count * lax.axis_size("seq")
    here = lax.axis_index("seq") * row_count + jnp.arange(row_count, dtype=jnp.int32)
    seq_lens = lengths[0]
    seq_ends = jnp.cumsum(seq_lens, dtype=jnp.int32)
    begins = jnp.sum(
        jnp.where(seq_ends[None, :] <= here[:, None], seq_lens[None, :], 0), axis=1, dtype=jnp.int32
    )
    key_block = math.gcd(group_rows, 1024)
    block_count = group_rows // key_block
    key_positions = jnp.arange(group_rows, dtype=jnp.int32).reshape(block_count, key_block)
    h_one_f, normed_one, factor_one = norm_rows(inputs_f, gain_one)
    h_one = h_one_f.astype(jnp.bfloat16)
    query_proj = jnp.dot(h_one, full_query, preferred_element_type=jnp.float32).astype(jnp.bfloat16)
    key_proj = jnp.dot(h_one, full_key, preferred_element_type=jnp.float32).astype(jnp.bfloat16)
    value_proj = jnp.dot(h_one, full_value, preferred_element_type=jnp.float32).astype(jnp.bfloat16)
    keys_all, values_all = (
        lax.all_gather(key_proj, "seq", axis=0, tiled=True),
        lax.all_gather(value_proj, "seq", axis=0, tiled=True),
    )
    query_heads = query_proj.reshape(row_count, HEADS, head_size)

    def split_blocks(array):
        return array.reshape(block_count, key_block, HEADS, head_size)

    def block_scores(key_piece, pos_piece):
        scores = (
            jnp.einsum("qhd,khd->hqk", query_heads, key_piece, preferred_element_type=jnp.float32)
            * 0.125
        )
        allowed = (pos_piece[None, :] <= here[:, None]) & (pos_piece[None, :] >= begins[:, None])
        return (scores, allowed[None])

    def max_step(running, pieces):
        key_piece, pos_piece = pieces
        scores, allowed = block_scores(key_piece, pos_piece)
        return (jnp.maximum(running, jnp.max(jnp.where(allowed, scores, -1e30), axis=-1)), None)

    row_max, _ = lax.scan(
        max_step,
        jnp.full((HEADS, row_count), -1e30, jnp.float32),
        (split_blocks(keys_all), key_positions),
    )

    def sum_step(running, pieces):
        key_piece, value_piece, pos_piece = pieces
        scores, allowed = block_scores(key_piece, pos_piece)
        expon = jnp.where(
            allowed, jnp.exp(jnp.where(allowed, scores, -1e30) - row_max[:, :, None]), 0.0
        )
        rounded = expon.astype(jnp.bfloat16)
        total_sum, raw_sum = running
        total_sum = total_sum + jnp.sum(rounded.astype(jnp.float32), axis=-1)
        raw_sum = raw_sum + jnp.einsum(
            "hqk,khd->qhd", rounded, value_piece, preferred_element_type=jnp.float32
        )
        return ((total_sum, raw_sum), None)

    (total_sum, raw_sum), _ = lax.scan(
        sum_step,
        (
            jnp.zeros((HEADS, row_count), jnp.float32),
            jnp.zeros((row_count, HEADS, head_size), jnp.float32),
        ),
        (split_blocks(keys_all), split_blocks(values_all), key_positions),
    )
    totals_rows = jnp.transpose(total_sum)
    attended = raw_sum / totals_rows[:, :, None]
    attended_low = attended.reshape(row_count, model_width).astype(jnp.bfloat16)
    resid = inputs_f + jnp.dot(attended_low, full_out, preferred_element_type=jnp.float32)
    h_two_f, normed_two, factor_two = norm_rows(resid, gain_two)
    h_two = h_two_f.astype(jnp.bfloat16)
    gate_proj = jnp.dot(h_two, full_gate, preferred_element_type=jnp.float32)
    up_proj = jnp.dot(h_two, full_up, preferred_element_type=jnp.float32)
    gate_sigmoid = jax.nn.sigmoid(gate_proj)
    gate_active = gate_proj * gate_sigmoid
    hidden = (gate_active * up_proj).astype(jnp.bfloat16)
    outputs = resid + jnp.dot(hidden, full_down, preferred_element_type=jnp.float32)
    latents_out = outputs.astype(jnp.bfloat16)[None]
    grad_out = d_out[0]
    grad_down = dot_left(hidden, grad_out)
    g_hidden = dot_right(grad_out, full_down)
    g_gate = (g_hidden * up_proj * gate_sigmoid * (1.0 + gate_proj * (1.0 - gate_sigmoid))).astype(
        jnp.bfloat16
    )
    g_up = (g_hidden * gate_active).astype(jnp.bfloat16)
    grad_gate = dot_left(h_two, g_gate)
    grad_up = dot_left(h_two, g_up)
    g_h_two = dot_right(g_gate, full_gate) + dot_right(g_up, full_up)
    g_norm_two, grad_gain_two = norm_back(g_h_two, normed_two, factor_two, gain_two)
    g_resid = grad_out.astype(jnp.float32) + g_norm_two
    g_branch = g_resid.astype(jnp.bfloat16)
    grad_out_proj = dot_left(attended_low, g_branch)
    g_att = dot_right(g_branch, full_out).reshape(row_count, HEADS, head_size).astype(jnp.bfloat16)
    g_att_f = g_att.astype(jnp.float32)
    g_raw = (g_att_f / totals_rows[:, :, None]).astype(jnp.bfloat16)
    g_total = jnp.transpose(-jnp.sum(g_att_f * raw_sum, axis=-1) / (totals_rows * totals_rows))
    keys_back, values_back = (
        lax.all_gather(key_proj, "seq", axis=0, tiled=True),
        lax.all_gather(value_proj, "seq", axis=0, tiled=True),
    )

    def score_grads(key_piece, value_piece, pos_piece):
        scores, allowed = block_scores(key_piece, pos_piece)
        expon = jnp.where(
            allowed, jnp.exp(jnp.where(allowed, scores, -1e30) - row_max[:, :, None]), 0.0
        )
        g_probs = jnp.einsum("qhd,khd->hqk", g_raw, value_piece, preferred_element_type=jnp.float32)
        g_scores = (expon * (g_probs + g_total[:, :, None])).astype(jnp.bfloat16)
        return (expon, g_scores)

    def grad_step(running, pieces):
        key_piece, value_piece, pos_piece = pieces
        expon, g_scores = score_grads(key_piece, value_piece, pos_piece)
        rounded = expon.astype(jnp.bfloat16)
        running = (
            running
            + jnp.einsum("hqk,khd->qhd", g_scores, key_piece, preferred_element_type=jnp.float32)
            * 0.125
        )
        g_key_piece = (
            jnp.einsum("hqk,qhd->khd", g_scores, query_heads, preferred_element_type=jnp.float32)
            * 0.125
        )
        g_value_piece = jnp.einsum(
            "hqk,qhd->khd", rounded, g_raw, preferred_element_type=jnp.float32
        )
        return (running, (g_key_piece, g_value_piece))

    g_query_f, (g_keys, g_values) = lax.scan(
        grad_step,
        jnp.zeros((row_count, HEADS, head_size), jnp.float32),
        (split_blocks(keys_back), split_blocks(values_back), key_positions),
    )
    mine_key, mine_value = (
        lax.psum_scatter(
            g_keys.reshape(group_rows, model_width).astype(jnp.bfloat16),
            "seq",
            scatter_dimension=0,
            tiled=True,
        ).astype(jnp.float32),
        lax.psum_scatter(
            g_values.reshape(group_rows, model_width).astype(jnp.bfloat16),
            "seq",
            scatter_dimension=0,
            tiled=True,
        ).astype(jnp.float32),
    )
    g_key = mine_key.astype(jnp.bfloat16)
    g_value = mine_value.astype(jnp.bfloat16)
    g_query = g_query_f.reshape(row_count, model_width).astype(jnp.bfloat16)
    grad_query = dot_left(h_one, g_query)
    grad_key = dot_left(h_one, g_key)
    grad_value = dot_left(h_one, g_value)
    g_h_one = (
        dot_right(g_query, full_query) + dot_right(g_key, full_key) + dot_right(g_value, full_value)
    )
    g_norm_one, grad_gain_one = norm_back(g_h_one, normed_one, factor_one, gain_one)
    d_latents = (g_resid + g_norm_one).astype(jnp.bfloat16)[None]
    gain_pair = jnp.stack((grad_gain_one, grad_gain_two), axis=1)
    summed = (
        lax.psum_scatter(gain_pair, ("dp", "seq"), scatter_dimension=0, tiled=True),
        lax.psum_scatter(grad_query, ("dp", "seq"), scatter_dimension=0, tiled=True),
        lax.psum_scatter(grad_key, ("dp", "seq"), scatter_dimension=0, tiled=True),
        lax.psum_scatter(grad_value, ("dp", "seq"), scatter_dimension=0, tiled=True),
        lax.psum_scatter(grad_out_proj, ("dp", "seq"), scatter_dimension=0, tiled=True),
        lax.psum_scatter(grad_gate, ("dp", "seq"), scatter_dimension=0, tiled=True),
        lax.psum_scatter(grad_up, ("dp", "seq"), scatter_dimension=0, tiled=True),
        lax.psum_scatter(grad_down, ("dp", "seq"), scatter_dimension=0, tiled=True),
    )
    return (
        latents_out,
        d_latents,
        summed[0][:, 0],
        summed[1],
        summed[2],
        summed[3],
        summed[4],
        summed[0][:, 1],
        summed[5],
        summed[6],
        summed[7],
    )


MESH = pl.DeviceIdType.MESH
BF = jnp.bfloat16
F32 = jnp.float32
DP, ZS, CORES = 4, 4, 2
RANKS = DP * CORES
GU = (1, 3, 4)


def units_of(rank):
    return [8 * (rank // CORES) + CORES * b + rank % CORES for b in range(ZS)]


def planes_fit(mesh):
    return mesh.shape["dp"] == DP and mesh.shape["seq"] == ZS * CORES


def dot_nn(left, right):
    return jnp.dot(left, right, preferred_element_type=F32)


def remote(src, dst, send_sem, recv_sem, device):
    return pltpu.make_async_remote_copy(
        src_ref=src,
        dst_ref=dst,
        send_sem=send_sem,
        recv_sem=recv_sem,
        device_id=device,
        device_id_type=MESH,
    )


def wait_for(ref, sem):
    pltpu.make_async_copy(ref, ref, sem).wait()


def on_diagonal(row):
    at = lax.broadcasted_iota(jnp.int32, (32, 32), 0) == lax.broadcasted_iota(jnp.int32, (32, 32), 1)
    return jnp.where(at, row.astype(F32), 0.0)


def layer_kernel(
    lat_in,
    dout_in,
    lengths_in,
    gain_one_in,
    gain_two_in,
    wq_in,
    wk_in,
    wv_in,
    wg_in,
    wu_in,
    wd_rows_in,
    wo_in,
    lat_o,
    dlat_o,
    gqkv_o,
    ggu_o,
    gd_o,
    go_o,
    gain_one,
    gain_two,
    wq_raw,
    wk_raw,
    wv_raw,
    wg_raw,
    wu_raw,
    wd_raw,
    in_r,
    lens_in,
    wqkv_in,
    wgu_in,
    wd_in,
    own_l,
    stop,
    lens,
    n_one,
    n_two,
    cot,
    gbr,
    wqkv,
    wgu,
    wd,
    wo,
    qkv,
    att,
    att_f,
    tot,
    probs,
    gsc,
    part_a,
    part_b,
    part_c,
    sib,
    rcv,
    turn,
    hid,
    ggu,
    slope,
    gatt,
    graw_two,
    q_two,
    gqkv,
    dwqkv,
    dwgu,
    dwd,
    dwo,
    zq,
    zgu,
    zd,
    zo,
    xo,
    xq,
    xgu,
    xd,
    down_sum,
    resid,
    gres,
    back,
    tr_s,
    tr_r,
    tx_r,
    tz_s,
    ln_s,
    ln_r,
    wa_s,
    wa_r,
    wz_s,
    wz_r,
    wd_r,
    wo_s,
    wo_r,
    ag_s,
    ag_r,
    ag_x,
    ag_d,
    rs_s,
    rs_r,
    rs_x,
    rs_d,
    gz_s,
    gz_r,
    gx_r,
    ga_s,
    ga_r,
    gd_r,
    go_s,
    go_r,
    go_x,
    go_z,
    tb_s,
    tb_r,
):
    k = lax.axis_index("dp")
    s = lax.axis_index("seq")
    z = s // CORES
    c = s % CORES
    oc = 1 - c
    rank = CORES * k + c

    def dev(kk, zz, cc):
        return (kk, CORES * zz + cc)

    def peer(i):
        return 2 * ((k // 2 + i // 2) % 2) + (k % 2 + i % 2) % 2

    def zpeer(i):
        return (z + i) % ZS

    sibling = dev(k, z, oc)

    loads = (
        (gain_one_in, gain_one),
        (gain_two_in, gain_two),
        (wq_in, wq_raw),
        (wk_in, wk_raw),
        (wv_in, wv_raw),
        (wd_rows_in, wd_raw),
        (wg_in, wg_raw),
        (wu_in, wu_raw),
    )
    loads = [pltpu.make_async_copy(src, dst, in_r.at[i]) for i, (src, dst) in enumerate(loads)]
    for load in loads:
        load.start()

    barrier = pltpu.get_barrier_semaphore()
    greeted = 0
    for di in range(4):
        for dz in range(4):
            if di or dz:
                pl.semaphore_signal(
                    barrier, inc=1, device_id=dev(peer(di), zpeer(dz), c), device_id_type=MESH
                )
                greeted += 1
            if di == 0 or dz == 0:
                pl.semaphore_signal(
                    barrier, inc=1, device_id=dev(peer(di), zpeer(dz), oc), device_id_type=MESH
                )
                greeted += 1

    def scaled_rows(w, gain):
        return dot_nn(on_diagonal(gain[...]).astype(BF), w[...])

    def units_to_ranks():
        both = [scaled_rows(w, gain_two) for w in (wg_raw, wu_raw)]
        gap = jnp.zeros((32, 8), F32)
        for r in range(RANKS):
            for j in range(3):
                for i, rows in enumerate(both):
                    parts = []
                    for unit in units_of(r):
                        at = 88 * unit + 32 * j
                        parts += [rows[:, at : at + 32]] if j < 2 else [rows[:, at : at + 24], gap]
                    lo = 256 * j + 128 * i
                    wgu_in[r, :, lo : lo + 128] = jnp.concatenate(parts, axis=1).astype(BF)

    tile_row = lax.broadcasted_iota(jnp.int32, (8, 128), 0)
    tile = jnp.zeros((8, 128), jnp.int32)
    for i in range(4):
        tile = jnp.where(tile_row == i, lengths_in[0, i], tile)
    lens_in[...] = tile

    pl.semaphore_wait(barrier, greeted)

    def spread(src, final_of, which, start):
        for q in range(4):
            piece = src.at[pl.ds(32 * q, 32)]

            @pl.when((z == k) & (k == q))
            def _():
                if start:
                    pltpu.make_async_copy(piece, final_of(q, z), tr_r.at[which, z]).start()

            @pl.when((z == k) & (k != q))
            def _():
                copy = remote(
                    piece, final_of(q, z), tr_s.at[which, q], tr_r.at[which, z], dev(q, z, c)
                )
                if start:
                    copy.start()
                else:
                    copy.wait_send()

            @pl.when((z != k) & (k != q))
            def _():
                copy = remote(
                    piece, stop.at[which, k], tr_s.at[which, q], tx_r.at[which, k], dev(q, z, c)
                )
                if start:
                    copy.start()
                else:
                    copy.wait_send()

    def spread_on(src, final_of, which, start):
        for i in range(1, 4):
            g = zpeer(i)

            def send(piece):
                copy = remote(
                    piece, final_of(k, z), tz_s.at[which, i], tr_r.at[which, z], dev(k, g, c)
                )
                if start:
                    copy.start()
                else:
                    copy.wait_send()

            @pl.when(g == k)
            def _():
                send(src.at[pl.ds(pl.multiple_of(32 * k, 32), 32)])

            @pl.when(g != k)
            def _():
                if start:
                    wait_for(stop.at[which, g], tx_r.at[which, g])
                send(stop.at[which, g])

    def lat_place(q, b):
        return own_l.at[b]

    def cot_place(q, b):
        return cot.at[q, b, c]

    def spread_lens(start):
        here = z == k

        @pl.when(here)
        def _():
            if start:
                pltpu.make_async_copy(lens_in, lens, ln_r).start()

        @pl.when(jnp.logical_not(here))
        def _():
            copy = remote(lens_in, lens, ln_s, ln_r, dev(z, k, c))
            if start:
                copy.start()
            else:
                copy.wait_send()

    def plane_weights(src, dst, which, start):
        for i in range(4):
            for same in (True, False):
                cc = c if same else oc
                target = CORES * peer(i) + cc
                piece = src.at[target]
                place = dst.at[k, z, c]
                if i == 0 and same:
                    if start:
                        pltpu.make_async_copy(piece, place, wa_r.at[which, rank]).start()
                else:
                    copy = remote(
                        piece,
                        place,
                        wa_s.at[which, 2 * i + (0 if same else 1)],
                        wa_r.at[which, rank],
                        dev(peer(i), z, cc),
                    )
                    if start:
                        copy.start()
                    else:
                        copy.wait_send()

    def plane_weights_here(dst, which):
        for kk in range(4):
            for cc in range(2):
                wait_for(dst.at[kk, z, cc], wa_r.at[which, CORES * kk + cc])

    middle = (z == 1) | (z == 2)
    near = (1 + z % 2, 2 + z // 2 - 2 * (z % 2))
    z_end = 3 * (z // 2)

    def far_of(place):
        return (6 - 3 * place, 3 - place)

    far = far_of(z)

    def line_copy(block, which, slot, b, place, src=None):
        src = block(b) if src is None else src
        return remote(src, block(b), wz_s.at[which, slot], wz_r.at[which, b], dev(k, place, c))

    def line_send(block, which, from_ends, from_middle, start=True, src=None):
        def send(slots):
            for j in slots:
                copy = line_copy(block, which, j, z, near[j], src)
                if start:
                    copy.start()
                else:
                    copy.wait_send()

        if from_ends:

            @pl.when(jnp.logical_not(middle))
            def _():
                send(from_ends)

        if from_middle:

            @pl.when(middle)
            def _():
                send(from_middle)

    def line_relay(block, which, j):
        @pl.when(middle)
        def _():
            wait_for(block(far[j]), wz_r.at[which, far[j]])
            line_copy(block, which, 2 + j, far[j], z_end).start()

    def line_sent(block, which, src=None):
        line_send(block, which, (0, 1), (0, 1), False, src)

        @pl.when(middle)
        def _():
            for j in range(2):
                line_copy(block, which, 2 + j, far[j], z_end).wait_send()

    def line_here(block, which):
        @pl.when(middle)
        def _():
            wait_for(block(z_end), wz_r.at[which, z_end])

        @pl.when(jnp.logical_not(middle))
        def _():
            for i in range(1, 4):
                wait_for(block(zpeer(i)), wz_r.at[which, zpeer(i)])

    def qkv_block(b):
        return wqkv.at[:, b]

    def gu_block(j):
        return lambda b: wgu.at[:, b, :, :, 256 * j : 256 * j + 256]

    def down_block(b):
        return wd.at[:, b]

    side = z // 2

    def out_block(b):
        return wo.at[pl.ds(2 * (b % 2), 2)]

    def out_across(start):
        place = wo.at[2 * (z % 2) + c]

        @pl.when(c == side)
        def _():
            if start:
                pltpu.make_async_copy(wo_in, place, wo_r.at[c]).start()

        @pl.when(c != side)
        def _():
            copy = remote(wo_in, place, wo_s.at[0], wo_r.at[c], sibling)
            if start:
                copy.start()
            else:
                copy.wait_send()

    def out_along(start):
        @pl.when(c == side)
        def _():
            if start:
                for i in range(2):
                    wait_for(wo.at[2 * (z % 2) + i], wo_r.at[i])
            for j in (1, 0):
                copy = line_copy(out_block, 5, j, z, near[j])
                if start:
                    copy.start()
                else:
                    copy.wait_send()

    def out_relay(start):
        @pl.when(middle & (c != side))
        def _():
            for j in range(2):
                if start:
                    wait_for(out_block(far[j]), wz_r.at[5, far[j]])
                copy = line_copy(out_block, 5, 2 + j, far[j], z_end)
                if start:
                    copy.start()
                else:
                    copy.wait_send()

    def out_here():
        @pl.when(c == side)
        def _():
            other = 4 * side + 1 - z
            wait_for(out_block(other), wz_r.at[5, other])

        @pl.when((c != side) & jnp.logical_not(middle))
        def _():
            for j in range(2):
                wait_for(out_block(2 * c + j), wz_r.at[5, 2 * c + j])

    def half(j):
        return pl.ds(2 * j, 2)

    def ag_copy(buf, which, i, j):
        own = buf.at[k, half(j), c]
        return remote(
            own, own, ag_s.at[which, 2 * i + j], ag_r.at[which, k, j], dev(peer(i), z, c)
        )

    def ag_turn(buf, which, i):
        block = buf.at[peer(i), half(i - 1), c]
        return remote(
            block, block, ag_s.at[which, 9 + i], ag_d.at[which, i - 1], dev(peer(3 - i), z, c)
        )

    def ag_across(buf, which, i):
        block = buf.at[peer(i), :, c]
        return remote(
            block, block, ag_s.at[which, 6 + i], ag_x.at[which, peer(i)], sibling
        )

    def ag_send(buf, which):
        for i, j in ((1, 0), (2, 1), (1, 1), (2, 0)):
            ag_copy(buf, which, i, j).start()
        ag_across(buf, which, 0).start()

    def ag_corner(buf, which):
        for i in (1, 2):
            m = peer(i)
            wait_for(buf.at[m, half(i - 1), c], ag_r.at[which, m, i - 1])
            ag_turn(buf, which, i).start()

    def ag_relay(buf, which, i):
        m = peer(i)
        if i < 3:
            wait_for(buf.at[m, half(2 - i), c], ag_r.at[which, m, 2 - i])
        else:
            for j in range(2):
                wait_for(buf.at[m, half(j), c], ag_d.at[which, j])
        ag_across(buf, which, i).start()

    def ag_other(buf, which, i):
        m = peer(i)
        wait_for(buf.at[m, :, oc], ag_x.at[which, m])

    def ag_end(buf, which):
        for i in (1, 2):
            for j in range(2):
                ag_copy(buf, which, i, j).wait_send()
            ag_turn(buf, which, i).wait_send()
        for i in range(4):
            ag_across(buf, which, i).wait_send()

    def rs_copy(part, which, i):
        m = peer(i)
        return remote(
            part.at[m, :, oc], sib.at[which, m], rs_s.at[which, i], rs_r.at[which, m], sibling
        )

    def rs_part(part, which, i, j):
        m = peer(i)
        return remote(
            part.at[m, half(j), c],
            rcv.at[which, i - 1, half(j)],
            rs_s.at[which, 2 + 2 * i + j],
            rs_x.at[which, i - 1, j],
            dev(m, z, c),
        )

    def rs_turn(part, which, j):
        return remote(
            part.at[peer(3), half(j), c],
            turn.at[which, j],
            rs_s.at[which, 8 + j],
            rs_d.at[which, j],
            dev(peer(j + 1), z, c),
        )

    def rs_pair(part, which, i):
        m = peer(i)
        wait_for(sib.at[which, m], rs_r.at[which, m])
        return part[m, :, c].astype(F32) + sib[which, m].astype(F32)

    def rs_halves(part, which, i):
        m = peer(i)
        part[m, :, c] = rs_pair(part, which, i).astype(BF)
        if i == 3:
            for j in range(2):
                rs_turn(part, which, j).start()
        else:
            rs_part(part, which, i, i - 1).start()

    def rs_start(part, which, compute):
        for i, ready in ((3, None), (1, 3), (2, 1), (0, 2)):
            compute(i)
            rs_copy(part, which, i).start()
            if ready:
                rs_halves(part, which, ready)

    def rs_corner(part, which):
        for j in range(2):
            wait_for(turn.at[which, j], rs_d.at[which, j])
            m = peer(2 - j)
            sums = part[m, half(j), c].astype(F32) + turn[which, j].astype(F32)
            part[m, half(j), c] = sums.astype(BF)
            rs_part(part, which, 2 - j, j).start()

    def rs_sum(part, which):
        total = rs_pair(part, which, 0)
        for i in (1, 2):
            for j in range(2):
                wait_for(rcv.at[which, i - 1, half(j)], rs_x.at[which, i - 1, j])
            total = total + rcv[which, i - 1].astype(F32)
        return total.reshape(128, 1024)

    def rs_end(part, which):
        for i in range(4):
            rs_copy(part, which, i).wait_send()
        for j in range(2):
            rs_turn(part, which, j).wait_send()
            for i in (1, 2):
                rs_part(part, which, i, j).wait_send()

    def grads_to_far(grad, land, which, j):
        return remote(
            grad(far[j]), land.at[z], gz_s.at[which, 1 + j], gz_r.at[which, z], dev(k, far[j], c)
        )

    def line_adds(grad, land, add, which, start):
        @pl.when(jnp.logical_not(middle))
        def _():
            mid = 1 + z // 2
            for j in range(2):
                copy = remote(
                    grad(far_of(mid)[j]),
                    add.at[j],
                    gz_s.at[which, j],
                    gx_r.at[which, j],
                    dev(k, mid, c),
                )
                if start:
                    copy.start()
                else:
                    copy.wait_send()

    def line_near(grad, land, add, which, start):
        @pl.when(middle)
        def _():
            copy = remote(
                grad(z_end), land.at[z], gz_s.at[which, 0], gz_r.at[which, z], dev(k, z_end, c)
            )
            if start:
                copy.start()
            else:
                copy.wait_send()
                for j in range(2):
                    grads_to_far(grad, land, which, j).wait_send()

        @pl.when(jnp.logical_not(middle))
        def _():
            mid = 1 + z // 2
            copy = remote(
                grad(mid), land.at[z], gz_s.at[which, 2], gz_r.at[which, z], dev(k, mid, c)
            )
            if start:
                copy.start()
            else:
                copy.wait_send()

    def line_grads(grad, land, add, which, start):
        line_adds(grad, land, add, which, start)
        line_near(grad, land, add, which, start)

    def line_grads_relay(grad, land, add, which, j):
        @pl.when(middle)
        def _():
            wait_for(add.at[j], gx_r.at[which, j])
            mine = grad(far[j])
            mine[...] = (mine[...].astype(F32) + add[j].astype(F32)).astype(BF)
            grads_to_far(grad, land, which, j).start()

    def line_sum(grad, land, which):
        total = grad(z)[...].astype(F32)
        for j in range(2):
            wait_for(land.at[near[j]], gz_r.at[which, near[j]])
            total = total + land[near[j]].astype(F32)
        return total

    def dwgu_block(j):
        return lambda b: dwgu.at[pl.ds(2 * j, 2), b]

    def units_line(j):
        return dwgu_block(j), zgu.at[:, pl.ds(2 * j, 2)], xgu.at[:, pl.ds(2 * j, 2)], (1, 5)[j]

    def dwqkv_block(b):
        return dwqkv.at[:, b]

    def dwd_block(j):
        return lambda b: dwd.at[j, b]

    def out_grads_add(start):
        @pl.when((c != side) & jnp.logical_not(middle))
        def _():
            copy = remote(dwo, xo, go_s.at[0], go_x, dev(k, 1 + side, c))
            if start:
                copy.start()
            else:
                copy.wait_send()

    def out_grads_near(start):
        @pl.when(c == side)
        def _():
            other = 4 * side + 1 - z
            copy = remote(
                dwo.at[pl.ds(2 * (other % 2), 2)], zo.at[0], go_s.at[0], go_z.at[0], dev(k, other, c)
            )
            if start:
                copy.start()
            else:
                copy.wait_send()

    def out_grads_relay(start):
        @pl.when((c != side) & middle)
        def _():
            if start:
                wait_for(xo, go_x)
                dwo[...] = (dwo[...].astype(F32) + xo[...].astype(F32)).astype(BF)
            for p in range(2):
                copy = remote(
                    dwo.at[pl.ds(2 * p, 2)], zo.at[1], go_s.at[p], go_z.at[1], dev(k, 2 * c + p, c)
                )
                if start:
                    copy.start()
                else:
                    copy.wait_send()

    def out_grads_home(start):
        @pl.when(c == side)
        def _():
            mine = dwo.at[pl.ds(2 * (z % 2), 2)]
            if start:
                total = mine[...].astype(F32)
                for j in range(2):
                    wait_for(zo.at[j], go_z.at[j])
                    total = total + zo[j].astype(F32)
                mine[...] = total.astype(BF)
                pltpu.make_async_copy(dwo.at[2 * (z % 2) + c], go_o, go_r).start()
            copy = remote(dwo.at[2 * (z % 2) + oc], go_o, go_s.at[1], go_r, sibling)
            if start:
                copy.start()
            else:
                copy.wait_send()

    def gather_back(which, dst, start):
        for b in range(4):
            here = (z == k) & (z == b)
            src = back.at[which, b]
            place = dst.at[pl.ds(pl.multiple_of(32 * k, 32), 32)]

            @pl.when(here)
            def _():
                if start:
                    pltpu.make_async_copy(src, place, tb_r.at[which, k]).start()

            @pl.when(jnp.logical_not(here))
            def _():
                copy = remote(src, place, tb_s.at[which, b], tb_r.at[which, k], dev(z, b, c))
                if start:
                    copy.start()
                else:
                    copy.wait_send()

    spread(lat_in, lat_place, 0, True)
    for load in loads[:5]:
        load.wait()
    for i, w in enumerate((wq_raw, wk_raw, wv_raw)):
        rows = scaled_rows(w, gain_one).astype(BF)
        for r in range(RANKS):
            wqkv_in[r, :, i * 128 : (i + 1) * 128] = rows[:, r * 128 : (r + 1) * 128]
    plane_weights(wqkv_in, wqkv, 0, True)
    spread_lens(True)
    loads[5].wait()
    wd_in[0] = wd_raw[0:32]
    wd_in[1] = wd_raw[32:64]
    wd_in[2, 0:16] = wd_raw[64:80]
    wd_in[2, 16:32] = jnp.concatenate([wd_raw[80:88], jnp.zeros((8, 1024), BF)], axis=0)
    out_across(True)
    own_down = pltpu.make_async_copy(wd_in, wd.at[:, z], wd_r)
    own_down.start()
    out_along(True)
    for load in loads[6:]:
        load.wait()
    units_to_ranks()
    spread_on(lat_in, lat_place, 0, True)
    plane_weights(wgu_in, wgu, 1, True)
    spread(dout_in, cot_place, 1, True)
    plane_weights_here(wqkv, 0)
    line_send(qkv_block, 0, (1, 0), (0, 1))
    out_relay(True)
    for b in range(4):
        wait_for(own_l.at[b], tr_r.at[0, b])
    lat_f = own_l[...].reshape(128, 1024).astype(F32)
    r_one = lax.rsqrt(jnp.mean(lat_f * lat_f, axis=-1, keepdims=True) + EPS)
    n_one[k, :, c] = (lat_f * r_one).astype(BF).reshape(4, 32, 1024)
    ag_send(n_one, 0)
    line_relay(qkv_block, 0, 0)
    ag_corner(n_one, 0)
    line_relay(qkv_block, 0, 1)
    spread_on(dout_in, cot_place, 1, True)
    plane_weights_here(wgu, 1)
    for j in range(2):
        line_send(gu_block(j), GU[j], (1, 0), (0, 1))
    ag_relay(n_one, 0, 1)
    ag_relay(n_one, 0, 2)
    ag_relay(n_one, 0, 3)

    line_here(qkv_block, 0)

    @pl.loop(0, 4)
    def _(i):
        ag_other(n_one, 0, i)
        m = peer(i)
        block = n_one[m].reshape(256, 1024)
        out = dot_nn(block, wqkv[...].reshape(1024, 384))
        qkv[:, m] = out.astype(BF).reshape(8, 32, 384)

    line_send(gu_block(2), GU[2], (1, 0), (0, 1))
    line_send(down_block, 2, (1, 0), (0, 1), src=wd_in)

    for b in range(4):
        wait_for(cot.at[k, b, c], tr_r.at[1, b])
    ag_send(cot, 1)
    wait_for(lens, ln_r)
    lane = lax.broadcasted_iota(jnp.int32, (128, 128), 1)
    row = lax.broadcasted_iota(jnp.int32, (128, 128), 0)
    first = lane < 64

    def two_heads(v):
        zero = jnp.zeros_like(v)
        return jnp.concatenate(
            [jnp.where(first, v, zero), jnp.where(first, zero, v)], axis=0
        )

    def one_of_two(v):
        return jnp.where(first, v[:128], v[128:])

    def part_of(t0, t1, col):
        return qkv[t0:t1, :, :, col * 128 : (col + 1) * 128].reshape((t1 - t0) * 128, 128)

    for t in range(8):
        span = (t + 1) * 128
        q = two_heads(part_of(t, t + 1, 0).astype(F32) * 0.125).astype(BF)
        keys = part_of(0, t + 1, 1)
        vals = part_of(0, t + 1, 2)
        pos = row + t * 128
        begin = jnp.zeros((128, 128), jnp.int32)
        end = jnp.zeros((1, 128), jnp.int32)
        for g in range(4):
            length = lens[g : g + 1, :]
            end = end + length
            begin = begin + jnp.where(end <= pos, length, 0)
        allowed = []
        for u in range(t + 1):
            ok = begin <= lane + u * 128
            if u == t:
                ok = ok & (lane <= row)
            allowed.append(ok)
        allowed = jnp.concatenate(allowed, axis=1)
        scores = dot_right(q, keys)
        sums = []
        raws = []
        for h in range(2):
            sc = jnp.where(allowed, scores[h * 128 : (h + 1) * 128], -1e30)
            top = jnp.max(sc, axis=-1, keepdims=True)
            expo = jnp.exp(sc - top)
            low = expo.astype(BF)
            probs[t, h * 128 : (h + 1) * 128, 0:span] = low
            sums.append(jnp.sum(low.astype(F32), axis=-1, keepdims=True))
        raw = dot_nn(probs[t, :, 0:span], vals)
        both = jnp.where(first, sums[0], sums[1])
        attended = one_of_two(raw) / both
        tot[t] = both
        att_f[t] = attended
        att[:, t] = attended.astype(BF).reshape(4, 32, 128)

    line_relay(gu_block(0), GU[0], 0)
    out_here()

    def project_out(i):
        m = peer(i)
        out = dot_nn(att[m].reshape(256, 128), wo[...].reshape(128, 1024))
        part_a[m] = out.astype(BF).reshape(4, 2, 32, 1024)

    rs_start(part_a, 0, project_out)
    ag_corner(cot, 1)
    line_relay(gu_block(0), GU[0], 1)
    line_relay(gu_block(1), GU[1], 0)
    rs_corner(part_a, 0)
    for i in (1, 2):
        ag_relay(cot, 1, i)
    line_relay(gu_block(1), GU[1], 1)
    line_relay(gu_block(2), GU[2], 0)
    res = own_l[...].reshape(128, 1024).astype(F32) + rs_sum(part_a, 0)
    resid[...] = res
    r_two = lax.rsqrt(jnp.mean(res * res, axis=-1, keepdims=True) + EPS)
    n_two[k, :, c] = (res * r_two).astype(BF).reshape(4, 32, 1024)
    ag_send(n_two, 2)
    ag_relay(cot, 1, 3)
    line_relay(gu_block(2), GU[2], 1)

    ag_corner(n_two, 2)
    line_relay(down_block, 2, 0)
    ag_relay(n_two, 2, 1)
    ag_relay(n_two, 2, 2)
    line_relay(down_block, 2, 1)

    def feed_forward(j, i):
        m = peer(i)
        lo, mid, hi = 256 * j, 256 * j + 128, 256 * j + 256
        gu = dot_nn(n_two[m].reshape(256, 1024), wgu[:, :, :, :, lo:hi].reshape(1024, 256))
        gate = gu[:, :128]
        up = gu[:, 128:]
        sig = jax.nn.sigmoid(gate)
        active = gate * sig
        hid[m, :, 128 * j : 128 * j + 128] = (active * up).astype(BF)
        slope[m, :, lo:mid] = up * sig * (1.0 + gate * (1.0 - sig))
        slope[m, :, mid:hi] = active

    def down_grad(j):
        left = hid[:, :, 128 * j : 128 * j + 128].reshape(1024, 128)

        dwd[j] = dot_left(left, cot[...].reshape(1024, 1024)).astype(BF).reshape(4, 32, 1024)
        line_grads(dwd_block(j), zd.at[j], xd.at[j], 2 + j, True)

    line_here(gu_block(0), GU[0])

    @pl.loop(0, 3)
    def _(i):
        ag_other(n_two, 2, i)
        feed_forward(0, i)

    ag_relay(n_two, 2, 3)
    ag_other(n_two, 2, 3)
    feed_forward(0, 3)
    for i in range(4):
        ag_other(cot, 1, i)
    down_grad(0)
    line_here(gu_block(1), GU[1])

    @pl.loop(0, 4)
    def _(i):
        feed_forward(1, i)

    down_grad(1)
    line_here(gu_block(2), GU[2])

    @pl.loop(0, 4)
    def _(i):
        feed_forward(2, i)

    down_grad(2)
    line_here(down_block, 2)
    own_down.wait()

    def feed_back(i):
        m = peer(i)
        g_hid = dot_right(cot[m].reshape(256, 1024), wd[...].reshape(384, 1024))
        for j in range(6):
            cols = slice(128 * j, 128 * j + 128)
            part = g_hid[:, 128 * (j // 2) : 128 * (j // 2) + 128]
            ggu[m, :, cols] = (part * slope[m, :, cols]).astype(BF)
        out = dot_right(ggu[m], wgu[...].reshape(1024, 768))
        part_b[m] = out.astype(BF).reshape(4, 2, 32, 1024)

    def down_relay(j):
        for i in range(2):
            line_grads_relay(dwd_block(j), zd.at[j], xd.at[j], 2 + j, i)

    rs_start(part_b, 1, feed_back)
    down_relay(0)

    def units_grad(d):
        cols = pl.ds(pl.multiple_of(d * 256, 256), 256)
        left = n_two[:, :, :, :, cols].reshape(1024, 256)
        out = dot_left(left, ggu[...].reshape(1024, 768))
        dwgu[d] = out.astype(BF).reshape(4, 2, 32, 768)

    @pl.loop(0, 2)
    def _(d):
        units_grad(d)

    line_adds(*units_line(0), True)
    rs_corner(part_b, 1)
    down_relay(1)

    @pl.loop(2, 4)
    def _(d):
        units_grad(d)

    line_adds(*units_line(1), True)
    for j in range(2):
        line_near(*units_line(j), True)
    down_relay(2)

    @pl.loop(0, 4)
    def _(i):
        m = peer(i)
        out = dot_nn(hid[m], wd[...].reshape(384, 1024))
        part_c[m] = out.astype(BF).reshape(4, 2, 32, 1024)
        rs_copy(part_c, 2, i).start()

    scaled = rs_sum(part_b, 1)
    res = resid[...]
    r_two = lax.rsqrt(jnp.mean(res * res, axis=-1, keepdims=True) + EPS)
    normed = res * r_two
    inner = jnp.mean(scaled * normed, axis=-1, keepdims=True)
    g_res = cot[k, :, c].reshape(128, 1024).astype(F32) + r_two * (scaled - normed * inner)
    gres[...] = g_res
    gbr[k, :, c] = g_res.astype(BF).reshape(4, 32, 1024)
    ag_send(gbr, 3)

    ag_corner(gbr, 3)
    ag_relay(gbr, 3, 1)
    ag_relay(gbr, 3, 2)
    line_grads_relay(*units_line(0), 0)

    def attended_grad(i):
        ag_other(gbr, 3, i)
        m = peer(i)
        out = dot_right(gbr[m].reshape(256, 1024), wo[...].reshape(128, 1024))
        gatt[:, m] = out.astype(BF).reshape(8, 32, 128)

    @pl.loop(0, 3)
    def _(i):
        attended_grad(i)

    ag_relay(gbr, 3, 3)
    for i in (3, 1, 2):
        rs_halves(part_c, 2, i)
    line_grads_relay(*units_line(0), 1)
    attended_grad(3)
    line_grads_relay(*units_line(1), 0)

    for t in range(8):
        span = (t + 1) * 128
        keys = part_of(0, t + 1, 1)
        vals = part_of(0, t + 1, 2)
        ratio = gatt[t].reshape(128, 128).astype(F32) / tot[t]
        g_raw = two_heads(ratio.astype(BF).astype(F32)).astype(BF)
        graw_two[t] = g_raw
        q_two[t] = two_heads(part_of(t, t + 1, 0).astype(F32)).astype(BF)
        prod = ratio * att_f[t]
        g_tot = -jnp.sum(two_heads(prod), axis=-1, keepdims=True)
        g_pr = dot_right(g_raw, vals)
        g_sc = probs[t, :, 0:span].astype(F32) * (g_pr + g_tot)
        gsc[t, :, 0:span] = g_sc.astype(BF)
        g_q = one_of_two(dot_nn(gsc[t, :, 0:span], keys)) * 0.125
        gqkv[:, t, :, 0:128] = g_q.astype(BF).reshape(4, 32, 128)
    @pl.loop(0, 4)
    def _(n):
        cols = pl.ds(pl.multiple_of(n * 256, 256), 256)
        right = gbr[:, :, :, :, cols].reshape(1024, 256)
        out = dot_left(att[...].reshape(1024, 128), right)
        dwo[:, :, cols] = out.astype(BF).reshape(4, 32, 256)

    line_grads_relay(*units_line(1), 1)
    rs_corner(part_c, 2)
    for u in range(8):
        cols = slice(u * 128, (u + 1) * 128)
        rows = (8 - u) * 256
        g_k = dot_left(gsc[u:, :, cols].reshape(rows, 128), q_two[u:].reshape(rows, 128)) * 0.125
        g_v = dot_left(probs[u:, :, cols].reshape(rows, 128), graw_two[u:].reshape(rows, 128))
        gqkv[:, u, :, 128:256] = g_k.astype(BF).reshape(4, 32, 128)
        gqkv[:, u, :, 256:384] = g_v.astype(BF).reshape(4, 32, 128)

    rs_end(part_a, 0)

    def heads_back(i):
        m = peer(i)
        out = dot_right(gqkv[m].reshape(256, 384), wqkv[...].reshape(1024, 384))
        part_a[m] = out.astype(BF).reshape(4, 2, 32, 1024)

    rs_start(part_a, 3, heads_back)

    @pl.loop(0, 4)
    def _(d):
        cols = pl.ds(pl.multiple_of(d * 256, 256), 256)
        left = n_one[:, :, :, :, cols].reshape(1024, 256)
        out = dot_left(left, gqkv[...].reshape(1024, 384))
        dwqkv[d] = out.astype(BF).reshape(4, 2, 32, 384)

    line_adds(dwqkv_block, zq, xq, 0, True)
    out_grads_add(True)
    out_grads_near(True)
    rs_corner(part_a, 3)


    out_f = resid[...] + rs_sum(part_c, 2)
    back[0] = out_f.astype(BF).reshape(4, 32, 1024)
    gather_back(0, lat_o, True)
    line_near(dwqkv_block, zq, xq, 0, True)

    def plane_grads(land, dst, which, start):
        for i in range(4):
            m = peer(i)
            for same in (True, False):
                cc = c if same else oc
                src = land.at[z, m, cc]
                place = dst.at[rank]
                if i == 0 and same:
                    if start:
                        pltpu.make_async_copy(src, place, ga_r.at[which, rank]).start()
                else:
                    copy = remote(
                        src,
                        place,
                        ga_s.at[which, 2 * i + (0 if same else 1)],
                        ga_r.at[which, rank],
                        dev(m, z, cc),
                    )
                    if start:
                        copy.start()
                    else:
                        copy.wait_send()

    line_grads_relay(dwqkv_block, zq, xq, 0, 0)
    line_grads_relay(dwqkv_block, zq, xq, 0, 1)
    scaled = rs_sum(part_a, 3)
    lat_f = own_l[...].reshape(128, 1024).astype(F32)
    r_one = lax.rsqrt(jnp.mean(lat_f * lat_f, axis=-1, keepdims=True) + EPS)
    normed = lat_f * r_one
    inner = jnp.mean(scaled * normed, axis=-1, keepdims=True)
    d_lat = gres[...] + r_one * (scaled - normed * inner)
    back[1] = d_lat.astype(BF).reshape(4, 32, 1024)
    gather_back(1, dlat_o, True)
    out_grads_relay(True)
    for j in range(2):
        grad, land, _, which = units_line(j)
        land[z] = line_sum(grad, land, which).astype(BF)
    plane_grads(zgu, ggu_o, 1, True)

    for j in range(3):
        down_sum[32 * j : 32 * j + 32] = line_sum(dwd_block(j), zd.at[j], 2 + j)
    down_out = pltpu.make_async_copy(down_sum.at[pl.ds(0, 88)], gd_o, gd_r)
    down_out.start()
    zq[z] = line_sum(dwqkv_block, zq, 0).astype(BF)
    plane_grads(zq, gqkv_o, 0, True)
    out_grads_home(True)

    for which, dst in ((0, lat_o), (1, dlat_o)):
        for b in range(4):
            wait_for(dst.at[pl.ds(32 * b, 32)], tb_r.at[which, b])
    wait_for(go_o, go_r)
    for which, dst in ((1, ggu_o), (0, gqkv_o)):
        for r in range(RANKS):
            wait_for(dst.at[r], ga_r.at[which, r])
    spread(lat_in, lat_place, 0, False)
    spread_on(lat_in, lat_place, 0, False)
    spread(dout_in, cot_place, 1, False)
    spread_on(dout_in, cot_place, 1, False)
    spread_lens(False)
    plane_weights(wqkv_in, wqkv, 0, False)
    plane_weights(wgu_in, wgu, 1, False)
    line_sent(qkv_block, 0)
    for j in range(3):
        line_sent(gu_block(j), GU[j])
    line_sent(down_block, 2, wd_in)
    down_out.wait()
    out_across(False)
    out_along(False)
    out_relay(False)
    for which, buf in enumerate((n_one, cot, n_two, gbr)):
        ag_end(buf, which)
    rs_end(part_b, 1)
    rs_end(part_c, 2)
    rs_end(part_a, 3)
    for j in range(2):
        line_grads(*units_line(j), False)
    line_grads(dwqkv_block, zq, xq, 0, False)
    for j in range(3):
        line_grads(dwd_block(j), zd.at[j], xd.at[j], 2 + j, False)
    plane_grads(zgu, ggu_o, 1, False)
    plane_grads(zq, gqkv_o, 0, False)
    out_grads_add(False)
    out_grads_near(False)
    out_grads_relay(False)
    out_grads_home(False)
    gather_back(0, lat_o, False)
    gather_back(1, dlat_o, False)


def run_layer(lat, dout, lengths, gain_one, gain_two, weights):
    vm = pltpu.VMEM
    dma = pltpu.SemaphoreType.DMA
    rows = (4, 4, 2, 32)
    return pl.pallas_call(
        layer_kernel,
        out_shape=(
            jax.ShapeDtypeStruct((128, 1024), BF),
            jax.ShapeDtypeStruct((128, 1024), BF),
            jax.ShapeDtypeStruct((RANKS, 32, 384), BF),
            jax.ShapeDtypeStruct((RANKS, 32, 768), BF),
            jax.ShapeDtypeStruct((88, 1024), F32),
            jax.ShapeDtypeStruct((32, 1024), BF),
        ),
        in_specs=[pl.BlockSpec(memory_space=pl.ANY)] * 2
        + [pl.BlockSpec(memory_space=pltpu.SMEM)]
        + [pl.BlockSpec(memory_space=pl.ANY)] * 9,
        out_specs=[pl.BlockSpec(memory_space=pl.ANY)] * 6,
        scratch_shapes=[
            vm((1, 32), BF),
            vm((1, 32), BF),
            vm((32, 1024), BF),
            vm((32, 1024), BF),
            vm((32, 1024), BF),
            vm((32, 2816), BF),
            vm((32, 2816), BF),
            vm((88, 1024), BF),
            dma((8,)),
            vm((8, 128), jnp.int32),
            vm((RANKS, 32, 384), BF),
            vm((RANKS, 32, 768), BF),
            vm((3, 32, 1024), BF),
            vm((4, 32, 1024), BF),
            vm((2, 4, 32, 1024), BF),
            vm((8, 128), jnp.int32),
            vm(rows + (1024,), BF),
            vm(rows + (1024,), BF),
            vm(rows + (1024,), BF),
            vm(rows + (1024,), BF),
            vm(rows + (384,), BF),
            vm(rows + (768,), BF),
            vm((3, 4, 32, 1024), BF),
            vm((4, 32, 1024), BF),
            vm((8, 4, 32, 384), BF),
            vm((4, 8, 32, 128), BF),
            vm((8, 128, 128), F32),
            vm((8, 128, 128), F32),
            vm((8, 256, 1024), BF),
            vm((8, 256, 1024), BF),
            vm(rows + (1024,), BF),
            vm(rows + (1024,), BF),
            vm(rows + (1024,), BF),
            vm((4, 4, 4, 32, 1024), BF),
            vm((4, 2, 4, 32, 1024), BF),
            vm((4, 2, 2, 32, 1024), BF),
            vm((4, 256, 384), BF),
            vm((4, 256, 768), BF),
            vm((4, 256, 768), F32),
            vm((8, 4, 32, 128), BF),
            vm((8, 256, 128), BF),
            vm((8, 256, 128), BF),
            vm((4, 8, 32, 384), BF),
            vm(rows + (384,), BF),
            vm(rows + (768,), BF),
            vm((3, 4, 32, 1024), BF),
            vm((4, 32, 1024), BF),
            vm((4, 4, 2, 32, 384), BF),
            vm((4, 4, 2, 32, 768), BF),
            vm((3, 4, 32, 1024), BF),
            vm((2, 2, 32, 1024), BF),
            vm((4, 32, 1024), BF),
            vm((2, 4, 2, 32, 384), BF),
            vm((2, 4, 2, 32, 768), BF),
            vm((3, 2, 32, 1024), BF),
            vm((96, 1024), F32),
            vm((128, 1024), F32),
            vm((128, 1024), F32),
            vm((2, 4, 32, 1024), BF),
            dma((2, 4)),
            dma((2, 4)),
            dma((2, 4)),
            dma((2, 4)),
            dma,
            dma,
            dma((2, 8)),
            dma((2, 8)),
            dma((6, 4)),
            dma((6, 4)),
            dma,
            dma((1,)),
            dma((2,)),
            dma((4, 12)),
            dma((4, 4, 2)),
            dma((4, 4)),
            dma((4, 2)),
            dma((4, 12)),
            dma((4, 4)),
            dma((4, 2, 2)),
            dma((4, 2)),
            dma((6, 4)),
            dma((6, 4)),
            dma((6, 2)),
            dma((2, 8)),
            dma((2, 8)),
            dma,
            dma((2,)),
            dma,
            dma,
            dma((2,)),
            dma((2, 4)),
            dma((2, 4)),
        ],
        compiler_params=pltpu.CompilerParams(
            collective_id=0, has_side_effects=True, vmem_limit_bytes=60 * 1024 * 1024
        ),
    )(lat, dout, lengths, gain_one, gain_two, *weights)


def finish_kernel(
    lat,
    dlat,
    gqkv_in,
    ggu_in,
    gd,
    go_in,
    gain_one,
    gain_two,
    wq,
    wk,
    wv,
    wg,
    wu,
    lat_o,
    dlat_o,
    g_one_o,
    gq_o,
    gk_o,
    gv_o,
    go_o,
    g_two_o,
    gg_o,
    gu_o,
    gd_o,
    gqkv,
    ggu,
    go,
    lat_v,
    dlat_v,
    gd_v,
    g_one_v,
    gq_v,
    gk_v,
    gv_v,
    go_v,
    g_two_v,
    gg_v,
    gu_v,
    sems,
    out_sems,
):
    moves = ((gqkv_in, gqkv), (ggu_in, ggu), (go_in, go), (lat, lat_v), (dlat, dlat_v), (gd, gd_v))
    copies = [pltpu.make_async_copy(src, dst, sems.at[i]) for i, (src, dst) in enumerate(moves)]
    for copy in copies:
        copy.start()
    leaving = []

    def leave(src, dst):
        copy = pltpu.make_async_copy(src, dst, out_sems.at[len(leaving)])
        copy.start()
        leaving.append(copy)

    col_one = jnp.sum(on_diagonal(gain_one[...]), axis=1, keepdims=True)
    col_two = jnp.sum(on_diagonal(gain_two[...]), axis=1, keepdims=True)

    def as_row(acc):
        return jnp.sum(on_diagonal(jnp.sum(acc, axis=1, keepdims=True)), axis=0, keepdims=True)

    for copy, src, dst in ((copies[3], lat_v, lat_o.at[0]), (copies[4], dlat_v, dlat_o.at[0]), (copies[5], gd_v, gd_o)):
        copy.wait()
        leave(src, dst)
    copies[0].wait()
    acc = jnp.zeros((32, 128), F32)
    for i, (w, out) in enumerate(((wq, gq_v), (wk, gk_v), (wv, gv_v))):
        for r in range(RANKS):
            cols = slice(r * 128, (r + 1) * 128)
            part = gqkv[r, :, i * 128 : (i + 1) * 128].astype(F32)
            out[:, cols] = part * col_one
            acc = acc + part * w[:, cols].astype(F32)
        leave(out, (gq_o, gk_o, gv_o)[i])
    g_one_v[...] = as_row(acc)
    leave(g_one_v, g_one_o)
    copies[1].wait()
    acc = jnp.zeros((32, 256), F32)
    for i, (w, out) in enumerate(((wg, gg_v), (wu, gu_v))):
        parts = [None] * 96
        for r in range(RANKS):
            for j in range(3):
                third = ggu[r, :, 256 * j + 128 * i : 256 * j + 128 * i + 128].astype(F32)
                for b, unit in enumerate(units_of(r)):
                    parts[3 * unit + j] = third[:, 32 * b : 32 * b + (24 if j == 2 else 32)]
        rows = jnp.concatenate(parts, axis=1)
        out[...] = rows * col_two
        leave(out, (gg_o, gu_o)[i])
        prod = rows * w[...].astype(F32)
        for n in range(11):
            acc = acc + prod[:, n * 256 : (n + 1) * 256]
    g_two_v[...] = as_row(acc)
    leave(g_two_v, g_two_o)
    copies[2].wait()
    go_v[...] = go[...].astype(F32)
    leave(go_v, go_o)
    for copy in leaving:
        copy.wait()


def finish(*arrays):
    outs = (
        ((1, 128, 1024), BF),
        ((1, 128, 1024), BF),
        ((1, 32), F32),
        ((32, 1024), F32),
        ((32, 1024), F32),
        ((32, 1024), F32),
        ((32, 1024), F32),
        ((1, 32), F32),
        ((32, 2816), F32),
        ((32, 2816), F32),
        ((88, 1024), F32),
    )
    hbm = pl.BlockSpec(memory_space=pltpu.HBM)
    vmem = pl.BlockSpec(memory_space=pltpu.VMEM)
    return pl.pallas_call(
        finish_kernel,
        out_shape=tuple(jax.ShapeDtypeStruct(*o) for o in outs),
        in_specs=[hbm] * 6 + [vmem] * 7,
        out_specs=[pl.BlockSpec(memory_space=pl.ANY)] * len(outs),
        scratch_shapes=[
            pltpu.VMEM((RANKS, 32, 384), BF),
            pltpu.VMEM((RANKS, 32, 768), BF),
            pltpu.VMEM((32, 1024), BF),
            pltpu.VMEM((128, 1024), BF),
            pltpu.VMEM((128, 1024), BF),
            pltpu.VMEM((88, 1024), F32),
            pltpu.VMEM((1, 32), F32),
            pltpu.VMEM((32, 1024), F32),
            pltpu.VMEM((32, 1024), F32),
            pltpu.VMEM((32, 1024), F32),
            pltpu.VMEM((32, 1024), F32),
            pltpu.VMEM((1, 32), F32),
            pltpu.VMEM((32, 2816), F32),
            pltpu.VMEM((32, 2816), F32),
            pltpu.SemaphoreType.DMA((6,)),
            pltpu.SemaphoreType.DMA((11,)),
        ],
        compiler_params=pltpu.CompilerParams(vmem_limit_bytes=60 * 1024 * 1024),
    )(*arrays)


def plane_device(
    latents,
    d_out,
    lengths,
    gain_attn,
    w_query,
    w_key,
    w_value,
    w_out,
    gain_ffn,
    w_gate,
    w_up,
    w_down,
):
    gains = gain_attn.reshape(1, 32), gain_ffn.reshape(1, 32)
    weights = w_query, w_key, w_value, w_gate, w_up, w_down, w_out
    parts = run_layer(latents[0], d_out[0], lengths, *gains, weights)
    outs = finish(*parts, *gains, w_query, w_key, w_value, w_gate, w_up)
    return tuple(o.reshape(32) if o.shape == (1, 32) else o for o in outs)


def solution(mesh):
    return jax.shard_map(
        plane_device if planes_fit(mesh) else per_device,
        mesh=mesh,
        in_specs=(
            P("dp", "seq", None),
            P("dp", "seq", None),
            P("dp", None),
            P(("dp", "seq")),
            P(("dp", "seq"), None),
            P(("dp", "seq"), None),
            P(("dp", "seq"), None),
            P(("dp", "seq"), None),
            P(("dp", "seq")),
            P(("dp", "seq"), None),
            P(("dp", "seq"), None),
            P(("dp", "seq"), None),
        ),
        out_specs=(
            P("dp", "seq", None),
            P("dp", "seq", None),
            P(("dp", "seq")),
            P(("dp", "seq"), None),
            P(("dp", "seq"), None),
            P(("dp", "seq"), None),
            P(("dp", "seq"), None),
            P(("dp", "seq")),
            P(("dp", "seq"), None),
            P(("dp", "seq"), None),
            P(("dp", "seq"), None),
        ),
        check_vma=False,
    )
```

```python
import functools
import math

import jax
import jax.numpy as jnp
from jax import lax
from jax.experimental import pallas as pl
from jax.experimental.pallas import tpu as pltpu
from jax.sharding import PartitionSpec as P

HEADS = 16


EPS = 1e-05


def norm_rows(values, gain_vec):
    factor = lax.rsqrt(jnp.mean(values * values, axis=-1, keepdims=True) + EPS)
    normed = values * factor
    return (normed * gain_vec, normed, factor)


def norm_back(grad_out, normed, factor, gain_vec):
    scaled = grad_out * gain_vec
    inner = jnp.mean(scaled * normed, axis=-1, keepdims=True)
    return (factor * (scaled - normed * inner), jnp.sum(grad_out * normed, axis=0))


def dot_left(left, right):
    return lax.dot_general(
        left, right, (((0,), (0,)), ((), ())), preferred_element_type=jnp.float32
    )


def dot_right(left, right):
    return lax.dot_general(
        left, right, (((1,), (1,)), ((), ())), preferred_element_type=jnp.float32
    )


def per_device(
    latents,
    d_out,
    lengths,
    gain_attn,
    w_query,
    w_key,
    w_value,
    w_out,
    gain_ffn,
    w_gate,
    w_up,
    w_down,
):
    g_attn, full_query, full_key, full_value, full_out, g_ffn, full_gate, full_up, full_down = (
        lax.all_gather(gain_attn, ("dp", "seq"), axis=0, tiled=True),
        lax.all_gather(w_query, ("dp", "seq"), axis=0, tiled=True),
        lax.all_gather(w_key, ("dp", "seq"), axis=0, tiled=True),
        lax.all_gather(w_value, ("dp", "seq"), axis=0, tiled=True),
        lax.all_gather(w_out, ("dp", "seq"), axis=0, tiled=True),
        lax.all_gather(gain_ffn, ("dp", "seq"), axis=0, tiled=True),
        lax.all_gather(w_gate, ("dp", "seq"), axis=0, tiled=True),
        lax.all_gather(w_up, ("dp", "seq"), axis=0, tiled=True),
        lax.all_gather(w_down, ("dp", "seq"), axis=0, tiled=True),
    )
    gain_one = g_attn.astype(jnp.float32)
    gain_two = g_ffn.astype(jnp.float32)
    inputs_f = latents[0].astype(jnp.float32)
    row_count, model_width = inputs_f.shape
    head_size = model_width // HEADS
    group_rows = row_count * lax.axis_size("seq")
    here = lax.axis_index("seq") * row_count + jnp.arange(row_count, dtype=jnp.int32)
    seq_lens = lengths[0]
    seq_ends = jnp.cumsum(seq_lens, dtype=jnp.int32)
    begins = jnp.sum(
        jnp.where(seq_ends[None, :] <= here[:, None], seq_lens[None, :], 0), axis=1, dtype=jnp.int32
    )
    key_block = math.gcd(group_rows, 1024)
    block_count = group_rows // key_block
    key_positions = jnp.arange(group_rows, dtype=jnp.int32).reshape(block_count, key_block)
    h_one_f, normed_one, factor_one = norm_rows(inputs_f, gain_one)
    h_one = h_one_f.astype(jnp.bfloat16)
    query_proj = jnp.dot(h_one, full_query, preferred_element_type=jnp.float32).astype(jnp.bfloat16)
    key_proj = jnp.dot(h_one, full_key, preferred_element_type=jnp.float32).astype(jnp.bfloat16)
    value_proj = jnp.dot(h_one, full_value, preferred_element_type=jnp.float32).astype(jnp.bfloat16)
    keys_all, values_all = (
        lax.all_gather(key_proj, "seq", axis=0, tiled=True),
        lax.all_gather(value_proj, "seq", axis=0, tiled=True),
    )
    query_heads = query_proj.reshape(row_count, HEADS, head_size)

    def split_blocks(array):
        return array.reshape(block_count, key_block, HEADS, head_size)

    def block_scores(key_piece, pos_piece):
        scores = (
            jnp.einsum("qhd,khd->hqk", query_heads, key_piece, preferred_element_type=jnp.float32)
            * 0.125
        )
        allowed = (pos_piece[None, :] <= here[:, None]) & (pos_piece[None, :] >= begins[:, None])
        return (scores, allowed[None])

    def max_step(running, pieces):
        key_piece, pos_piece = pieces
        scores, allowed = block_scores(key_piece, pos_piece)
        return (jnp.maximum(running, jnp.max(jnp.where(allowed, scores, -1e30), axis=-1)), None)

    row_max, _ = lax.scan(
        max_step,
        jnp.full((HEADS, row_count), -1e30, jnp.float32),
        (split_blocks(keys_all), key_positions),
    )

    def sum_step(running, pieces):
        key_piece, value_piece, pos_piece = pieces
        scores, allowed = block_scores(key_piece, pos_piece)
        expon = jnp.where(
            allowed, jnp.exp(jnp.where(allowed, scores, -1e30) - row_max[:, :, None]), 0.0
        )
        rounded = expon.astype(jnp.bfloat16)
        total_sum, raw_sum = running
        total_sum = total_sum + jnp.sum(rounded.astype(jnp.float32), axis=-1)
        raw_sum = raw_sum + jnp.einsum(
            "hqk,khd->qhd", rounded, value_piece, preferred_element_type=jnp.float32
        )
        return ((total_sum, raw_sum), None)

    (total_sum, raw_sum), _ = lax.scan(
        sum_step,
        (
            jnp.zeros((HEADS, row_count), jnp.float32),
            jnp.zeros((row_count, HEADS, head_size), jnp.float32),
        ),
        (split_blocks(keys_all), split_blocks(values_all), key_positions),
    )
    totals_rows = jnp.transpose(total_sum)
    attended = raw_sum / totals_rows[:, :, None]
    attended_low = attended.reshape(row_count, model_width).astype(jnp.bfloat16)
    resid = inputs_f + jnp.dot(attended_low, full_out, preferred_element_type=jnp.float32)
    h_two_f, normed_two, factor_two = norm_rows(resid, gain_two)
    h_two = h_two_f.astype(jnp.bfloat16)
    gate_proj = jnp.dot(h_two, full_gate, preferred_element_type=jnp.float32)
    up_proj = jnp.dot(h_two, full_up, preferred_element_type=jnp.float32)
    gate_sigmoid = jax.nn.sigmoid(gate_proj)
    gate_active = gate_proj * gate_sigmoid
    hidden = (gate_active * up_proj).astype(jnp.bfloat16)
    outputs = resid + jnp.dot(hidden, full_down, preferred_element_type=jnp.float32)
    latents_out = outputs.astype(jnp.bfloat16)[None]
    grad_out = d_out[0]
    grad_down = dot_left(hidden, grad_out)
    g_hidden = dot_right(grad_out, full_down)
    g_gate = (g_hidden * up_proj * gate_sigmoid * (1.0 + gate_proj * (1.0 - gate_sigmoid))).astype(
        jnp.bfloat16
    )
    g_up = (g_hidden * gate_active).astype(jnp.bfloat16)
    grad_gate = dot_left(h_two, g_gate)
    grad_up = dot_left(h_two, g_up)
    g_h_two = dot_right(g_gate, full_gate) + dot_right(g_up, full_up)
    g_norm_two, grad_gain_two = norm_back(g_h_two, normed_two, factor_two, gain_two)
    g_resid = grad_out.astype(jnp.float32) + g_norm_two
    g_branch = g_resid.astype(jnp.bfloat16)
    grad_out_proj = dot_left(attended_low, g_branch)
    g_att = dot_right(g_branch, full_out).reshape(row_count, HEADS, head_size).astype(jnp.bfloat16)
    g_att_f = g_att.astype(jnp.float32)
    g_raw = (g_att_f / totals_rows[:, :, None]).astype(jnp.bfloat16)
    g_total = jnp.transpose(-jnp.sum(g_att_f * raw_sum, axis=-1) / (totals_rows * totals_rows))
    keys_back, values_back = (
        lax.all_gather(key_proj, "seq", axis=0, tiled=True),
        lax.all_gather(value_proj, "seq", axis=0, tiled=True),
    )

    def score_grads(key_piece, value_piece, pos_piece):
        scores, allowed = block_scores(key_piece, pos_piece)
        expon = jnp.where(
            allowed, jnp.exp(jnp.where(allowed, scores, -1e30) - row_max[:, :, None]), 0.0
        )
        g_probs = jnp.einsum("qhd,khd->hqk", g_raw, value_piece, preferred_element_type=jnp.float32)
        g_scores = (expon * (g_probs + g_total[:, :, None])).astype(jnp.bfloat16)
        return (expon, g_scores)

    def grad_step(running, pieces):
        key_piece, value_piece, pos_piece = pieces
        expon, g_scores = score_grads(key_piece, value_piece, pos_piece)
        rounded = expon.astype(jnp.bfloat16)
        running = (
            running
            + jnp.einsum("hqk,khd->qhd", g_scores, key_piece, preferred_element_type=jnp.float32)
            * 0.125
        )
        g_key_piece = (
            jnp.einsum("hqk,qhd->khd", g_scores, query_heads, preferred_element_type=jnp.float32)
            * 0.125
        )
        g_value_piece = jnp.einsum(
            "hqk,qhd->khd", rounded, g_raw, preferred_element_type=jnp.float32
        )
        return (running, (g_key_piece, g_value_piece))

    g_query_f, (g_keys, g_values) = lax.scan(
        grad_step,
        jnp.zeros((row_count, HEADS, head_size), jnp.float32),
        (split_blocks(keys_back), split_blocks(values_back), key_positions),
    )
    mine_key, mine_value = (
        lax.psum_scatter(
            g_keys.reshape(group_rows, model_width).astype(jnp.bfloat16),
            "seq",
            scatter_dimension=0,
            tiled=True,
        ).astype(jnp.float32),
        lax.psum_scatter(
            g_values.reshape(group_rows, model_width).astype(jnp.bfloat16),
            "seq",
            scatter_dimension=0,
            tiled=True,
        ).astype(jnp.float32),
    )
    g_key = mine_key.astype(jnp.bfloat16)
    g_value = mine_value.astype(jnp.bfloat16)
    g_query = g_query_f.reshape(row_count, model_width).astype(jnp.bfloat16)
    grad_query = dot_left(h_one, g_query)
    grad_key = dot_left(h_one, g_key)
    grad_value = dot_left(h_one, g_value)
    g_h_one = (
        dot_right(g_query, full_query) + dot_right(g_key, full_key) + dot_right(g_value, full_value)
    )
    g_norm_one, grad_gain_one = norm_back(g_h_one, normed_one, factor_one, gain_one)
    d_latents = (g_resid + g_norm_one).astype(jnp.bfloat16)[None]
    gain_pair = jnp.stack((grad_gain_one, grad_gain_two), axis=1)
    summed = (
        lax.psum_scatter(gain_pair, ("dp", "seq"), scatter_dimension=0, tiled=True),
        lax.psum_scatter(grad_query, ("dp", "seq"), scatter_dimension=0, tiled=True),
        lax.psum_scatter(grad_key, ("dp", "seq"), scatter_dimension=0, tiled=True),
        lax.psum_scatter(grad_value, ("dp", "seq"), scatter_dimension=0, tiled=True),
        lax.psum_scatter(grad_out_proj, ("dp", "seq"), scatter_dimension=0, tiled=True),
        lax.psum_scatter(grad_gate, ("dp", "seq"), scatter_dimension=0, tiled=True),
        lax.psum_scatter(grad_up, ("dp", "seq"), scatter_dimension=0, tiled=True),
        lax.psum_scatter(grad_down, ("dp", "seq"), scatter_dimension=0, tiled=True),
    )
    return (
        latents_out,
        d_latents,
        summed[0][:, 0],
        summed[1],
        summed[2],
        summed[3],
        summed[4],
        summed[0][:, 1],
        summed[5],
        summed[6],
        summed[7],
    )


MESH = pl.DeviceIdType.MESH
BF = jnp.bfloat16
F32 = jnp.float32
DP, ZS, CORES = 4, 4, 2
RANKS = DP * CORES
GU = (1, 3, 4)


def units_of(rank):
    return [8 * (rank // CORES) + CORES * b + rank % CORES for b in range(ZS)]


def planes_fit(mesh):
    return mesh.shape["dp"] == DP and mesh.shape["seq"] == ZS * CORES


def dot_nn(left, right):
    return jnp.dot(left, right, preferred_element_type=F32)


def remote(src, dst, send_sem, recv_sem, device):
    return pltpu.make_async_remote_copy(
        src_ref=src,
        dst_ref=dst,
        send_sem=send_sem,
        recv_sem=recv_sem,
        device_id=device,
        device_id_type=MESH,
    )


def wait_for(ref, sem):
    pltpu.make_async_copy(ref, ref, sem).wait()


def on_diagonal(row):
    at = lax.broadcasted_iota(jnp.int32, (32, 32), 0) == lax.broadcasted_iota(jnp.int32, (32, 32), 1)
    return jnp.where(at, row.astype(F32), 0.0)


def layer_kernel(
    lat_in,
    dout_in,
    lengths_in,
    gain_one_in,
    gain_two_in,
    wq_in,
    wk_in,
    wv_in,
    wg_in,
    wu_in,
    wd_rows_in,
    wo_in,
    lat_o,
    dlat_o,
    gqkv_o,
    ggu_o,
    gd_o,
    go_o,
    gain_one,
    gain_two,
    wq_raw,
    wk_raw,
    wv_raw,
    wg_raw,
    wu_raw,
    wd_raw,
    in_r,
    lens_in,
    wqkv_in,
    wgu_in,
    wd_in,
    own_l,
    stop,
    lens,
    n_one,
    n_two,
    cot,
    gbr,
    wqkv,
    wgu,
    wd,
    wo,
    qkv,
    att,
    att_f,
    tot,
    probs,
    gsc,
    part_a,
    part_b,
    part_c,
    sib,
    rcv,
    turn,
    hid,
    ggu,
    slope,
    gatt,
    graw_two,
    q_two,
    gqkv,
    dwqkv,
    dwgu,
    dwd,
    dwo,
    zq,
    zgu,
    zd,
    zo,
    xo,
    xq,
    xgu,
    xd,
    down_sum,
    resid,
    gres,
    back,
    tr_s,
    tr_r,
    tx_r,
    tz_s,
    ln_s,
    ln_r,
    wa_s,
    wa_r,
    wz_s,
    wz_r,
    wd_r,
    wo_s,
    wo_r,
    ag_s,
    ag_r,
    ag_x,
    ag_d,
    rs_s,
    rs_r,
    rs_x,
    rs_d,
    gz_s,
    gz_r,
    gx_r,
    ga_s,
    ga_r,
    gd_r,
    go_s,
    go_r,
    go_x,
    go_z,
    tb_s,
    tb_r,
):
    k = lax.axis_index("dp")
    s = lax.axis_index("seq")
    z = s // CORES
    c = s % CORES
    oc = 1 - c
    rank = CORES * k + c

    def dev(kk, zz, cc):
        return (kk, CORES * zz + cc)

    def peer(i):
        return 2 * ((k // 2 + i // 2) % 2) + (k % 2 + i % 2) % 2

    def zpeer(i):
        return (z + i) % ZS

    sibling = dev(k, z, oc)

    loads = (
        (gain_one_in, gain_one),
        (gain_two_in, gain_two),
        (wq_in, wq_raw),
        (wk_in, wk_raw),
        (wv_in, wv_raw),
        (wd_rows_in, wd_raw),
        (wg_in, wg_raw),
        (wu_in, wu_raw),
    )
    loads = [pltpu.make_async_copy(src, dst, in_r.at[i]) for i, (src, dst) in enumerate(loads)]
    for load in loads:
        load.start()

    barrier = pltpu.get_barrier_semaphore()
    greeted = 0
    for di in range(4):
        for dz in range(4):
            if di or dz:
                pl.semaphore_signal(
                    barrier, inc=1, device_id=dev(peer(di), zpeer(dz), c), device_id_type=MESH
                )
                greeted += 1
            if di == 0 or dz == 0:
                pl.semaphore_signal(
                    barrier, inc=1, device_id=dev(peer(di), zpeer(dz), oc), device_id_type=MESH
                )
                greeted += 1

    def scaled_rows(w, gain):
        return dot_nn(on_diagonal(gain[...]).astype(BF), w[...])

    def units_to_ranks():
        both = [scaled_rows(w, gain_two) for w in (wg_raw, wu_raw)]
        gap = jnp.zeros((32, 8), F32)
        for r in range(RANKS):
            for j in range(3):
                for i, rows in enumerate(both):
                    parts = []
                    for unit in units_of(r):
                        at = 88 * unit + 32 * j
                        parts += [rows[:, at : at + 32]] if j < 2 else [rows[:, at : at + 24], gap]
                    lo = 256 * j + 128 * i
                    wgu_in[r, :, lo : lo + 128] = jnp.concatenate(parts, axis=1).astype(BF)

    tile_row = lax.broadcasted_iota(jnp.int32, (8, 128), 0)
    tile = jnp.zeros((8, 128), jnp.int32)
    for i in range(4):
        tile = jnp.where(tile_row == i, lengths_in[0, i], tile)
    lens_in[...] = tile

    pl.semaphore_wait(barrier, greeted)

    def spread(src, final_of, which, start):
        for q in range(4):
            piece = src.at[pl.ds(32 * q, 32)]

            @pl.when((z == k) & (k == q))
            def _():
                if start:
                    pltpu.make_async_copy(piece, final_of(q, z), tr_r.at[which, z]).start()

            @pl.when((z == k) & (k != q))
            def _():
                copy = remote(
                    piece, final_of(q, z), tr_s.at[which, q], tr_r.at[which, z], dev(q, z, c)
                )
                if start:
                    copy.start()
                else:
                    copy.wait_send()

            @pl.when((z != k) & (k != q))
            def _():
                copy = remote(
                    piece, stop.at[which, k], tr_s.at[which, q], tx_r.at[which, k], dev(q, z, c)
                )
                if start:
                    copy.start()
                else:
                    copy.wait_send()

    def spread_on(src, final_of, which, start):
        for i in range(1, 4):
            g = zpeer(i)

            def send(piece):
                copy = remote(
                    piece, final_of(k, z), tz_s.at[which, i], tr_r.at[which, z], dev(k, g, c)
                )
                if start:
                    copy.start()
                else:
                    copy.wait_send()

            @pl.when(g == k)
            def _():
                send(src.at[pl.ds(pl.multiple_of(32 * k, 32), 32)])

            @pl.when(g != k)
            def _():
                if start:
                    wait_for(stop.at[which, g], tx_r.at[which, g])
                send(stop.at[which, g])

    def lat_place(q, b):
        return own_l.at[b]

    def cot_place(q, b):
        return cot.at[q, b, c]

    def spread_lens(start):
        here = z == k

        @pl.when(here)
        def _():
            if start:
                pltpu.make_async_copy(lens_in, lens, ln_r).start()

        @pl.when(jnp.logical_not(here))
        def _():
            copy = remote(lens_in, lens, ln_s, ln_r, dev(z, k, c))
            if start:
                copy.start()
            else:
                copy.wait_send()

    def plane_weights(src, dst, which, start):
        for i in range(4):
            for same in (True, False):
                cc = c if same else oc
                target = CORES * peer(i) + cc
                piece = src.at[target]
                place = dst.at[k, z, c]
                if i == 0 and same:
                    if start:
                        pltpu.make_async_copy(piece, place, wa_r.at[which, rank]).start()
                else:
                    copy = remote(
                        piece,
                        place,
                        wa_s.at[which, 2 * i + (0 if same else 1)],
                        wa_r.at[which, rank],
                        dev(peer(i), z, cc),
                    )
                    if start:
                        copy.start()
                    else:
                        copy.wait_send()

    def plane_weights_here(dst, which):
        for kk in range(4):
            for cc in range(2):
                wait_for(dst.at[kk, z, cc], wa_r.at[which, CORES * kk + cc])

    middle = (z == 1) | (z == 2)
    near = (1 + z % 2, 2 + z // 2 - 2 * (z % 2))
    z_end = 3 * (z // 2)

    def far_of(place):
        return (6 - 3 * place, 3 - place)

    far = far_of(z)

    def line_copy(block, which, slot, b, place, src=None):
        src = block(b) if src is None else src
        return remote(src, block(b), wz_s.at[which, slot], wz_r.at[which, b], dev(k, place, c))

    def line_send(block, which, from_ends, from_middle, start=True, src=None):
        def send(slots):
            for j in slots:
                copy = line_copy(block, which, j, z, near[j], src)
                if start:
                    copy.start()
                else:
                    copy.wait_send()

        if from_ends:

            @pl.when(jnp.logical_not(middle))
            def _():
                send(from_ends)

        if from_middle:

            @pl.when(middle)
            def _():
                send(from_middle)

    def line_relay(block, which, j):
        @pl.when(middle)
        def _():
            wait_for(block(far[j]), wz_r.at[which, far[j]])
            line_copy(block, which, 2 + j, far[j], z_end).start()

    def line_sent(block, which, src=None):
        line_send(block, which, (0, 1), (0, 1), False, src)

        @pl.when(middle)
        def _():
            for j in range(2):
                line_copy(block, which, 2 + j, far[j], z_end).wait_send()

    def line_here(block, which):
        @pl.when(middle)
        def _():
            wait_for(block(z_end), wz_r.at[which, z_end])

        @pl.when(jnp.logical_not(middle))
        def _():
            for i in range(1, 4):
                wait_for(block(zpeer(i)), wz_r.at[which, zpeer(i)])

    def qkv_block(b):
        return wqkv.at[:, b]

    def gu_block(j):
        return lambda b: wgu.at[:, b, :, :, 256 * j : 256 * j + 256]

    def down_block(b):
        return wd.at[:, b]

    side = z // 2

    def out_block(b):
        return wo.at[pl.ds(2 * (b % 2), 2)]

    def out_across(start):
        place = wo.at[2 * (z % 2) + c]

        @pl.when(c == side)
        def _():
            if start:
                pltpu.make_async_copy(wo_in, place, wo_r.at[c]).start()

        @pl.when(c != side)
        def _():
            copy = remote(wo_in, place, wo_s.at[0], wo_r.at[c], sibling)
            if start:
                copy.start()
            else:
                copy.wait_send()

    def out_along(start):
        @pl.when(c == side)
        def _():
            if start:
                for i in range(2):
                    wait_for(wo.at[2 * (z % 2) + i], wo_r.at[i])
            for j in (1, 0):
                copy = line_copy(out_block, 5, j, z, near[j])
                if start:
                    copy.start()
                else:
                    copy.wait_send()

    def out_relay(start):
        @pl.when(middle & (c != side))
        def _():
            for j in range(2):
                if start:
                    wait_for(out_block(far[j]), wz_r.at[5, far[j]])
                copy = line_copy(out_block, 5, 2 + j, far[j], z_end)
                if start:
                    copy.start()
                else:
                    copy.wait_send()

    def out_here():
        @pl.when(c == side)
        def _():
            other = 4 * side + 1 - z
            wait_for(out_block(other), wz_r.at[5, other])

        @pl.when((c != side) & jnp.logical_not(middle))
        def _():
            for j in range(2):
                wait_for(out_block(2 * c + j), wz_r.at[5, 2 * c + j])

    def half(j):
        return pl.ds(2 * j, 2)

    def ag_copy(buf, which, i, j):
        own = buf.at[k, half(j), c]
        return remote(
            own, own, ag_s.at[which, 2 * i + j], ag_r.at[which, k, j], dev(peer(i), z, c)
        )

    def ag_turn(buf, which, i):
        block = buf.at[peer(i), half(i - 1), c]
        return remote(
            block, block, ag_s.at[which, 9 + i], ag_d.at[which, i - 1], dev(peer(3 - i), z, c)
        )

    def ag_across(buf, which, i):
        block = buf.at[peer(i), :, c]
        return remote(
            block, block, ag_s.at[which, 6 + i], ag_x.at[which, peer(i)], sibling
        )

    def ag_send(buf, which):
        for i, j in ((1, 0), (2, 1), (1, 1), (2, 0)):
            ag_copy(buf, which, i, j).start()
        ag_across(buf, which, 0).start()

    def ag_corner(buf, which):
        for i in (1, 2):
            m = peer(i)
            wait_for(buf.at[m, half(i - 1), c], ag_r.at[which, m, i - 1])
            ag_turn(buf, which, i).start()

    def ag_relay(buf, which, i):
        m = peer(i)
        if i < 3:
            wait_for(buf.at[m, half(2 - i), c], ag_r.at[which, m, 2 - i])
        else:
            for j in range(2):
                wait_for(buf.at[m, half(j), c], ag_d.at[which, j])
        ag_across(buf, which, i).start()

    def ag_other(buf, which, i):
        m = peer(i)
        wait_for(buf.at[m, :, oc], ag_x.at[which, m])

    def ag_end(buf, which):
        for i in (1, 2):
            for j in range(2):
                ag_copy(buf, which, i, j).wait_send()
            ag_turn(buf, which, i).wait_send()
        for i in range(4):
            ag_across(buf, which, i).wait_send()

    def rs_copy(part, which, i):
        m = peer(i)
        return remote(
            part.at[m, :, oc], sib.at[which, m], rs_s.at[which, i], rs_r.at[which, m], sibling
        )

    def rs_part(part, which, i, j):
        m = peer(i)
        return remote(
            part.at[m, half(j), c],
            rcv.at[which, i - 1, half(j)],
            rs_s.at[which, 2 + 2 * i + j],
            rs_x.at[which, i - 1, j],
            dev(m, z, c),
        )

    def rs_turn(part, which, j):
        return remote(
            part.at[peer(3), half(j), c],
            turn.at[which, j],
            rs_s.at[which, 8 + j],
            rs_d.at[which, j],
            dev(peer(j + 1), z, c),
        )

    def rs_pair(part, which, i):
        m = peer(i)
        wait_for(sib.at[which, m], rs_r.at[which, m])
        return part[m, :, c].astype(F32) + sib[which, m].astype(F32)

    def rs_halves(part, which, i):
        m = peer(i)
        part[m, :, c] = rs_pair(part, which, i).astype(BF)
        if i == 3:
            for j in range(2):
                rs_turn(part, which, j).start()
        else:
            rs_part(part, which, i, i - 1).start()

    def rs_start(part, which, compute):
        for i, ready in ((3, None), (1, 3), (2, 1), (0, 2)):
            compute(i)
            rs_copy(part, which, i).start()
            if ready:
                rs_halves(part, which, ready)

    def rs_corner(part, which):
        for j in range(2):
            wait_for(turn.at[which, j], rs_d.at[which, j])
            m = peer(2 - j)
            sums = part[m, half(j), c].astype(F32) + turn[which, j].astype(F32)
            part[m, half(j), c] = sums.astype(BF)
            rs_part(part, which, 2 - j, j).start()

    def rs_sum(part, which):
        total = rs_pair(part, which, 0)
        for i in (1, 2):
            for j in range(2):
                wait_for(rcv.at[which, i - 1, half(j)], rs_x.at[which, i - 1, j])
            total = total + rcv[which, i - 1].astype(F32)
        return total.reshape(128, 1024)

    def rs_end(part, which):
        for i in range(4):
            rs_copy(part, which, i).wait_send()
        for j in range(2):
            rs_turn(part, which, j).wait_send()
            for i in (1, 2):
                rs_part(part, which, i, j).wait_send()

    def grads_to_far(grad, land, which, j):
        return remote(
            grad(far[j]), land.at[z], gz_s.at[which, 1 + j], gz_r.at[which, z], dev(k, far[j], c)
        )

    def line_adds(grad, land, add, which, start):
        @pl.when(jnp.logical_not(middle))
        def _():
            mid = 1 + z // 2
            for j in range(2):
                copy = remote(
                    grad(far_of(mid)[j]),
                    add.at[j],
                    gz_s.at[which, j],
                    gx_r.at[which, j],
                    dev(k, mid, c),
                )
                if start:
                    copy.start()
                else:
                    copy.wait_send()

    def line_near(grad, land, add, which, start):
        @pl.when(middle)
        def _():
            copy = remote(
                grad(z_end), land.at[z], gz_s.at[which, 0], gz_r.at[which, z], dev(k, z_end, c)
            )
            if start:
                copy.start()
            else:
                copy.wait_send()
                for j in range(2):
                    grads_to_far(grad, land, which, j).wait_send()

        @pl.when(jnp.logical_not(middle))
        def _():
            mid = 1 + z // 2
            copy = remote(
                grad(mid), land.at[z], gz_s.at[which, 2], gz_r.at[which, z], dev(k, mid, c)
            )
            if start:
                copy.start()
            else:
                copy.wait_send()

    def line_grads(grad, land, add, which, start):
        line_adds(grad, land, add, which, start)
        line_near(grad, land, add, which, start)

    def line_grads_relay(grad, land, add, which, j):
        @pl.when(middle)
        def _():
            wait_for(add.at[j], gx_r.at[which, j])
            mine = grad(far[j])
            mine[...] = (mine[...].astype(F32) + add[j].astype(F32)).astype(BF)
            grads_to_far(grad, land, which, j).start()

    def line_sum(grad, land, which):
        total = grad(z)[...].astype(F32)
        for j in range(2):
            wait_for(land.at[near[j]], gz_r.at[which, near[j]])
            total = total + land[near[j]].astype(F32)
        return total

    def dwgu_block(j):
        return lambda b: dwgu.at[pl.ds(2 * j, 2), b]

    def units_line(j):
        return dwgu_block(j), zgu.at[:, pl.ds(2 * j, 2)], xgu.at[:, pl.ds(2 * j, 2)], (1, 5)[j]

    def dwqkv_block(b):
        return dwqkv.at[:, b]

    def dwd_block(j):
        return lambda b: dwd.at[j, b]

    def out_grads_add(start):
        @pl.when((c != side) & jnp.logical_not(middle))
        def _():
            copy = remote(dwo, xo, go_s.at[0], go_x, dev(k, 1 + side, c))
            if start:
                copy.start()
            else:
                copy.wait_send()

    def out_grads_near(start):
        @pl.when(c == side)
        def _():
            other = 4 * side + 1 - z
            copy = remote(
                dwo.at[pl.ds(2 * (other % 2), 2)], zo.at[0], go_s.at[0], go_z.at[0], dev(k, other, c)
            )
            if start:
                copy.start()
            else:
                copy.wait_send()

    def out_grads_relay(start):
        @pl.when((c != side) & middle)
        def _():
            if start:
                wait_for(xo, go_x)
                dwo[...] = (dwo[...].astype(F32) + xo[...].astype(F32)).astype(BF)
            for p in range(2):
                copy = remote(
                    dwo.at[pl.ds(2 * p, 2)], zo.at[1], go_s.at[p], go_z.at[1], dev(k, 2 * c + p, c)
                )
                if start:
                    copy.start()
                else:
                    copy.wait_send()

    def out_grads_home(start):
        @pl.when(c == side)
        def _():
            mine = dwo.at[pl.ds(2 * (z % 2), 2)]
            if start:
                total = mine[...].astype(F32)
                for j in range(2):
                    wait_for(zo.at[j], go_z.at[j])
                    total = total + zo[j].astype(F32)
                mine[...] = total.astype(BF)
                pltpu.make_async_copy(dwo.at[2 * (z % 2) + c], go_o, go_r).start()
            copy = remote(dwo.at[2 * (z % 2) + oc], go_o, go_s.at[1], go_r, sibling)
            if start:
                copy.start()
            else:
                copy.wait_send()

    def gather_back(which, dst, start):
        for b in range(4):
            here = (z == k) & (z == b)
            src = back.at[which, b]
            place = dst.at[pl.ds(pl.multiple_of(32 * k, 32), 32)]

            @pl.when(here)
            def _():
                if start:
                    pltpu.make_async_copy(src, place, tb_r.at[which, k]).start()

            @pl.when(jnp.logical_not(here))
            def _():
                copy = remote(src, place, tb_s.at[which, b], tb_r.at[which, k], dev(z, b, c))
                if start:
                    copy.start()
                else:
                    copy.wait_send()

    spread(lat_in, lat_place, 0, True)
    for load in loads[:5]:
        load.wait()
    for i, w in enumerate((wq_raw, wk_raw, wv_raw)):
        rows = scaled_rows(w, gain_one).astype(BF)
        for r in range(RANKS):
            wqkv_in[r, :, i * 128 : (i + 1) * 128] = rows[:, r * 128 : (r + 1) * 128]
    plane_weights(wqkv_in, wqkv, 0, True)
    spread_lens(True)
    loads[5].wait()
    wd_in[0] = wd_raw[0:32]
    wd_in[1] = wd_raw[32:64]
    wd_in[2, 0:16] = wd_raw[64:80]
    wd_in[2, 16:32] = jnp.concatenate([wd_raw[80:88], jnp.zeros((8, 1024), BF)], axis=0)
    out_across(True)
    own_down = pltpu.make_async_copy(wd_in, wd.at[:, z], wd_r)
    own_down.start()
    out_along(True)
    for load in loads[6:]:
        load.wait()
    units_to_ranks()
    spread_on(lat_in, lat_place, 0, True)
    plane_weights(wgu_in, wgu, 1, True)
    spread(dout_in, cot_place, 1, True)
    plane_weights_here(wqkv, 0)
    line_send(qkv_block, 0, (1, 0), (0, 1))
    out_relay(True)
    for b in range(4):
        wait_for(own_l.at[b], tr_r.at[0, b])
    lat_f = own_l[...].reshape(128, 1024).astype(F32)
    r_one = lax.rsqrt(jnp.mean(lat_f * lat_f, axis=-1, keepdims=True) + EPS)
    n_one[k, :, c] = (lat_f * r_one).astype(BF).reshape(4, 32, 1024)
    ag_send(n_one, 0)
    line_relay(qkv_block, 0, 0)
    ag_corner(n_one, 0)
    line_relay(qkv_block, 0, 1)
    spread_on(dout_in, cot_place, 1, True)
    plane_weights_here(wgu, 1)
    for j in range(2):
        line_send(gu_block(j), GU[j], (1, 0), (0, 1))
    ag_relay(n_one, 0, 1)
    ag_relay(n_one, 0, 2)
    ag_relay(n_one, 0, 3)

    line_here(qkv_block, 0)

    @pl.loop(0, 4)
    def _(i):
        ag_other(n_one, 0, i)
        m = peer(i)
        block = n_one[m].reshape(256, 1024)
        out = dot_nn(block, wqkv[...].reshape(1024, 384))
        qkv[:, m] = out.astype(BF).reshape(8, 32, 384)

    line_send(gu_block(2), GU[2], (1, 0), (0, 1))
    line_send(down_block, 2, (1, 0), (0, 1), src=wd_in)

    for b in range(4):
        wait_for(cot.at[k, b, c], tr_r.at[1, b])
    ag_send(cot, 1)
    wait_for(lens, ln_r)
    lane = lax.broadcasted_iota(jnp.int32, (128, 128), 1)
    row = lax.broadcasted_iota(jnp.int32, (128, 128), 0)
    first = lane < 64

    def two_heads(v):
        zero = jnp.zeros_like(v)
        return jnp.concatenate(
            [jnp.where(first, v, zero), jnp.where(first, zero, v)], axis=0
        )

    def one_of_two(v):
        return jnp.where(first, v[:128], v[128:])

    def part_of(t0, t1, col):
        return qkv[t0:t1, :, :, col * 128 : (col + 1) * 128].reshape((t1 - t0) * 128, 128)

    for t in range(8):
        span = (t + 1) * 128
        q = two_heads(part_of(t, t + 1, 0).astype(F32) * 0.125).astype(BF)
        keys = part_of(0, t + 1, 1)
        vals = part_of(0, t + 1, 2)
        pos = row + t * 128
        begin = jnp.zeros((128, 128), jnp.int32)
        end = jnp.zeros((1, 128), jnp.int32)
        for g in range(4):
            length = lens[g : g + 1, :]
            end = end + length
            begin = begin + jnp.where(end <= pos, length, 0)
        allowed = []
        for u in range(t + 1):
            ok = begin <= lane + u * 128
            if u == t:
                ok = ok & (lane <= row)
            allowed.append(ok)
        allowed = jnp.concatenate(allowed, axis=1)
        scores = dot_right(q, keys)
        sums = []
        raws = []
        for h in range(2):
            sc = jnp.where(allowed, scores[h * 128 : (h + 1) * 128], -1e30)
            top = jnp.max(sc, axis=-1, keepdims=True)
            expo = jnp.exp(sc - top)
            low = expo.astype(BF)
            probs[t, h * 128 : (h + 1) * 128, 0:span] = low
            sums.append(jnp.sum(low.astype(F32), axis=-1, keepdims=True))
        raw = dot_nn(probs[t, :, 0:span], vals)
        both = jnp.where(first, sums[0], sums[1])
        attended = one_of_two(raw) / both
        tot[t] = both
        att_f[t] = attended
        att[:, t] = attended.astype(BF).reshape(4, 32, 128)

    line_relay(gu_block(0), GU[0], 0)
    out_here()

    def project_out(i):
        m = peer(i)
        out = dot_nn(att[m].reshape(256, 128), wo[...].reshape(128, 1024))
        part_a[m] = out.astype(BF).reshape(4, 2, 32, 1024)

    rs_start(part_a, 0, project_out)
    for t in range(8):
        q_two[t] = two_heads(part_of(t, t + 1, 0).astype(F32)).astype(BF)
    ag_corner(cot, 1)
    line_relay(gu_block(0), GU[0], 1)
    line_relay(gu_block(1), GU[1], 0)
    rs_corner(part_a, 0)
    for i in (1, 2):
        ag_relay(cot, 1, i)
    line_relay(gu_block(1), GU[1], 1)
    line_relay(gu_block(2), GU[2], 0)
    res = own_l[...].reshape(128, 1024).astype(F32) + rs_sum(part_a, 0)
    resid[...] = res
    r_two = lax.rsqrt(jnp.mean(res * res, axis=-1, keepdims=True) + EPS)
    n_two[k, :, c] = (res * r_two).astype(BF).reshape(4, 32, 1024)
    ag_send(n_two, 2)
    ag_relay(cot, 1, 3)
    line_relay(gu_block(2), GU[2], 1)

    ag_corner(n_two, 2)
    line_relay(down_block, 2, 0)
    ag_relay(n_two, 2, 1)
    ag_relay(n_two, 2, 2)
    line_relay(down_block, 2, 1)

    def feed_forward(j, i):
        m = peer(i)
        lo, mid, hi = 256 * j, 256 * j + 128, 256 * j + 256
        gu = dot_nn(n_two[m].reshape(256, 1024), wgu[:, :, :, :, lo:hi].reshape(1024, 256))
        gate = gu[:, :128]
        up = gu[:, 128:]
        sig = jax.nn.sigmoid(gate)
        active = gate * sig
        hid[m, :, 128 * j : 128 * j + 128] = (active * up).astype(BF)
        slope[m, :, lo:mid] = up * sig * (1.0 + gate * (1.0 - sig))
        slope[m, :, mid:hi] = active

    def down_grad(j):
        left = hid[:, :, 128 * j : 128 * j + 128].reshape(1024, 128)

        dwd[j] = dot_left(left, cot[...].reshape(1024, 1024)).astype(BF).reshape(4, 32, 1024)
        line_grads(dwd_block(j), zd.at[j], xd.at[j], 2 + j, True)

    line_here(gu_block(0), GU[0])

    @pl.loop(0, 3)
    def _(i):
        ag_other(n_two, 2, i)
        feed_forward(0, i)

    ag_relay(n_two, 2, 3)
    ag_other(n_two, 2, 3)
    feed_forward(0, 3)
    for i in range(4):
        ag_other(cot, 1, i)
    down_grad(0)
    line_here(gu_block(1), GU[1])

    @pl.loop(0, 4)
    def _(i):
        feed_forward(1, i)

    down_grad(1)
    line_here(gu_block(2), GU[2])

    @pl.loop(0, 4)
    def _(i):
        feed_forward(2, i)

    down_grad(2)
    line_here(down_block, 2)
    own_down.wait()

    def feed_back(i):
        m = peer(i)
        g_hid = dot_right(cot[m].reshape(256, 1024), wd[...].reshape(384, 1024))
        for j in range(6):
            cols = slice(128 * j, 128 * j + 128)
            part = g_hid[:, 128 * (j // 2) : 128 * (j // 2) + 128]
            ggu[m, :, cols] = (part * slope[m, :, cols]).astype(BF)
        out = dot_right(ggu[m], wgu[...].reshape(1024, 768))
        part_b[m] = out.astype(BF).reshape(4, 2, 32, 1024)

    def down_relay(j):
        for i in range(2):
            line_grads_relay(dwd_block(j), zd.at[j], xd.at[j], 2 + j, i)

    rs_start(part_b, 1, feed_back)
    down_relay(0)

    def units_grad(d):
        cols = pl.ds(pl.multiple_of(d * 256, 256), 256)
        left = n_two[:, :, :, :, cols].reshape(1024, 256)
        out = dot_left(left, ggu[...].reshape(1024, 768))
        dwgu[d] = out.astype(BF).reshape(4, 2, 32, 768)

    @pl.loop(0, 2)
    def _(d):
        units_grad(d)

    line_adds(*units_line(0), True)
    rs_corner(part_b, 1)
    down_relay(1)

    @pl.loop(2, 4)
    def _(d):
        units_grad(d)

    line_adds(*units_line(1), True)
    for j in range(2):
        line_near(*units_line(j), True)
    down_relay(2)

    @pl.loop(0, 4)
    def _(i):
        m = peer(i)
        out = dot_nn(hid[m], wd[...].reshape(384, 1024))
        part_c[m] = out.astype(BF).reshape(4, 2, 32, 1024)
        rs_copy(part_c, 2, i).start()

    scaled = rs_sum(part_b, 1)
    res = resid[...]
    r_two = lax.rsqrt(jnp.mean(res * res, axis=-1, keepdims=True) + EPS)
    normed = res * r_two
    inner = jnp.mean(scaled * normed, axis=-1, keepdims=True)
    g_res = cot[k, :, c].reshape(128, 1024).astype(F32) + r_two * (scaled - normed * inner)
    gres[...] = g_res
    gbr[k, :, c] = g_res.astype(BF).reshape(4, 32, 1024)
    ag_send(gbr, 3)

    ag_corner(gbr, 3)
    ag_relay(gbr, 3, 1)
    ag_relay(gbr, 3, 2)
    line_grads_relay(*units_line(0), 0)

    def attended_grad(i):
        ag_other(gbr, 3, i)
        m = peer(i)
        out = dot_right(gbr[m].reshape(256, 1024), wo[...].reshape(128, 1024))
        gatt[:, m] = out.astype(BF).reshape(8, 32, 128)

    @pl.loop(0, 3)
    def _(i):
        attended_grad(i)

    ag_relay(gbr, 3, 3)
    for i in (3, 1, 2):
        rs_halves(part_c, 2, i)
    line_grads_relay(*units_line(0), 1)
    attended_grad(3)
    line_grads_relay(*units_line(1), 0)

    for t in range(8):
        span = (t + 1) * 128
        keys = part_of(0, t + 1, 1)
        vals = part_of(0, t + 1, 2)
        ratio = gatt[t].reshape(128, 128).astype(F32) / tot[t]
        g_raw = two_heads(ratio.astype(BF).astype(F32)).astype(BF)
        graw_two[t] = g_raw
        prod = ratio * att_f[t]
        g_tot = -jnp.sum(two_heads(prod), axis=-1, keepdims=True)
        g_pr = dot_right(g_raw, vals)
        g_sc = probs[t, :, 0:span].astype(F32) * (g_pr + g_tot)
        gsc[t, :, 0:span] = g_sc.astype(BF)
        g_q = one_of_two(dot_nn(gsc[t, :, 0:span], keys)) * 0.125
        gqkv[:, t, :, 0:128] = g_q.astype(BF).reshape(4, 32, 128)
    line_grads_relay(*units_line(1), 1)
    for u in range(8):
        cols = slice(u * 128, (u + 1) * 128)
        rows = (8 - u) * 256
        g_k = dot_left(gsc[u:, :, cols].reshape(rows, 128), q_two[u:].reshape(rows, 128)) * 0.125
        g_v = dot_left(probs[u:, :, cols].reshape(rows, 128), graw_two[u:].reshape(rows, 128))
        gqkv[:, u, :, 128:256] = g_k.astype(BF).reshape(4, 32, 128)
        gqkv[:, u, :, 256:384] = g_v.astype(BF).reshape(4, 32, 128)

    rs_corner(part_c, 2)
    rs_end(part_a, 0)

    def heads_back(i):
        m = peer(i)
        out = dot_right(gqkv[m].reshape(256, 384), wqkv[...].reshape(1024, 384))
        part_a[m] = out.astype(BF).reshape(4, 2, 32, 1024)

    rs_start(part_a, 3, heads_back)

    for d in range(2):
        left = n_one[:, :, :, :, 512 * d : 512 * d + 512].reshape(1024, 512)
        out = dot_left(left, gqkv[...].reshape(1024, 384))
        dwqkv[2 * d : 2 * d + 2] = out.astype(BF).reshape(2, 4, 2, 32, 384)

    line_adds(dwqkv_block, zq, xq, 0, True)
    dwo[...] = dot_left(att[...].reshape(1024, 128), gbr[...].reshape(1024, 1024)).astype(BF).reshape(4, 32, 1024)
    out_grads_add(True)
    out_grads_near(True)
    rs_corner(part_a, 3)


    out_f = resid[...] + rs_sum(part_c, 2)
    back[0] = out_f.astype(BF).reshape(4, 32, 1024)
    gather_back(0, lat_o, True)
    line_near(dwqkv_block, zq, xq, 0, True)

    def plane_grads(land, dst, which, start):
        for i in range(4):
            m = peer(i)
            for same in (True, False):
                cc = c if same else oc
                src = land.at[z, m, cc]
                place = dst.at[rank]
                if i == 0 and same:
                    if start:
                        pltpu.make_async_copy(src, place, ga_r.at[which, rank]).start()
                else:
                    copy = remote(
                        src,
                        place,
                        ga_s.at[which, 2 * i + (0 if same else 1)],
                        ga_r.at[which, rank],
                        dev(m, z, cc),
                    )
                    if start:
                        copy.start()
                    else:
                        copy.wait_send()

    line_grads_relay(dwqkv_block, zq, xq, 0, 0)
    line_grads_relay(dwqkv_block, zq, xq, 0, 1)
    scaled = rs_sum(part_a, 3)
    lat_f = own_l[...].reshape(128, 1024).astype(F32)
    r_one = lax.rsqrt(jnp.mean(lat_f * lat_f, axis=-1, keepdims=True) + EPS)
    normed = lat_f * r_one
    inner = jnp.mean(scaled * normed, axis=-1, keepdims=True)
    d_lat = gres[...] + r_one * (scaled - normed * inner)
    back[1] = d_lat.astype(BF).reshape(4, 32, 1024)
    gather_back(1, dlat_o, True)
    out_grads_relay(True)
    for j in range(2):
        grad, land, _, which = units_line(j)
        land[z] = line_sum(grad, land, which).astype(BF)
    plane_grads(zgu, ggu_o, 1, True)

    for j in range(3):
        down_sum[32 * j : 32 * j + 32] = line_sum(dwd_block(j), zd.at[j], 2 + j)
    down_out = pltpu.make_async_copy(down_sum.at[pl.ds(0, 88)], gd_o, gd_r)
    down_out.start()
    zq[z] = line_sum(dwqkv_block, zq, 0).astype(BF)
    plane_grads(zq, gqkv_o, 0, True)
    out_grads_home(True)

    for which, dst in ((0, lat_o), (1, dlat_o)):
        for b in range(4):
            wait_for(dst.at[pl.ds(32 * b, 32)], tb_r.at[which, b])
    wait_for(go_o, go_r)
    for which, dst in ((1, ggu_o), (0, gqkv_o)):
        for r in range(RANKS):
            wait_for(dst.at[r], ga_r.at[which, r])
    spread(lat_in, lat_place, 0, False)
    spread_on(lat_in, lat_place, 0, False)
    spread(dout_in, cot_place, 1, False)
    spread_on(dout_in, cot_place, 1, False)
    spread_lens(False)
    plane_weights(wqkv_in, wqkv, 0, False)
    plane_weights(wgu_in, wgu, 1, False)
    line_sent(qkv_block, 0)
    for j in range(3):
        line_sent(gu_block(j), GU[j])
    line_sent(down_block, 2, wd_in)
    down_out.wait()
    out_across(False)
    out_along(False)
    out_relay(False)
    for which, buf in enumerate((n_one, cot, n_two, gbr)):
        ag_end(buf, which)
    rs_end(part_b, 1)
    rs_end(part_c, 2)
    rs_end(part_a, 3)
    for j in range(2):
        line_grads(*units_line(j), False)
    line_grads(dwqkv_block, zq, xq, 0, False)
    for j in range(3):
        line_grads(dwd_block(j), zd.at[j], xd.at[j], 2 + j, False)
    plane_grads(zgu, ggu_o, 1, False)
    plane_grads(zq, gqkv_o, 0, False)
    out_grads_add(False)
    out_grads_near(False)
    out_grads_relay(False)
    out_grads_home(False)
    gather_back(0, lat_o, False)
    gather_back(1, dlat_o, False)


def run_layer(lat, dout, lengths, gain_one, gain_two, weights):
    vm = pltpu.VMEM
    dma = pltpu.SemaphoreType.DMA
    rows = (4, 4, 2, 32)
    return pl.pallas_call(
        layer_kernel,
        out_shape=(
            jax.ShapeDtypeStruct((128, 1024), BF),
            jax.ShapeDtypeStruct((128, 1024), BF),
            jax.ShapeDtypeStruct((RANKS, 32, 384), BF),
            jax.ShapeDtypeStruct((RANKS, 32, 768), BF),
            jax.ShapeDtypeStruct((88, 1024), F32),
            jax.ShapeDtypeStruct((32, 1024), BF),
        ),
        in_specs=[pl.BlockSpec(memory_space=pl.ANY)] * 2
        + [pl.BlockSpec(memory_space=pltpu.SMEM)]
        + [pl.BlockSpec(memory_space=pl.ANY)] * 9,
        out_specs=[pl.BlockSpec(memory_space=pl.ANY)] * 6,
        scratch_shapes=[
            vm((1, 32), BF),
            vm((1, 32), BF),
            vm((32, 1024), BF),
            vm((32, 1024), BF),
            vm((32, 1024), BF),
            vm((32, 2816), BF),
            vm((32, 2816), BF),
            vm((88, 1024), BF),
            dma((8,)),
            vm((8, 128), jnp.int32),
            vm((RANKS, 32, 384), BF),
            vm((RANKS, 32, 768), BF),
            vm((3, 32, 1024), BF),
            vm((4, 32, 1024), BF),
            vm((2, 4, 32, 1024), BF),
            vm((8, 128), jnp.int32),
            vm(rows + (1024,), BF),
            vm(rows + (1024,), BF),
            vm(rows + (1024,), BF),
            vm(rows + (1024,), BF),
            vm(rows + (384,), BF),
            vm(rows + (768,), BF),
            vm((3, 4, 32, 1024), BF),
            vm((4, 32, 1024), BF),
            vm((8, 4, 32, 384), BF),
            vm((4, 8, 32, 128), BF),
            vm((8, 128, 128), F32),
            vm((8, 128, 128), F32),
            vm((8, 256, 1024), BF),
            vm((8, 256, 1024), BF),
            vm(rows + (1024,), BF),
            vm(rows + (1024,), BF),
            vm(rows + (1024,), BF),
            vm((4, 4, 4, 32, 1024), BF),
            vm((4, 2, 4, 32, 1024), BF),
            vm((4, 2, 2, 32, 1024), BF),
            vm((4, 256, 384), BF),
            vm((4, 256, 768), BF),
            vm((4, 256, 768), F32),
            vm((8, 4, 32, 128), BF),
            vm((8, 256, 128), BF),
            vm((8, 256, 128), BF),
            vm((4, 8, 32, 384), BF),
            vm(rows + (384,), BF),
            vm(rows + (768,), BF),
            vm((3, 4, 32, 1024), BF),
            vm((4, 32, 1024), BF),
            vm((4, 4, 2, 32, 384), BF),
            vm((4, 4, 2, 32, 768), BF),
            vm((3, 4, 32, 1024), BF),
            vm((2, 2, 32, 1024), BF),
            vm((4, 32, 1024), BF),
            vm((2, 4, 2, 32, 384), BF),
            vm((2, 4, 2, 32, 768), BF),
            vm((3, 2, 32, 1024), BF),
            vm((96, 1024), F32),
            vm((128, 1024), F32),
            vm((128, 1024), F32),
            vm((2, 4, 32, 1024), BF),
            dma((2, 4)),
            dma((2, 4)),
            dma((2, 4)),
            dma((2, 4)),
            dma,
            dma,
            dma((2, 8)),
            dma((2, 8)),
            dma((6, 4)),
            dma((6, 4)),
            dma,
            dma((1,)),
            dma((2,)),
            dma((4, 12)),
            dma((4, 4, 2)),
            dma((4, 4)),
            dma((4, 2)),
            dma((4, 12)),
            dma((4, 4)),
            dma((4, 2, 2)),
            dma((4, 2)),
            dma((6, 4)),
            dma((6, 4)),
            dma((6, 2)),
            dma((2, 8)),
            dma((2, 8)),
            dma,
            dma((2,)),
            dma,
            dma,
            dma((2,)),
            dma((2, 4)),
            dma((2, 4)),
        ],
        compiler_params=pltpu.CompilerParams(
            collective_id=0, has_side_effects=True, vmem_limit_bytes=60 * 1024 * 1024
        ),
    )(lat, dout, lengths, gain_one, gain_two, *weights)


def finish_kernel(
    lat,
    dlat,
    gqkv_in,
    ggu_in,
    gd,
    go_in,
    gain_one,
    gain_two,
    wq,
    wk,
    wv,
    wg,
    wu,
    lat_o,
    dlat_o,
    g_one_o,
    gq_o,
    gk_o,
    gv_o,
    go_o,
    g_two_o,
    gg_o,
    gu_o,
    gd_o,
    gqkv,
    ggu,
    go,
    lat_v,
    dlat_v,
    gd_v,
    g_one_v,
    gq_v,
    gk_v,
    gv_v,
    go_v,
    g_two_v,
    gg_v,
    gu_v,
    sems,
    out_sems,
):
    moves = ((gqkv_in, gqkv), (ggu_in, ggu), (go_in, go), (lat, lat_v), (dlat, dlat_v), (gd, gd_v))
    copies = [pltpu.make_async_copy(src, dst, sems.at[i]) for i, (src, dst) in enumerate(moves)]
    for copy in copies:
        copy.start()
    leaving = []

    def leave(src, dst):
        copy = pltpu.make_async_copy(src, dst, out_sems.at[len(leaving)])
        copy.start()
        leaving.append(copy)

    col_one = jnp.sum(on_diagonal(gain_one[...]), axis=1, keepdims=True)
    col_two = jnp.sum(on_diagonal(gain_two[...]), axis=1, keepdims=True)

    def as_row(acc):
        return jnp.sum(on_diagonal(jnp.sum(acc, axis=1, keepdims=True)), axis=0, keepdims=True)

    for copy, src, dst in ((copies[3], lat_v, lat_o.at[0]), (copies[4], dlat_v, dlat_o.at[0]), (copies[5], gd_v, gd_o)):
        copy.wait()
        leave(src, dst)
    copies[0].wait()
    acc = jnp.zeros((32, 128), F32)
    for i, (w, out) in enumerate(((wq, gq_v), (wk, gk_v), (wv, gv_v))):
        for r in range(RANKS):
            cols = slice(r * 128, (r + 1) * 128)
            part = gqkv[r, :, i * 128 : (i + 1) * 128].astype(F32)
            out[:, cols] = part * col_one
            acc = acc + part * w[:, cols].astype(F32)
        leave(out, (gq_o, gk_o, gv_o)[i])
    g_one_v[...] = as_row(acc)
    leave(g_one_v, g_one_o)
    copies[1].wait()
    acc = jnp.zeros((32, 256), F32)
    for i, (w, out) in enumerate(((wg, gg_v), (wu, gu_v))):
        parts = [None] * 96
        for r in range(RANKS):
            for j in range(3):
                third = ggu[r, :, 256 * j + 128 * i : 256 * j + 128 * i + 128].astype(F32)
                for b, unit in enumerate(units_of(r)):
                    parts[3 * unit + j] = third[:, 32 * b : 32 * b + (24 if j == 2 else 32)]
        rows = jnp.concatenate(parts, axis=1)
        out[...] = rows * col_two
        leave(out, (gg_o, gu_o)[i])
        prod = rows * w[...].astype(F32)
        for n in range(11):
            acc = acc + prod[:, n * 256 : (n + 1) * 256]
    g_two_v[...] = as_row(acc)
    leave(g_two_v, g_two_o)
    copies[2].wait()
    go_v[...] = go[...].astype(F32)
    leave(go_v, go_o)
    for copy in leaving:
        copy.wait()


def finish(*arrays):
    outs = (
        ((1, 128, 1024), BF),
        ((1, 128, 1024), BF),
        ((1, 32), F32),
        ((32, 1024), F32),
        ((32, 1024), F32),
        ((32, 1024), F32),
        ((32, 1024), F32),
        ((1, 32), F32),
        ((32, 2816), F32),
        ((32, 2816), F32),
        ((88, 1024), F32),
    )
    hbm = pl.BlockSpec(memory_space=pltpu.HBM)
    vmem = pl.BlockSpec(memory_space=pltpu.VMEM)
    return pl.pallas_call(
        finish_kernel,
        out_shape=tuple(jax.ShapeDtypeStruct(*o) for o in outs),
        in_specs=[hbm] * 6 + [vmem] * 7,
        out_specs=[pl.BlockSpec(memory_space=pl.ANY)] * len(outs),
        scratch_shapes=[
            pltpu.VMEM((RANKS, 32, 384), BF),
            pltpu.VMEM((RANKS, 32, 768), BF),
            pltpu.VMEM((32, 1024), BF),
            pltpu.VMEM((128, 1024), BF),
            pltpu.VMEM((128, 1024), BF),
            pltpu.VMEM((88, 1024), F32),
            pltpu.VMEM((1, 32), F32),
            pltpu.VMEM((32, 1024), F32),
            pltpu.VMEM((32, 1024), F32),
            pltpu.VMEM((32, 1024), F32),
            pltpu.VMEM((32, 1024), F32),
            pltpu.VMEM((1, 32), F32),
            pltpu.VMEM((32, 2816), F32),
            pltpu.VMEM((32, 2816), F32),
            pltpu.SemaphoreType.DMA((6,)),
            pltpu.SemaphoreType.DMA((11,)),
        ],
        compiler_params=pltpu.CompilerParams(vmem_limit_bytes=60 * 1024 * 1024),
    )(*arrays)


def plane_device(
    latents,
    d_out,
    lengths,
    gain_attn,
    w_query,
    w_key,
    w_value,
    w_out,
    gain_ffn,
    w_gate,
    w_up,
    w_down,
):
    gains = gain_attn.reshape(1, 32), gain_ffn.reshape(1, 32)
    weights = w_query, w_key, w_value, w_gate, w_up, w_down, w_out
    parts = run_layer(latents[0], d_out[0], lengths, *gains, weights)
    outs = finish(*parts, *gains, w_query, w_key, w_value, w_gate, w_up)
    return tuple(o.reshape(32) if o.shape == (1, 32) else o for o in outs)


def solution(mesh):
    return jax.shard_map(
        plane_device if planes_fit(mesh) else per_device,
        mesh=mesh,
        in_specs=(
            P("dp", "seq", None),
            P("dp", "seq", None),
            P("dp", None),
            P(("dp", "seq")),
            P(("dp", "seq"), None),
            P(("dp", "seq"), None),
            P(("dp", "seq"), None),
            P(("dp", "seq"), None),
            P(("dp", "seq")),
            P(("dp", "seq"), None),
            P(("dp", "seq"), None),
            P(("dp", "seq"), None),
        ),
        out_specs=(
            P("dp", "seq", None),
            P("dp", "seq", None),
            P(("dp", "seq")),
            P(("dp", "seq"), None),
            P(("dp", "seq"), None),
            P(("dp", "seq"), None),
            P(("dp", "seq"), None),
            P(("dp", "seq")),
            P(("dp", "seq"), None),
            P(("dp", "seq"), None),
            P(("dp", "seq"), None),
        ),
        check_vma=False,
    )
```

```python
import functools
import math

import jax
import jax.numpy as jnp
from jax import lax
from jax.experimental import pallas as pl
from jax.experimental.pallas import tpu as pltpu
from jax.sharding import PartitionSpec as P

HEADS = 16


EPS = 1e-05


def norm_rows(values, gain_vec):
    factor = lax.rsqrt(jnp.mean(values * values, axis=-1, keepdims=True) + EPS)
    normed = values * factor
    return (normed * gain_vec, normed, factor)


def norm_back(grad_out, normed, factor, gain_vec):
    scaled = grad_out * gain_vec
    inner = jnp.mean(scaled * normed, axis=-1, keepdims=True)
    return (factor * (scaled - normed * inner), jnp.sum(grad_out * normed, axis=0))


def dot_left(left, right):
    return lax.dot_general(
        left, right, (((0,), (0,)), ((), ())), preferred_element_type=jnp.float32
    )


def dot_right(left, right):
    return lax.dot_general(
        left, right, (((1,), (1,)), ((), ())), preferred_element_type=jnp.float32
    )


def per_device(
    latents,
    d_out,
    lengths,
    gain_attn,
    w_query,
    w_key,
    w_value,
    w_out,
    gain_ffn,
    w_gate,
    w_up,
    w_down,
):
    g_attn, full_query, full_key, full_value, full_out, g_ffn, full_gate, full_up, full_down = (
        lax.all_gather(gain_attn, ("dp", "seq"), axis=0, tiled=True),
        lax.all_gather(w_query, ("dp", "seq"), axis=0, tiled=True),
        lax.all_gather(w_key, ("dp", "seq"), axis=0, tiled=True),
        lax.all_gather(w_value, ("dp", "seq"), axis=0, tiled=True),
        lax.all_gather(w_out, ("dp", "seq"), axis=0, tiled=True),
        lax.all_gather(gain_ffn, ("dp", "seq"), axis=0, tiled=True),
        lax.all_gather(w_gate, ("dp", "seq"), axis=0, tiled=True),
        lax.all_gather(w_up, ("dp", "seq"), axis=0, tiled=True),
        lax.all_gather(w_down, ("dp", "seq"), axis=0, tiled=True),
    )
    gain_one = g_attn.astype(jnp.float32)
    gain_two = g_ffn.astype(jnp.float32)
    inputs_f = latents[0].astype(jnp.float32)
    row_count, model_width = inputs_f.shape
    head_size = model_width // HEADS
    group_rows = row_count * lax.axis_size("seq")
    here = lax.axis_index("seq") * row_count + jnp.arange(row_count, dtype=jnp.int32)
    seq_lens = lengths[0]
    seq_ends = jnp.cumsum(seq_lens, dtype=jnp.int32)
    begins = jnp.sum(
        jnp.where(seq_ends[None, :] <= here[:, None], seq_lens[None, :], 0), axis=1, dtype=jnp.int32
    )
    key_block = math.gcd(group_rows, 1024)
    block_count = group_rows // key_block
    key_positions = jnp.arange(group_rows, dtype=jnp.int32).reshape(block_count, key_block)
    h_one_f, normed_one, factor_one = norm_rows(inputs_f, gain_one)
    h_one = h_one_f.astype(jnp.bfloat16)
    query_proj = jnp.dot(h_one, full_query, preferred_element_type=jnp.float32).astype(jnp.bfloat16)
    key_proj = jnp.dot(h_one, full_key, preferred_element_type=jnp.float32).astype(jnp.bfloat16)
    value_proj = jnp.dot(h_one, full_value, preferred_element_type=jnp.float32).astype(jnp.bfloat16)
    keys_all, values_all = (
        lax.all_gather(key_proj, "seq", axis=0, tiled=True),
        lax.all_gather(value_proj, "seq", axis=0, tiled=True),
    )
    query_heads = query_proj.reshape(row_count, HEADS, head_size)

    def split_blocks(array):
        return array.reshape(block_count, key_block, HEADS, head_size)

    def block_scores(key_piece, pos_piece):
        scores = (
            jnp.einsum("qhd,khd->hqk", query_heads, key_piece, preferred_element_type=jnp.float32)
            * 0.125
        )
        allowed = (pos_piece[None, :] <= here[:, None]) & (pos_piece[None, :] >= begins[:, None])
        return (scores, allowed[None])

    def max_step(running, pieces):
        key_piece, pos_piece = pieces
        scores, allowed = block_scores(key_piece, pos_piece)
        return (jnp.maximum(running, jnp.max(jnp.where(allowed, scores, -1e30), axis=-1)), None)

    row_max, _ = lax.scan(
        max_step,
        jnp.full((HEADS, row_count), -1e30, jnp.float32),
        (split_blocks(keys_all), key_positions),
    )

    def sum_step(running, pieces):
        key_piece, value_piece, pos_piece = pieces
        scores, allowed = block_scores(key_piece, pos_piece)
        expon = jnp.where(
            allowed, jnp.exp(jnp.where(allowed, scores, -1e30) - row_max[:, :, None]), 0.0
        )
        rounded = expon.astype(jnp.bfloat16)
        total_sum, raw_sum = running
        total_sum = total_sum + jnp.sum(rounded.astype(jnp.float32), axis=-1)
        raw_sum = raw_sum + jnp.einsum(
            "hqk,khd->qhd", rounded, value_piece, preferred_element_type=jnp.float32
        )
        return ((total_sum, raw_sum), None)

    (total_sum, raw_sum), _ = lax.scan(
        sum_step,
        (
            jnp.zeros((HEADS, row_count), jnp.float32),
            jnp.zeros((row_count, HEADS, head_size), jnp.float32),
        ),
        (split_blocks(keys_all), split_blocks(values_all), key_positions),
    )
    totals_rows = jnp.transpose(total_sum)
    attended = raw_sum / totals_rows[:, :, None]
    attended_low = attended.reshape(row_count, model_width).astype(jnp.bfloat16)
    resid = inputs_f + jnp.dot(attended_low, full_out, preferred_element_type=jnp.float32)
    h_two_f, normed_two, factor_two = norm_rows(resid, gain_two)
    h_two = h_two_f.astype(jnp.bfloat16)
    gate_proj = jnp.dot(h_two, full_gate, preferred_element_type=jnp.float32)
    up_proj = jnp.dot(h_two, full_up, preferred_element_type=jnp.float32)
    gate_sigmoid = jax.nn.sigmoid(gate_proj)
    gate_active = gate_proj * gate_sigmoid
    hidden = (gate_active * up_proj).astype(jnp.bfloat16)
    outputs = resid + jnp.dot(hidden, full_down, preferred_element_type=jnp.float32)
    latents_out = outputs.astype(jnp.bfloat16)[None]
    grad_out = d_out[0]
    grad_down = dot_left(hidden, grad_out)
    g_hidden = dot_right(grad_out, full_down)
    g_gate = (g_hidden * up_proj * gate_sigmoid * (1.0 + gate_proj * (1.0 - gate_sigmoid))).astype(
        jnp.bfloat16
    )
    g_up = (g_hidden * gate_active).astype(jnp.bfloat16)
    grad_gate = dot_left(h_two, g_gate)
    grad_up = dot_left(h_two, g_up)
    g_h_two = dot_right(g_gate, full_gate) + dot_right(g_up, full_up)
    g_norm_two, grad_gain_two = norm_back(g_h_two, normed_two, factor_two, gain_two)
    g_resid = grad_out.astype(jnp.float32) + g_norm_two
    g_branch = g_resid.astype(jnp.bfloat16)
    grad_out_proj = dot_left(attended_low, g_branch)
    g_att = dot_right(g_branch, full_out).reshape(row_count, HEADS, head_size).astype(jnp.bfloat16)
    g_att_f = g_att.astype(jnp.float32)
    g_raw = (g_att_f / totals_rows[:, :, None]).astype(jnp.bfloat16)
    g_total = jnp.transpose(-jnp.sum(g_att_f * raw_sum, axis=-1) / (totals_rows * totals_rows))
    keys_back, values_back = (
        lax.all_gather(key_proj, "seq", axis=0, tiled=True),
        lax.all_gather(value_proj, "seq", axis=0, tiled=True),
    )

    def score_grads(key_piece, value_piece, pos_piece):
        scores, allowed = block_scores(key_piece, pos_piece)
        expon = jnp.where(
            allowed, jnp.exp(jnp.where(allowed, scores, -1e30) - row_max[:, :, None]), 0.0
        )
        g_probs = jnp.einsum("qhd,khd->hqk", g_raw, value_piece, preferred_element_type=jnp.float32)
        g_scores = (expon * (g_probs + g_total[:, :, None])).astype(jnp.bfloat16)
        return (expon, g_scores)

    def grad_step(running, pieces):
        key_piece, value_piece, pos_piece = pieces
        expon, g_scores = score_grads(key_piece, value_piece, pos_piece)
        rounded = expon.astype(jnp.bfloat16)
        running = (
            running
            + jnp.einsum("hqk,khd->qhd", g_scores, key_piece, preferred_element_type=jnp.float32)
            * 0.125
        )
        g_key_piece = (
            jnp.einsum("hqk,qhd->khd", g_scores, query_heads, preferred_element_type=jnp.float32)
            * 0.125
        )
        g_value_piece = jnp.einsum(
            "hqk,qhd->khd", rounded, g_raw, preferred_element_type=jnp.float32
        )
        return (running, (g_key_piece, g_value_piece))

    g_query_f, (g_keys, g_values) = lax.scan(
        grad_step,
        jnp.zeros((row_count, HEADS, head_size), jnp.float32),
        (split_blocks(keys_back), split_blocks(values_back), key_positions),
    )
    mine_key, mine_value = (
        lax.psum_scatter(
            g_keys.reshape(group_rows, model_width).astype(jnp.bfloat16),
            "seq",
            scatter_dimension=0,
            tiled=True,
        ).astype(jnp.float32),
        lax.psum_scatter(
            g_values.reshape(group_rows, model_width).astype(jnp.bfloat16),
            "seq",
            scatter_dimension=0,
            tiled=True,
        ).astype(jnp.float32),
    )
    g_key = mine_key.astype(jnp.bfloat16)
    g_value = mine_value.astype(jnp.bfloat16)
    g_query = g_query_f.reshape(row_count, model_width).astype(jnp.bfloat16)
    grad_query = dot_left(h_one, g_query)
    grad_key = dot_left(h_one, g_key)
    grad_value = dot_left(h_one, g_value)
    g_h_one = (
        dot_right(g_query, full_query) + dot_right(g_key, full_key) + dot_right(g_value, full_value)
    )
    g_norm_one, grad_gain_one = norm_back(g_h_one, normed_one, factor_one, gain_one)
    d_latents = (g_resid + g_norm_one).astype(jnp.bfloat16)[None]
    gain_pair = jnp.stack((grad_gain_one, grad_gain_two), axis=1)
    summed = (
        lax.psum_scatter(gain_pair, ("dp", "seq"), scatter_dimension=0, tiled=True),
        lax.psum_scatter(grad_query, ("dp", "seq"), scatter_dimension=0, tiled=True),
        lax.psum_scatter(grad_key, ("dp", "seq"), scatter_dimension=0, tiled=True),
        lax.psum_scatter(grad_value, ("dp", "seq"), scatter_dimension=0, tiled=True),
        lax.psum_scatter(grad_out_proj, ("dp", "seq"), scatter_dimension=0, tiled=True),
        lax.psum_scatter(grad_gate, ("dp", "seq"), scatter_dimension=0, tiled=True),
        lax.psum_scatter(grad_up, ("dp", "seq"), scatter_dimension=0, tiled=True),
        lax.psum_scatter(grad_down, ("dp", "seq"), scatter_dimension=0, tiled=True),
    )
    return (
        latents_out,
        d_latents,
        summed[0][:, 0],
        summed[1],
        summed[2],
        summed[3],
        summed[4],
        summed[0][:, 1],
        summed[5],
        summed[6],
        summed[7],
    )


MESH = pl.DeviceIdType.MESH
BF = jnp.bfloat16
F32 = jnp.float32
DP, ZS, CORES = 4, 4, 2
RANKS = DP * CORES
GU = (1, 3, 4)


def units_of(rank):
    return [8 * (rank // CORES) + CORES * b + rank % CORES for b in range(ZS)]


def planes_fit(mesh):
    return mesh.shape["dp"] == DP and mesh.shape["seq"] == ZS * CORES


def dot_nn(left, right):
    return jnp.dot(left, right, preferred_element_type=F32)


def remote(src, dst, send_sem, recv_sem, device):
    return pltpu.make_async_remote_copy(
        src_ref=src,
        dst_ref=dst,
        send_sem=send_sem,
        recv_sem=recv_sem,
        device_id=device,
        device_id_type=MESH,
    )


def wait_for(ref, sem):
    pltpu.make_async_copy(ref, ref, sem).wait()


def on_diagonal(row):
    at = lax.broadcasted_iota(jnp.int32, (32, 32), 0) == lax.broadcasted_iota(jnp.int32, (32, 32), 1)
    return jnp.where(at, row.astype(F32), 0.0)


def layer_kernel(
    lat_in,
    dout_in,
    lengths_in,
    gain_one_in,
    gain_two_in,
    wq_in,
    wk_in,
    wv_in,
    wg_in,
    wu_in,
    wd_rows_in,
    wo_in,
    lat_o,
    dlat_o,
    gqkv_o,
    ggu_o,
    gd_o,
    go_o,
    gain_one,
    gain_two,
    wq_raw,
    wk_raw,
    wv_raw,
    wg_raw,
    wu_raw,
    wd_raw,
    in_r,
    lens_in,
    wqkv_in,
    wgu_in,
    wd_in,
    own_l,
    stop,
    lens,
    n_one,
    n_two,
    cot,
    gbr,
    wqkv,
    wgu,
    wd,
    wo,
    qkv,
    att,
    att_f,
    tot,
    probs,
    gsc,
    part_a,
    part_b,
    part_c,
    sib,
    rcv,
    turn,
    hid,
    ggu,
    slope,
    gatt,
    graw_two,
    q_two,
    gqkv,
    dwqkv,
    dwgu,
    dwd,
    dwo,
    zq,
    zgu,
    zd,
    zo,
    xo,
    xq,
    xgu,
    xd,
    down_sum,
    resid,
    gres,
    back,
    tr_s,
    tr_r,
    tx_r,
    tz_s,
    ln_s,
    ln_r,
    wa_s,
    wa_r,
    wz_s,
    wz_r,
    wd_r,
    wo_s,
    wo_r,
    ag_s,
    ag_r,
    ag_x,
    ag_d,
    rs_s,
    rs_r,
    rs_x,
    rs_d,
    gz_s,
    gz_r,
    gx_r,
    ga_s,
    ga_r,
    gd_r,
    go_s,
    go_r,
    go_x,
    go_z,
    tb_s,
    tb_r,
):
    k = lax.axis_index("dp")
    s = lax.axis_index("seq")
    z = s // CORES
    c = s % CORES
    oc = 1 - c
    rank = CORES * k + c

    def dev(kk, zz, cc):
        return (kk, CORES * zz + cc)

    def peer(i):
        return 2 * ((k // 2 + i // 2) % 2) + (k % 2 + i % 2) % 2

    def zpeer(i):
        return (z + i) % ZS

    sibling = dev(k, z, oc)

    loads = (
        (gain_one_in, gain_one),
        (gain_two_in, gain_two),
        (wq_in, wq_raw),
        (wk_in, wk_raw),
        (wv_in, wv_raw),
        (wd_rows_in, wd_raw),
        (wg_in, wg_raw),
        (wu_in, wu_raw),
    )
    loads = [pltpu.make_async_copy(src, dst, in_r.at[i]) for i, (src, dst) in enumerate(loads)]
    for load in loads:
        load.start()

    barrier = pltpu.get_barrier_semaphore()
    greeted = 0
    for di in range(4):
        for dz in range(4):
            if di or dz:
                pl.semaphore_signal(
                    barrier, inc=1, device_id=dev(peer(di), zpeer(dz), c), device_id_type=MESH
                )
                greeted += 1
            if di == 0 or dz == 0:
                pl.semaphore_signal(
                    barrier, inc=1, device_id=dev(peer(di), zpeer(dz), oc), device_id_type=MESH
                )
                greeted += 1

    def scaled_rows(w, gain):
        return dot_nn(on_diagonal(gain[...]).astype(BF), w[...])

    def units_to_ranks():
        both = [scaled_rows(w, gain_two) for w in (wg_raw, wu_raw)]
        gap = jnp.zeros((32, 8), F32)
        for r in range(RANKS):
            for j in range(3):
                for i, rows in enumerate(both):
                    parts = []
                    for unit in units_of(r):
                        at = 88 * unit + 32 * j
                        parts += [rows[:, at : at + 32]] if j < 2 else [rows[:, at : at + 24], gap]
                    lo = 256 * j + 128 * i
                    wgu_in[r, :, lo : lo + 128] = jnp.concatenate(parts, axis=1).astype(BF)

    tile_row = lax.broadcasted_iota(jnp.int32, (8, 128), 0)
    tile = jnp.zeros((8, 128), jnp.int32)
    for i in range(4):
        tile = jnp.where(tile_row == i, lengths_in[0, i], tile)
    lens_in[...] = tile

    pl.semaphore_wait(barrier, greeted)

    def spread(src, final_of, which, start):
        for q in range(4):
            piece = src.at[pl.ds(32 * q, 32)]

            @pl.when((z == k) & (k == q))
            def _():
                if start:
                    pltpu.make_async_copy(piece, final_of(q, z), tr_r.at[which, z]).start()

            @pl.when((z == k) & (k != q))
            def _():
                copy = remote(
                    piece, final_of(q, z), tr_s.at[which, q], tr_r.at[which, z], dev(q, z, c)
                )
                if start:
                    copy.start()
                else:
                    copy.wait_send()

            @pl.when((z != k) & (k != q))
            def _():
                copy = remote(
                    piece, stop.at[which, k], tr_s.at[which, q], tx_r.at[which, k], dev(q, z, c)
                )
                if start:
                    copy.start()
                else:
                    copy.wait_send()

    def spread_on(src, final_of, which, start):
        for i in range(1, 4):
            g = zpeer(i)

            def send(piece):
                copy = remote(
                    piece, final_of(k, z), tz_s.at[which, i], tr_r.at[which, z], dev(k, g, c)
                )
                if start:
                    copy.start()
                else:
                    copy.wait_send()

            @pl.when(g == k)
            def _():
                send(src.at[pl.ds(pl.multiple_of(32 * k, 32), 32)])

            @pl.when(g != k)
            def _():
                if start:
                    wait_for(stop.at[which, g], tx_r.at[which, g])
                send(stop.at[which, g])

    def lat_place(q, b):
        return own_l.at[b]

    def cot_place(q, b):
        return cot.at[q, b, c]

    def spread_lens(start):
        here = z == k

        @pl.when(here)
        def _():
            if start:
                pltpu.make_async_copy(lens_in, lens, ln_r).start()

        @pl.when(jnp.logical_not(here))
        def _():
            copy = remote(lens_in, lens, ln_s, ln_r, dev(z, k, c))
            if start:
                copy.start()
            else:
                copy.wait_send()

    def plane_weights(src, dst, which, start):
        for i in range(4):
            for same in (True, False):
                cc = c if same else oc
                target = CORES * peer(i) + cc
                piece = src.at[target]
                place = dst.at[k, z, c]
                if i == 0 and same:
                    if start:
                        pltpu.make_async_copy(piece, place, wa_r.at[which, rank]).start()
                else:
                    copy = remote(
                        piece,
                        place,
                        wa_s.at[which, 2 * i + (0 if same else 1)],
                        wa_r.at[which, rank],
                        dev(peer(i), z, cc),
                    )
                    if start:
                        copy.start()
                    else:
                        copy.wait_send()

    def plane_weights_here(dst, which):
        for kk in range(4):
            for cc in range(2):
                wait_for(dst.at[kk, z, cc], wa_r.at[which, CORES * kk + cc])

    middle = (z == 1) | (z == 2)
    near = (1 + z % 2, 2 + z // 2 - 2 * (z % 2))
    z_end = 3 * (z // 2)

    def far_of(place):
        return (6 - 3 * place, 3 - place)

    far = far_of(z)

    def line_copy(block, which, slot, b, place, src=None):
        src = block(b) if src is None else src
        return remote(src, block(b), wz_s.at[which, slot], wz_r.at[which, b], dev(k, place, c))

    def line_send(block, which, from_ends, from_middle, start=True, src=None):
        def send(slots):
            for j in slots:
                copy = line_copy(block, which, j, z, near[j], src)
                if start:
                    copy.start()
                else:
                    copy.wait_send()

        if from_ends:

            @pl.when(jnp.logical_not(middle))
            def _():
                send(from_ends)

        if from_middle:

            @pl.when(middle)
            def _():
                send(from_middle)

    def line_relay(block, which, j):
        @pl.when(middle)
        def _():
            wait_for(block(far[j]), wz_r.at[which, far[j]])
            line_copy(block, which, 2 + j, far[j], z_end).start()

    def line_sent(block, which, src=None):
        line_send(block, which, (0, 1), (0, 1), False, src)

        @pl.when(middle)
        def _():
            for j in range(2):
                line_copy(block, which, 2 + j, far[j], z_end).wait_send()

    def line_here(block, which):
        @pl.when(middle)
        def _():
            wait_for(block(z_end), wz_r.at[which, z_end])

        @pl.when(jnp.logical_not(middle))
        def _():
            for i in range(1, 4):
                wait_for(block(zpeer(i)), wz_r.at[which, zpeer(i)])

    def qkv_block(b):
        return wqkv.at[:, b]

    def gu_block(j):
        return lambda b: wgu.at[:, b, :, :, 256 * j : 256 * j + 256]

    def down_block(b):
        return wd.at[:, b]

    side = z // 2

    def out_block(b):
        return wo.at[pl.ds(2 * (b % 2), 2)]

    def out_across(start):
        place = wo.at[2 * (z % 2) + c]

        @pl.when(c == side)
        def _():
            if start:
                pltpu.make_async_copy(wo_in, place, wo_r.at[c]).start()

        @pl.when(c != side)
        def _():
            copy = remote(wo_in, place, wo_s.at[0], wo_r.at[c], sibling)
            if start:
                copy.start()
            else:
                copy.wait_send()

    def out_along(start):
        @pl.when(c == side)
        def _():
            if start:
                for i in range(2):
                    wait_for(wo.at[2 * (z % 2) + i], wo_r.at[i])
            for j in (1, 0):
                copy = line_copy(out_block, 5, j, z, near[j])
                if start:
                    copy.start()
                else:
                    copy.wait_send()

    def out_relay(start):
        @pl.when(middle & (c != side))
        def _():
            for j in range(2):
                if start:
                    wait_for(out_block(far[j]), wz_r.at[5, far[j]])
                copy = line_copy(out_block, 5, 2 + j, far[j], z_end)
                if start:
                    copy.start()
                else:
                    copy.wait_send()

    def out_here():
        @pl.when(c == side)
        def _():
            other = 4 * side + 1 - z
            wait_for(out_block(other), wz_r.at[5, other])

        @pl.when((c != side) & jnp.logical_not(middle))
        def _():
            for j in range(2):
                wait_for(out_block(2 * c + j), wz_r.at[5, 2 * c + j])

    def half(j):
        return pl.ds(2 * j, 2)

    def ag_copy(buf, which, i, j):
        own = buf.at[k, half(j), c]
        return remote(
            own, own, ag_s.at[which, 2 * i + j], ag_r.at[which, k, j], dev(peer(i), z, c)
        )

    def ag_turn(buf, which, i):
        block = buf.at[peer(i), half(i - 1), c]
        return remote(
            block, block, ag_s.at[which, 9 + i], ag_d.at[which, i - 1], dev(peer(3 - i), z, c)
        )

    def ag_across(buf, which, i):
        block = buf.at[peer(i), :, c]
        return remote(
            block, block, ag_s.at[which, 6 + i], ag_x.at[which, peer(i)], sibling
        )

    def ag_send(buf, which):
        for i, j in ((1, 0), (2, 1), (1, 1), (2, 0)):
            ag_copy(buf, which, i, j).start()
        ag_across(buf, which, 0).start()

    def ag_corner(buf, which):
        for i in (1, 2):
            m = peer(i)
            wait_for(buf.at[m, half(i - 1), c], ag_r.at[which, m, i - 1])
            ag_turn(buf, which, i).start()

    def ag_relay(buf, which, i):
        m = peer(i)
        if i < 3:
            wait_for(buf.at[m, half(2 - i), c], ag_r.at[which, m, 2 - i])
        else:
            for j in range(2):
                wait_for(buf.at[m, half(j), c], ag_d.at[which, j])
        ag_across(buf, which, i).start()

    def ag_other(buf, which, i):
        m = peer(i)
        wait_for(buf.at[m, :, oc], ag_x.at[which, m])

    def ag_end(buf, which):
        for i in (1, 2):
            for j in range(2):
                ag_copy(buf, which, i, j).wait_send()
            ag_turn(buf, which, i).wait_send()
        for i in range(4):
            ag_across(buf, which, i).wait_send()

    def rs_copy(part, which, i):
        m = peer(i)
        return remote(
            part.at[m, :, oc], sib.at[which, m], rs_s.at[which, i], rs_r.at[which, m], sibling
        )

    def rs_part(part, which, i, j):
        m = peer(i)
        return remote(
            part.at[m, half(j), c],
            rcv.at[which, i - 1, half(j)],
            rs_s.at[which, 2 + 2 * i + j],
            rs_x.at[which, i - 1, j],
            dev(m, z, c),
        )

    def rs_turn(part, which, j):
        return remote(
            part.at[peer(3), half(j), c],
            turn.at[which, j],
            rs_s.at[which, 8 + j],
            rs_d.at[which, j],
            dev(peer(j + 1), z, c),
        )

    def rs_pair(part, which, i):
        m = peer(i)
        wait_for(sib.at[which, m], rs_r.at[which, m])
        return part[m, :, c].astype(F32) + sib[which, m].astype(F32)

    def rs_halves(part, which, i):
        m = peer(i)
        part[m, :, c] = rs_pair(part, which, i).astype(BF)
        if i == 3:
            for j in range(2):
                rs_turn(part, which, j).start()
        else:
            rs_part(part, which, i, i - 1).start()

    def rs_start(part, which, compute):
        for i, ready in ((3, None), (1, 3), (2, 1), (0, 2)):
            compute(i)
            rs_copy(part, which, i).start()
            if ready:
                rs_halves(part, which, ready)

    def rs_corner(part, which):
        for j in range(2):
            wait_for(turn.at[which, j], rs_d.at[which, j])
            m = peer(2 - j)
            sums = part[m, half(j), c].astype(F32) + turn[which, j].astype(F32)
            part[m, half(j), c] = sums.astype(BF)
            rs_part(part, which, 2 - j, j).start()

    def rs_sum(part, which):
        total = rs_pair(part, which, 0)
        for i in (1, 2):
            for j in range(2):
                wait_for(rcv.at[which, i - 1, half(j)], rs_x.at[which, i - 1, j])
            total = total + rcv[which, i - 1].astype(F32)
        return total.reshape(128, 1024)

    def rs_end(part, which):
        for i in range(4):
            rs_copy(part, which, i).wait_send()
        for j in range(2):
            rs_turn(part, which, j).wait_send()
            for i in (1, 2):
                rs_part(part, which, i, j).wait_send()

    def grads_to_far(grad, land, which, j):
        return remote(
            grad(far[j]), land.at[z], gz_s.at[which, 1 + j], gz_r.at[which, z], dev(k, far[j], c)
        )

    def line_adds(grad, land, add, which, start):
        @pl.when(jnp.logical_not(middle))
        def _():
            mid = 1 + z // 2
            for j in range(2):
                copy = remote(
                    grad(far_of(mid)[j]),
                    add.at[j],
                    gz_s.at[which, j],
                    gx_r.at[which, j],
                    dev(k, mid, c),
                )
                if start:
                    copy.start()
                else:
                    copy.wait_send()

    def line_near(grad, land, add, which, start):
        @pl.when(middle)
        def _():
            copy = remote(
                grad(z_end), land.at[z], gz_s.at[which, 0], gz_r.at[which, z], dev(k, z_end, c)
            )
            if start:
                copy.start()
            else:
                copy.wait_send()
                for j in range(2):
                    grads_to_far(grad, land, which, j).wait_send()

        @pl.when(jnp.logical_not(middle))
        def _():
            mid = 1 + z // 2
            copy = remote(
                grad(mid), land.at[z], gz_s.at[which, 2], gz_r.at[which, z], dev(k, mid, c)
            )
            if start:
                copy.start()
            else:
                copy.wait_send()

    def line_grads(grad, land, add, which, start):
        line_adds(grad, land, add, which, start)
        line_near(grad, land, add, which, start)

    def line_grads_relay(grad, land, add, which, j):
        @pl.when(middle)
        def _():
            wait_for(add.at[j], gx_r.at[which, j])
            mine = grad(far[j])
            mine[...] = (mine[...].astype(F32) + add[j].astype(F32)).astype(BF)
            grads_to_far(grad, land, which, j).start()

    def line_sum(grad, land, which):
        total = grad(z)[...].astype(F32)
        for j in range(2):
            wait_for(land.at[near[j]], gz_r.at[which, near[j]])
            total = total + land[near[j]].astype(F32)
        return total

    def dwgu_block(j):
        return lambda b: dwgu.at[pl.ds(2 * j, 2), b]

    def units_line(j):
        return dwgu_block(j), zgu.at[:, pl.ds(2 * j, 2)], xgu.at[:, pl.ds(2 * j, 2)], (1, 5)[j]

    def dwqkv_block(b):
        return dwqkv.at[:, b]

    def dwd_block(j):
        return lambda b: dwd.at[j, b]

    def out_grads_add(start):
        @pl.when((c != side) & jnp.logical_not(middle))
        def _():
            copy = remote(dwo, xo, go_s.at[0], go_x, dev(k, 1 + side, c))
            if start:
                copy.start()
            else:
                copy.wait_send()

    def out_grads_near(start):
        @pl.when(c == side)
        def _():
            other = 4 * side + 1 - z
            copy = remote(
                dwo.at[pl.ds(2 * (other % 2), 2)], zo.at[0], go_s.at[0], go_z.at[0], dev(k, other, c)
            )
            if start:
                copy.start()
            else:
                copy.wait_send()

    def out_grads_relay(start):
        @pl.when((c != side) & middle)
        def _():
            if start:
                wait_for(xo, go_x)
                dwo[...] = (dwo[...].astype(F32) + xo[...].astype(F32)).astype(BF)
            for p in range(2):
                copy = remote(
                    dwo.at[pl.ds(2 * p, 2)], zo.at[1], go_s.at[p], go_z.at[1], dev(k, 2 * c + p, c)
                )
                if start:
                    copy.start()
                else:
                    copy.wait_send()

    def out_grads_home(start):
        @pl.when(c == side)
        def _():
            mine = dwo.at[pl.ds(2 * (z % 2), 2)]
            if start:
                total = mine[...].astype(F32)
                for j in range(2):
                    wait_for(zo.at[j], go_z.at[j])
                    total = total + zo[j].astype(F32)
                mine[...] = total.astype(BF)
                pltpu.make_async_copy(dwo.at[2 * (z % 2) + c], go_o, go_r).start()
            copy = remote(dwo.at[2 * (z % 2) + oc], go_o, go_s.at[1], go_r, sibling)
            if start:
                copy.start()
            else:
                copy.wait_send()

    def gather_back(which, dst, start):
        for b in range(4):
            here = (z == k) & (z == b)
            src = back.at[which, b]
            place = dst.at[pl.ds(pl.multiple_of(32 * k, 32), 32)]

            @pl.when(here)
            def _():
                if start:
                    pltpu.make_async_copy(src, place, tb_r.at[which, k]).start()

            @pl.when(jnp.logical_not(here))
            def _():
                copy = remote(src, place, tb_s.at[which, b], tb_r.at[which, k], dev(z, b, c))
                if start:
                    copy.start()
                else:
                    copy.wait_send()

    spread(lat_in, lat_place, 0, True)
    for load in loads[:5]:
        load.wait()
    for i, w in enumerate((wq_raw, wk_raw, wv_raw)):
        rows = scaled_rows(w, gain_one).astype(BF)
        for r in range(RANKS):
            wqkv_in[r, :, i * 128 : (i + 1) * 128] = rows[:, r * 128 : (r + 1) * 128]
    plane_weights(wqkv_in, wqkv, 0, True)
    spread_lens(True)
    loads[5].wait()
    wd_in[0] = wd_raw[0:32]
    wd_in[1] = wd_raw[32:64]
    wd_in[2, 0:16] = wd_raw[64:80]
    wd_in[2, 16:32] = jnp.concatenate([wd_raw[80:88], jnp.zeros((8, 1024), BF)], axis=0)
    out_across(True)
    own_down = pltpu.make_async_copy(wd_in, wd.at[:, z], wd_r)
    own_down.start()
    out_along(True)
    for load in loads[6:]:
        load.wait()
    units_to_ranks()
    spread_on(lat_in, lat_place, 0, True)
    plane_weights(wgu_in, wgu, 1, True)
    spread(dout_in, cot_place, 1, True)
    plane_weights_here(wqkv, 0)
    line_send(qkv_block, 0, (1, 0), (0, 1))
    out_relay(True)
    for b in range(4):
        wait_for(own_l.at[b], tr_r.at[0, b])
    lat_f = own_l[...].reshape(128, 1024).astype(F32)
    r_one = lax.rsqrt(jnp.mean(lat_f * lat_f, axis=-1, keepdims=True) + EPS)
    n_one[k, :, c] = (lat_f * r_one).astype(BF).reshape(4, 32, 1024)
    ag_send(n_one, 0)
    line_relay(qkv_block, 0, 0)
    ag_corner(n_one, 0)
    line_relay(qkv_block, 0, 1)
    spread_on(dout_in, cot_place, 1, True)
    plane_weights_here(wgu, 1)
    for j in range(2):
        line_send(gu_block(j), GU[j], (1, 0), (0, 1))
    ag_relay(n_one, 0, 1)
    ag_relay(n_one, 0, 2)
    ag_relay(n_one, 0, 3)

    line_here(qkv_block, 0)

    @pl.loop(0, 4)
    def _(i):
        ag_other(n_one, 0, i)
        m = peer(i)
        block = n_one[m].reshape(256, 1024)
        out = dot_nn(block, wqkv[...].reshape(1024, 384))
        qkv[:, m] = out.astype(BF).reshape(8, 32, 384)

    line_send(gu_block(2), GU[2], (1, 0), (0, 1))
    line_send(down_block, 2, (1, 0), (0, 1), src=wd_in)

    for b in range(4):
        wait_for(cot.at[k, b, c], tr_r.at[1, b])
    ag_send(cot, 1)
    wait_for(lens, ln_r)
    lane = lax.broadcasted_iota(jnp.int32, (128, 128), 1)
    row = lax.broadcasted_iota(jnp.int32, (128, 128), 0)
    first = lane < 64

    def two_heads(v):
        zero = jnp.zeros_like(v)
        return jnp.concatenate(
            [jnp.where(first, v, zero), jnp.where(first, zero, v)], axis=0
        )

    def one_of_two(v):
        return jnp.where(first, v[:128], v[128:])

    def part_of(t0, t1, col):
        return qkv[t0:t1, :, :, col * 128 : (col + 1) * 128].reshape((t1 - t0) * 128, 128)

    for t in range(8):
        span = (t + 1) * 128
        q = two_heads(part_of(t, t + 1, 0).astype(F32) * 0.125).astype(BF)
        keys = part_of(0, t + 1, 1)
        vals = part_of(0, t + 1, 2)
        pos = row + t * 128
        begin = jnp.zeros((128, 128), jnp.int32)
        end = jnp.zeros((1, 128), jnp.int32)
        for g in range(4):
            length = lens[g : g + 1, :]
            end = end + length
            begin = begin + jnp.where(end <= pos, length, 0)
        allowed = []
        for u in range(t + 1):
            ok = begin <= lane + u * 128
            if u == t:
                ok = ok & (lane <= row)
            allowed.append(ok)
        allowed = jnp.concatenate(allowed, axis=1)
        scores = dot_right(q, keys)
        sums = []
        raws = []
        for h in range(2):
            sc = jnp.where(allowed, scores[h * 128 : (h + 1) * 128], -1e30)
            top = jnp.max(sc, axis=-1, keepdims=True)
            expo = jnp.exp(sc - top)
            low = expo.astype(BF)
            probs[t, h * 128 : (h + 1) * 128, 0:span] = low
            sums.append(jnp.sum(low.astype(F32), axis=-1, keepdims=True))
        raw = dot_nn(probs[t, :, 0:span], vals)
        both = jnp.where(first, sums[0], sums[1])
        attended = one_of_two(raw) / both
        tot[t] = both
        att_f[t] = attended
        att[:, t] = attended.astype(BF).reshape(4, 32, 128)

    line_relay(gu_block(0), GU[0], 0)
    out_here()

    def project_out(i):
        m = peer(i)
        out = dot_nn(att[m].reshape(256, 128), wo[...].reshape(128, 1024))
        part_a[m] = out.astype(BF).reshape(4, 2, 32, 1024)

    rs_start(part_a, 0, project_out)
    for t in range(8):
        q_two[t] = two_heads(part_of(t, t + 1, 0).astype(F32)).astype(BF)
    ag_corner(cot, 1)
    line_relay(gu_block(0), GU[0], 1)
    line_relay(gu_block(1), GU[1], 0)
    rs_corner(part_a, 0)
    for i in (1, 2):
        ag_relay(cot, 1, i)
    line_relay(gu_block(1), GU[1], 1)
    line_relay(gu_block(2), GU[2], 0)
    res = own_l[...].reshape(128, 1024).astype(F32) + rs_sum(part_a, 0)
    resid[...] = res
    r_two = lax.rsqrt(jnp.mean(res * res, axis=-1, keepdims=True) + EPS)
    n_two[k, :, c] = (res * r_two).astype(BF).reshape(4, 32, 1024)
    ag_send(n_two, 2)
    ag_relay(cot, 1, 3)
    line_relay(gu_block(2), GU[2], 1)

    ag_corner(n_two, 2)
    line_relay(down_block, 2, 0)
    ag_relay(n_two, 2, 1)
    ag_relay(n_two, 2, 2)
    line_relay(down_block, 2, 1)

    def feed_forward(j, i):
        m = peer(i)
        lo, mid, hi = 256 * j, 256 * j + 128, 256 * j + 256
        gu = dot_nn(n_two[m].reshape(256, 1024), wgu[:, :, :, :, lo:hi].reshape(1024, 256))
        gate = gu[:, :128]
        up = gu[:, 128:]
        sig = jax.nn.sigmoid(gate)
        active = gate * sig
        hid[m, :, 128 * j : 128 * j + 128] = (active * up).astype(BF)
        slope[m, :, lo:mid] = up * sig * (1.0 + gate * (1.0 - sig))
        slope[m, :, mid:hi] = active

    def feed_forward_rows(j, at, count):
        lo, mid, hi = 256 * j, 256 * j + 128, 256 * j + 256
        rows = pl.ds(at, count)
        gu = dot_nn(n_two[rows].reshape(256 * count, 1024), wgu[:, :, :, :, lo:hi].reshape(1024, 256))
        gate = gu[:, :128]
        up = gu[:, 128:]
        sig = jax.nn.sigmoid(gate)
        active = gate * sig
        hid[rows, :, 128 * j : 128 * j + 128] = (active * up).astype(BF).reshape(count, 256, 128)
        slope[rows, :, lo:mid] = (up * sig * (1.0 + gate * (1.0 - sig))).reshape(count, 256, 128)
        slope[rows, :, mid:hi] = active.reshape(count, 256, 128)

    def down_grad(j):
        left = hid[:, :, 128 * j : 128 * j + 128].reshape(1024, 128)

        dwd[j] = dot_left(left, cot[...].reshape(1024, 1024)).astype(BF).reshape(4, 32, 1024)
        line_grads(dwd_block(j), zd.at[j], xd.at[j], 2 + j, True)

    line_here(gu_block(0), GU[0])

    @pl.loop(0, 3)
    def _(i):
        ag_other(n_two, 2, i)
        feed_forward(0, i)

    ag_relay(n_two, 2, 3)
    ag_other(n_two, 2, 3)
    feed_forward(0, 3)
    for i in range(4):
        ag_other(cot, 1, i)
    down_grad(0)
    line_here(gu_block(1), GU[1])

    @pl.loop(0, 2)
    def _(i):
        feed_forward_rows(1, 2 * i, 2)

    down_grad(1)
    line_here(gu_block(2), GU[2])

    @pl.loop(0, 2)
    def _(i):
        feed_forward_rows(2, 2 * i, 2)

    down_grad(2)
    line_here(down_block, 2)
    own_down.wait()

    def feed_back(i):
        m = peer(i)
        g_hid = dot_right(cot[m].reshape(256, 1024), wd[...].reshape(384, 1024))
        for j in range(6):
            cols = slice(128 * j, 128 * j + 128)
            part = g_hid[:, 128 * (j // 2) : 128 * (j // 2) + 128]
            ggu[m, :, cols] = (part * slope[m, :, cols]).astype(BF)
        out = dot_right(ggu[m], wgu[...].reshape(1024, 768))
        part_b[m] = out.astype(BF).reshape(4, 2, 32, 1024)

    def down_relay(j):
        for i in range(2):
            line_grads_relay(dwd_block(j), zd.at[j], xd.at[j], 2 + j, i)

    rs_start(part_b, 1, feed_back)
    down_relay(0)

    def units_grad(d):
        cols = slice(512 * d, 512 * d + 512)
        left = n_two[:, :, :, :, cols].reshape(1024, 512)
        out = dot_left(left, ggu[...].reshape(1024, 768))
        dwgu[2 * d : 2 * d + 2] = out.astype(BF).reshape(2, 4, 2, 32, 768)

    units_grad(0)

    line_adds(*units_line(0), True)
    rs_corner(part_b, 1)
    down_relay(1)

    units_grad(1)

    line_adds(*units_line(1), True)
    for j in range(2):
        line_near(*units_line(j), True)
    down_relay(2)

    @pl.loop(0, 4)
    def _(i):
        m = peer(i)
        out = dot_nn(hid[m], wd[...].reshape(384, 1024))
        part_c[m] = out.astype(BF).reshape(4, 2, 32, 1024)
        rs_copy(part_c, 2, i).start()

    scaled = rs_sum(part_b, 1)
    res = resid[...]
    r_two = lax.rsqrt(jnp.mean(res * res, axis=-1, keepdims=True) + EPS)
    normed = res * r_two
    inner = jnp.mean(scaled * normed, axis=-1, keepdims=True)
    g_res = cot[k, :, c].reshape(128, 1024).astype(F32) + r_two * (scaled - normed * inner)
    gres[...] = g_res
    gbr[k, :, c] = g_res.astype(BF).reshape(4, 32, 1024)
    ag_send(gbr, 3)

    ag_corner(gbr, 3)
    ag_relay(gbr, 3, 1)
    ag_relay(gbr, 3, 2)
    line_grads_relay(*units_line(0), 0)

    def attended_grad(i):
        ag_other(gbr, 3, i)
        m = peer(i)
        out = dot_right(gbr[m].reshape(256, 1024), wo[...].reshape(128, 1024))
        gatt[:, m] = out.astype(BF).reshape(8, 32, 128)

    @pl.loop(0, 3)
    def _(i):
        attended_grad(i)

    ag_relay(gbr, 3, 3)
    for i in (3, 1, 2):
        rs_halves(part_c, 2, i)
    line_grads_relay(*units_line(0), 1)
    attended_grad(3)
    line_grads_relay(*units_line(1), 0)

    for t in range(8):
        span = (t + 1) * 128
        keys = part_of(0, t + 1, 1)
        vals = part_of(0, t + 1, 2)
        ratio = gatt[t].reshape(128, 128).astype(F32) / tot[t]
        g_raw = two_heads(ratio.astype(BF).astype(F32)).astype(BF)
        graw_two[t] = g_raw
        prod = ratio * att_f[t]
        g_tot = -jnp.sum(two_heads(prod), axis=-1, keepdims=True)
        g_pr = dot_right(g_raw, vals)
        g_sc = probs[t, :, 0:span].astype(F32) * (g_pr + g_tot)
        gsc[t, :, 0:span] = g_sc.astype(BF)
        g_q = one_of_two(dot_nn(gsc[t, :, 0:span], keys)) * 0.125
        gqkv[:, t, :, 0:128] = g_q.astype(BF).reshape(4, 32, 128)
    line_grads_relay(*units_line(1), 1)
    for u in range(8):
        cols = slice(u * 128, (u + 1) * 128)
        rows = (8 - u) * 256
        g_k = dot_left(gsc[u:, :, cols].reshape(rows, 128), q_two[u:].reshape(rows, 128)) * 0.125
        g_v = dot_left(probs[u:, :, cols].reshape(rows, 128), graw_two[u:].reshape(rows, 128))
        gqkv[:, u, :, 128:256] = g_k.astype(BF).reshape(4, 32, 128)
        gqkv[:, u, :, 256:384] = g_v.astype(BF).reshape(4, 32, 128)

    rs_corner(part_c, 2)
    rs_end(part_a, 0)

    def heads_back(i):
        m = peer(i)
        out = dot_right(gqkv[m].reshape(256, 384), wqkv[...].reshape(1024, 384))
        part_a[m] = out.astype(BF).reshape(4, 2, 32, 1024)

    rs_start(part_a, 3, heads_back)

    for d in range(2):
        left = n_one[:, :, :, :, 512 * d : 512 * d + 512].reshape(1024, 512)
        out = dot_left(left, gqkv[...].reshape(1024, 384))
        dwqkv[2 * d : 2 * d + 2] = out.astype(BF).reshape(2, 4, 2, 32, 384)

    line_adds(dwqkv_block, zq, xq, 0, True)
    dwo[...] = dot_left(att[...].reshape(1024, 128), gbr[...].reshape(1024, 1024)).astype(BF).reshape(4, 32, 1024)
    out_grads_add(True)
    out_grads_near(True)
    rs_corner(part_a, 3)


    out_f = resid[...] + rs_sum(part_c, 2)
    back[0] = out_f.astype(BF).reshape(4, 32, 1024)
    gather_back(0, lat_o, True)
    line_near(dwqkv_block, zq, xq, 0, True)

    def plane_grads(land, dst, which, start):
        for i in range(4):
            m = peer(i)
            for same in (True, False):
                cc = c if same else oc
                src = land.at[z, m, cc]
                place = dst.at[rank]
                if i == 0 and same:
                    if start:
                        pltpu.make_async_copy(src, place, ga_r.at[which, rank]).start()
                else:
                    copy = remote(
                        src,
                        place,
                        ga_s.at[which, 2 * i + (0 if same else 1)],
                        ga_r.at[which, rank],
                        dev(m, z, cc),
                    )
                    if start:
                        copy.start()
                    else:
                        copy.wait_send()

    line_grads_relay(dwqkv_block, zq, xq, 0, 0)
    line_grads_relay(dwqkv_block, zq, xq, 0, 1)
    scaled = rs_sum(part_a, 3)
    lat_f = own_l[...].reshape(128, 1024).astype(F32)
    r_one = lax.rsqrt(jnp.mean(lat_f * lat_f, axis=-1, keepdims=True) + EPS)
    normed = lat_f * r_one
    inner = jnp.mean(scaled * normed, axis=-1, keepdims=True)
    d_lat = gres[...] + r_one * (scaled - normed * inner)
    back[1] = d_lat.astype(BF).reshape(4, 32, 1024)
    gather_back(1, dlat_o, True)
    out_grads_relay(True)
    for j in range(2):
        grad, land, _, which = units_line(j)
        land[z] = line_sum(grad, land, which).astype(BF)
    plane_grads(zgu, ggu_o, 1, True)

    for j in range(3):
        down_sum[32 * j : 32 * j + 32] = line_sum(dwd_block(j), zd.at[j], 2 + j)
    down_out = pltpu.make_async_copy(down_sum.at[pl.ds(0, 88)], gd_o, gd_r)
    down_out.start()
    zq[z] = line_sum(dwqkv_block, zq, 0).astype(BF)
    plane_grads(zq, gqkv_o, 0, True)
    out_grads_home(True)

    for which, dst in ((0, lat_o), (1, dlat_o)):
        for b in range(4):
            wait_for(dst.at[pl.ds(32 * b, 32)], tb_r.at[which, b])
    wait_for(go_o, go_r)
    for which, dst in ((1, ggu_o), (0, gqkv_o)):
        for r in range(RANKS):
            wait_for(dst.at[r], ga_r.at[which, r])
    spread(lat_in, lat_place, 0, False)
    spread_on(lat_in, lat_place, 0, False)
    spread(dout_in, cot_place, 1, False)
    spread_on(dout_in, cot_place, 1, False)
    spread_lens(False)
    plane_weights(wqkv_in, wqkv, 0, False)
    plane_weights(wgu_in, wgu, 1, False)
    line_sent(qkv_block, 0)
    for j in range(3):
        line_sent(gu_block(j), GU[j])
    line_sent(down_block, 2, wd_in)
    down_out.wait()
    out_across(False)
    out_along(False)
    out_relay(False)
    for which, buf in enumerate((n_one, cot, n_two, gbr)):
        ag_end(buf, which)
    rs_end(part_b, 1)
    rs_end(part_c, 2)
    rs_end(part_a, 3)
    for j in range(2):
        line_grads(*units_line(j), False)
    line_grads(dwqkv_block, zq, xq, 0, False)
    for j in range(3):
        line_grads(dwd_block(j), zd.at[j], xd.at[j], 2 + j, False)
    plane_grads(zgu, ggu_o, 1, False)
    plane_grads(zq, gqkv_o, 0, False)
    out_grads_add(False)
    out_grads_near(False)
    out_grads_relay(False)
    out_grads_home(False)
    gather_back(0, lat_o, False)
    gather_back(1, dlat_o, False)


def run_layer(lat, dout, lengths, gain_one, gain_two, weights):
    vm = pltpu.VMEM
    dma = pltpu.SemaphoreType.DMA
    rows = (4, 4, 2, 32)
    return pl.pallas_call(
        layer_kernel,
        out_shape=(
            jax.ShapeDtypeStruct((128, 1024), BF),
            jax.ShapeDtypeStruct((128, 1024), BF),
            jax.ShapeDtypeStruct((RANKS, 32, 384), BF),
            jax.ShapeDtypeStruct((RANKS, 32, 768), BF),
            jax.ShapeDtypeStruct((88, 1024), F32),
            jax.ShapeDtypeStruct((32, 1024), BF),
        ),
        in_specs=[pl.BlockSpec(memory_space=pl.ANY)] * 2
        + [pl.BlockSpec(memory_space=pltpu.SMEM)]
        + [pl.BlockSpec(memory_space=pl.ANY)] * 9,
        out_specs=[pl.BlockSpec(memory_space=pl.ANY)] * 6,
        scratch_shapes=[
            vm((1, 32), BF),
            vm((1, 32), BF),
            vm((32, 1024), BF),
            vm((32, 1024), BF),
            vm((32, 1024), BF),
            vm((32, 2816), BF),
            vm((32, 2816), BF),
            vm((88, 1024), BF),
            dma((8,)),
            vm((8, 128), jnp.int32),
            vm((RANKS, 32, 384), BF),
            vm((RANKS, 32, 768), BF),
            vm((3, 32, 1024), BF),
            vm((4, 32, 1024), BF),
            vm((2, 4, 32, 1024), BF),
            vm((8, 128), jnp.int32),
            vm(rows + (1024,), BF),
            vm(rows + (1024,), BF),
            vm(rows + (1024,), BF),
            vm(rows + (1024,), BF),
            vm(rows + (384,), BF),
            vm(rows + (768,), BF),
            vm((3, 4, 32, 1024), BF),
            vm((4, 32, 1024), BF),
            vm((8, 4, 32, 384), BF),
            vm((4, 8, 32, 128), BF),
            vm((8, 128, 128), F32),
            vm((8, 128, 128), F32),
            vm((8, 256, 1024), BF),
            vm((8, 256, 1024), BF),
            vm(rows + (1024,), BF),
            vm(rows + (1024,), BF),
            vm(rows + (1024,), BF),
            vm((4, 4, 4, 32, 1024), BF),
            vm((4, 2, 4, 32, 1024), BF),
            vm((4, 2, 2, 32, 1024), BF),
            vm((4, 256, 384), BF),
            vm((4, 256, 768), BF),
            vm((4, 256, 768), F32),
            vm((8, 4, 32, 128), BF),
            vm((8, 256, 128), BF),
            vm((8, 256, 128), BF),
            vm((4, 8, 32, 384), BF),
            vm(rows + (384,), BF),
            vm(rows + (768,), BF),
            vm((3, 4, 32, 1024), BF),
            vm((4, 32, 1024), BF),
            vm((4, 4, 2, 32, 384), BF),
            vm((4, 4, 2, 32, 768), BF),
            vm((3, 4, 32, 1024), BF),
            vm((2, 2, 32, 1024), BF),
            vm((4, 32, 1024), BF),
            vm((2, 4, 2, 32, 384), BF),
            vm((2, 4, 2, 32, 768), BF),
            vm((3, 2, 32, 1024), BF),
            vm((96, 1024), F32),
            vm((128, 1024), F32),
            vm((128, 1024), F32),
            vm((2, 4, 32, 1024), BF),
            dma((2, 4)),
            dma((2, 4)),
            dma((2, 4)),
            dma((2, 4)),
            dma,
            dma,
            dma((2, 8)),
            dma((2, 8)),
            dma((6, 4)),
            dma((6, 4)),
            dma,
            dma((1,)),
            dma((2,)),
            dma((4, 12)),
            dma((4, 4, 2)),
            dma((4, 4)),
            dma((4, 2)),
            dma((4, 12)),
            dma((4, 4)),
            dma((4, 2, 2)),
            dma((4, 2)),
            dma((6, 4)),
            dma((6, 4)),
            dma((6, 2)),
            dma((2, 8)),
            dma((2, 8)),
            dma,
            dma((2,)),
            dma,
            dma,
            dma((2,)),
            dma((2, 4)),
            dma((2, 4)),
        ],
        compiler_params=pltpu.CompilerParams(
            collective_id=0, has_side_effects=True, vmem_limit_bytes=60 * 1024 * 1024
        ),
    )(lat, dout, lengths, gain_one, gain_two, *weights)


def finish_kernel(
    lat,
    dlat,
    gqkv_in,
    ggu_in,
    gd,
    go_in,
    gain_one,
    gain_two,
    wq,
    wk,
    wv,
    wg,
    wu,
    lat_o,
    dlat_o,
    g_one_o,
    gq_o,
    gk_o,
    gv_o,
    go_o,
    g_two_o,
    gg_o,
    gu_o,
    gd_o,
    gqkv,
    ggu,
    go,
    lat_v,
    dlat_v,
    gd_v,
    g_one_v,
    gq_v,
    gk_v,
    gv_v,
    go_v,
    g_two_v,
    gg_v,
    gu_v,
    sems,
    out_sems,
):
    moves = ((gqkv_in, gqkv), (ggu_in, ggu), (go_in, go), (lat, lat_v), (dlat, dlat_v), (gd, gd_v))
    copies = [pltpu.make_async_copy(src, dst, sems.at[i]) for i, (src, dst) in enumerate(moves)]
    for copy in copies:
        copy.start()
    leaving = []

    def leave(src, dst):
        copy = pltpu.make_async_copy(src, dst, out_sems.at[len(leaving)])
        copy.start()
        leaving.append(copy)

    col_one = jnp.sum(on_diagonal(gain_one[...]), axis=1, keepdims=True)
    col_two = jnp.sum(on_diagonal(gain_two[...]), axis=1, keepdims=True)

    def as_row(acc):
        return jnp.sum(on_diagonal(jnp.sum(acc, axis=1, keepdims=True)), axis=0, keepdims=True)

    for copy, src, dst in ((copies[3], lat_v, lat_o.at[0]), (copies[4], dlat_v, dlat_o.at[0]), (copies[5], gd_v, gd_o)):
        copy.wait()
        leave(src, dst)
    copies[0].wait()
    acc = jnp.zeros((32, 128), F32)
    for i, (w, out) in enumerate(((wq, gq_v), (wk, gk_v), (wv, gv_v))):
        for r in range(RANKS):
            cols = slice(r * 128, (r + 1) * 128)
            part = gqkv[r, :, i * 128 : (i + 1) * 128].astype(F32)
            out[:, cols] = part * col_one
            acc = acc + part * w[:, cols].astype(F32)
        leave(out, (gq_o, gk_o, gv_o)[i])
    g_one_v[...] = as_row(acc)
    leave(g_one_v, g_one_o)
    copies[1].wait()
    acc = jnp.zeros((32, 256), F32)
    for i, (w, out) in enumerate(((wg, gg_v), (wu, gu_v))):
        parts = [None] * 96
        for r in range(RANKS):
            for j in range(3):
                third = ggu[r, :, 256 * j + 128 * i : 256 * j + 128 * i + 128].astype(F32)
                for b, unit in enumerate(units_of(r)):
                    parts[3 * unit + j] = third[:, 32 * b : 32 * b + (24 if j == 2 else 32)]
        rows = jnp.concatenate(parts, axis=1)
        out[...] = rows * col_two
        leave(out, (gg_o, gu_o)[i])
        prod = rows * w[...].astype(F32)
        for n in range(11):
            acc = acc + prod[:, n * 256 : (n + 1) * 256]
    g_two_v[...] = as_row(acc)
    leave(g_two_v, g_two_o)
    copies[2].wait()
    go_v[...] = go[...].astype(F32)
    leave(go_v, go_o)
    for copy in leaving:
        copy.wait()


def finish(*arrays):
    outs = (
        ((1, 128, 1024), BF),
        ((1, 128, 1024), BF),
        ((1, 32), F32),
        ((32, 1024), F32),
        ((32, 1024), F32),
        ((32, 1024), F32),
        ((32, 1024), F32),
        ((1, 32), F32),
        ((32, 2816), F32),
        ((32, 2816), F32),
        ((88, 1024), F32),
    )
    hbm = pl.BlockSpec(memory_space=pltpu.HBM)
    vmem = pl.BlockSpec(memory_space=pltpu.VMEM)
    return pl.pallas_call(
        finish_kernel,
        out_shape=tuple(jax.ShapeDtypeStruct(*o) for o in outs),
        in_specs=[hbm] * 6 + [vmem] * 7,
        out_specs=[pl.BlockSpec(memory_space=pl.ANY)] * len(outs),
        scratch_shapes=[
            pltpu.VMEM((RANKS, 32, 384), BF),
            pltpu.VMEM((RANKS, 32, 768), BF),
            pltpu.VMEM((32, 1024), BF),
            pltpu.VMEM((128, 1024), BF),
            pltpu.VMEM((128, 1024), BF),
            pltpu.VMEM((88, 1024), F32),
            pltpu.VMEM((1, 32), F32),
            pltpu.VMEM((32, 1024), F32),
            pltpu.VMEM((32, 1024), F32),
            pltpu.VMEM((32, 1024), F32),
            pltpu.VMEM((32, 1024), F32),
            pltpu.VMEM((1, 32), F32),
            pltpu.VMEM((32, 2816), F32),
            pltpu.VMEM((32, 2816), F32),
            pltpu.SemaphoreType.DMA((6,)),
            pltpu.SemaphoreType.DMA((11,)),
        ],
        compiler_params=pltpu.CompilerParams(vmem_limit_bytes=60 * 1024 * 1024),
    )(*arrays)


def plane_device(
    latents,
    d_out,
    lengths,
    gain_attn,
    w_query,
    w_key,
    w_value,
    w_out,
    gain_ffn,
    w_gate,
    w_up,
    w_down,
):
    gains = gain_attn.reshape(1, 32), gain_ffn.reshape(1, 32)
    weights = w_query, w_key, w_value, w_gate, w_up, w_down, w_out
    parts = run_layer(latents[0], d_out[0], lengths, *gains, weights)
    outs = finish(*parts, *gains, w_query, w_key, w_value, w_gate, w_up)
    return tuple(o.reshape(32) if o.shape == (1, 32) else o for o in outs)


def solution(mesh):
    return jax.shard_map(
        plane_device if planes_fit(mesh) else per_device,
        mesh=mesh,
        in_specs=(
            P("dp", "seq", None),
            P("dp", "seq", None),
            P("dp", None),
            P(("dp", "seq")),
            P(("dp", "seq"), None),
            P(("dp", "seq"), None),
            P(("dp", "seq"), None),
            P(("dp", "seq"), None),
            P(("dp", "seq")),
            P(("dp", "seq"), None),
            P(("dp", "seq"), None),
            P(("dp", "seq"), None),
        ),
        out_specs=(
            P("dp", "seq", None),
            P("dp", "seq", None),
            P(("dp", "seq")),
            P(("dp", "seq"), None),
            P(("dp", "seq"), None),
            P(("dp", "seq"), None),
            P(("dp", "seq"), None),
            P(("dp", "seq")),
            P(("dp", "seq"), None),
            P(("dp", "seq"), None),
            P(("dp", "seq"), None),
        ),
        check_vma=False,
    )
```
